32 devices in a mesh: ctx: 4 (over y, x), exp: 8 (over z, core).
Axes of the slice: x: 2, y: 2, z: 4, core: 2. Of those that a mesh axis runs over, the one named last changes fastest.
Arguments:
- queries: bfloat16 [8, 512, 2048], P('exp', 'ctx')
- key_rows: bfloat16 [8, 512, 2048], P('exp', 'ctx')
- value_rows: bfloat16 [8, 512, 2048], P('exp', 'ctx'), may hold values from -6 to 6
- out_grad: bfloat16 [8, 512, 2048], P('exp', 'ctx'), may hold values from -6 to 6
- moe_input: bfloat16 [8, 512, 2048], P('exp', 'ctx'), may hold values from -6 to 6
- routes: int32 [8, 512, 4], P('exp', 'ctx'), may hold values from 0 to 31, all different within a row; in each aligned block of 128 rows (0 to 127, 128 to 255, ..., all dimensions but the last counted through in order) at most 24 rows name the same one
- route_gates: float32 [8, 512, 4], P('exp', 'ctx'), may hold values from 0.1 to 1
- up_weight: bfloat16 [32, 2048, 768], P('exp'), may hold values from -0.125 to 0.125
- down_weight: bfloat16 [32, 768, 2048], P('exp'), may hold values from -0.21875 to 0.21875
Outputs:
- query_grad: bfloat16 [8, 512, 2048], P('exp', 'ctx')
- key_grad: bfloat16 [8, 512, 2048], P('exp', 'ctx')
- value_grad: bfloat16 [8, 512, 2048], P('exp', 'ctx')
- input_grad: bfloat16 [8, 512, 2048], P('exp', 'ctx')
The draws below stay inside these ranges and needn't reach their ends.
Inputs may be any that keep to these rules, and one draw needn't show every extreme that they name: In the bins of one device no expert is named by more than 24 routes, a bound that some block reaches; the 4 experts of a bin differ.
All inputs are finite; a program needn't handle non-finite values.
Results may differ from the reference program's by a relative error of at most 0.0064.
Values may be sent and summed in bfloat16 or wider, within the bound.
No kernel may reach another device: no remote copies, remote signals or barrier semaphores. Data moves between devices by JAX's collectives and lax.ppermute only.
A program may use at most 128 MiB of HBM per device.

```python
import math
import jax
import jax.numpy as jnp
import numpy as np
from jax import lax

H = 16
HD = 128
D = 2048
EXPERTS = 32
FFH = 768
TOPK = 4
BINS_DEV = 128
CAP = 24
L = 512
SEQS = 8
N_CTX = 4


def drawn_pair(key):
    head_shape = (SEQS, L, H, HD)
    query_draw = jax.random.truncated_normal(jax.random.fold_in(key, 1), -5.0, 5.0, head_shape, jnp.float32) * 1.4
    key_draw = jax.random.truncated_normal(jax.random.fold_in(key, 2), -5.0, 5.0, head_shape, jnp.float32) * 1.4
    return (query_draw.reshape(SEQS, L, D), key_draw.reshape(SEQS, L, D))


def draw_queries(key, part):
    return drawn_pair(key)[0].astype(jnp.bfloat16)


def draw_key_rows(key, part):
    return drawn_pair(key)[1].astype(jnp.bfloat16)


def block_scale(own_key, shape, split, low, high):
    loudness = 1.0
    for position, shards_of in split:
        heights = jax.random.uniform(jax.random.fold_in(jax.random.fold_in(own_key, 6), position), (shards_of,), jnp.float32, low / len(split), high / len(split))
        loudness = loudness * jnp.repeat(jnp.exp(heights), shape[position] // shards_of).reshape((-1,) + (1,) * (len(shape) - 1 - position))
    return loudness


def routed_block(stream_key, own, number, rows, count, top, limit, skew):
    ranking = jax.random.permutation(stream_key, count)
    packed, ordinary = load_shares(count, rows * top, limit, skew, True), load_shares(count, rows * top, limit, skew, False)
    places = jnp.arange(count)

    def named(sizes, offset_by):
        used = int((sizes > 0).sum())
        fixed = max(1, used // 4)
        shifted = fixed + (places - fixed + offset_by * (used - fixed)) % max(1, count - fixed)
        return jnp.zeros((count,), jnp.int32).at[ranking[jnp.where(places < fixed, places, shifted)]].set(jnp.asarray(sizes, jnp.int32))

    sizes = jnp.where(number % 4 == 0, named(packed, number // 4), named(ordinary, number - number // 4 - 1))
    mixed = jax.random.permutation(jax.random.fold_in(own, 3), count)
    donor, sink = mixed[0:count // 2 * 2:2], mixed[1:count // 2 * 2:2]
    margin = jnp.minimum(sizes[donor] - 1, limit - sizes[sink]) // 2
    margin = jnp.where((donor == ranking[0]) | (sink == ranking[0]) | (sizes[sink] == 0), 0, jnp.maximum(margin, 0))
    shifted = jax.random.randint(jax.random.fold_in(own, 4), (count // 2,), 0, 1 << 20) % (margin + 1)
    sizes = sizes.at[donor].add(-shifted).at[sink].add(shifted)
    members = jnp.searchsorted(jnp.cumsum(sizes), jnp.arange(rows * top), side="right").astype(jnp.int32)
    listing = members.reshape(top, rows).T
    listing = listing[jax.random.permutation(jax.random.fold_in(own, 1), rows)]
    offset_by = jax.random.randint(jax.random.fold_in(own, 2), (rows, 1), 0, top)
    return jnp.take_along_axis(listing, (jnp.arange(top)[None, :] + offset_by) % top, axis=1)


def load_shares(count, total, limit, slope, full):
    weights = [(1 << 20) // math.isqrt(grade ** slope) + 1 for grade in range(1, count + 1)]
    largest = limit if full else min(limit, max(-(-total // count), total * weights[0] // sum(weights)))
    least = 1 if total - largest >= count - 1 else 0
    given, surplus = [largest] + [least] * (count - 1), total - largest - least * (count - 1)
    while surplus > 0:
        candidates = [i for i in range(1, count) if given[i] < largest] or [i for i in range(1, count) if given[i] < limit]
        pool, left = sum([weights[i] for i in candidates]), surplus
        for i in candidates:
            addition = min(limit - given[i], max(1, left * weights[i] // pool), surplus)
            given[i] = given[i] + addition
            surplus = surplus - addition
    return np.array(given)


def noise(own_key, dims, deviation, limit, split=(), kind=jnp.bfloat16):
    array = jax.random.normal(own_key, dims, jnp.float32) * deviation
    if len(split) > 0:
        array = block_scale(own_key, dims, split, -0.22, 0.18) * array
    return jnp.clip(array, min=-limit, max=limit).astype(kind)


def setup_inputs(seed: int = 0) -> dict:
    seeds = jax.random.split(jax.random.key(seed), 10)
    queries = draw_queries(jax.random.fold_in(seeds[9], 71), 0)
    key_rows = draw_key_rows(jax.random.fold_in(seeds[9], 71), 0)
    value_rows = noise(seeds[2], (SEQS, L, D), 1.0, 6.0, ((0, 8), (1, 4)))
    out_grad = jnp.clip(jax.random.uniform(seeds[3], (SEQS, L, D), jnp.float32, -6.0, 6.0) * block_scale(seeds[3], (SEQS, L, D), ((0, 8), (1, 4)), -0.4, 0.0), -6.0, 6.0).astype(jnp.bfloat16)
    moe_input = noise(seeds[4], (SEQS, L, D), 1.0, 6.0, ((0, 8), (1, 4)))
    routes_keys = jax.random.split(jax.random.fold_in(seeds[5], 1), SEQS * L // BINS_DEV)
    routes_turns = jax.random.permutation(jax.random.fold_in(seeds[5], 3), SEQS * L // BINS_DEV)
    routes = jax.vmap(lambda own, number: routed_block(jax.random.fold_in(seeds[5], 2), own, number, BINS_DEV, EXPERTS, TOPK, CAP, 2))(routes_keys, routes_turns).reshape((SEQS, L, TOPK))
    route_gates = jnp.clip(jnp.exp(math.log(1.0) - 2.3025851 * jax.random.uniform(seeds[6], (SEQS, L, TOPK), jnp.float32) ** block_scale(seeds[6], (SEQS, L, TOPK), ((0, 8), (1, 4)), -0.2, 0.2)), 0.1, 1.0)
    up_weight = noise(seeds[7], (EXPERTS, D, FFH), D ** -0.5, 0.125, ((0, 8),))
    down_weight = noise(seeds[8], (EXPERTS, FFH, D), FFH ** -0.5, 0.21875, ((0, 8),))
    return dict(queries=queries, key_rows=key_rows, value_rows=value_rows, out_grad=out_grad, moe_input=moe_input, routes=routes, route_gates=route_gates, up_weight=up_weight, down_weight=down_weight)


def head_back(operands):
    query_head, key_head, value_head, grad_head = operands
    score_scale = HD ** -0.5
    scores = jnp.dot(query_head, key_head.T, preferred_element_type=jnp.float32) * score_scale
    probs = jax.nn.softmax(scores, axis=-1)
    rounded = probs.astype(jnp.bfloat16)
    prob_grad = jnp.dot(grad_head, value_head.T, preferred_element_type=jnp.float32)
    row_delta = jnp.sum(probs * prob_grad, axis=-1, keepdims=True)
    score_grad = (probs * (prob_grad - row_delta)).astype(jnp.bfloat16)
    query_part = (jnp.dot(score_grad, key_head, preferred_element_type=jnp.float32) * score_scale).astype(jnp.bfloat16)
    key_part = (jnp.dot(score_grad.T, query_head, preferred_element_type=jnp.float32) * score_scale).astype(jnp.bfloat16)
    value_part = jnp.dot(rounded.T, grad_head, preferred_element_type=jnp.float32).astype(jnp.bfloat16)
    return query_part, key_part, value_part


def to_heads(member):
    return member.reshape(SEQS, L, H, HD).transpose(0, 2, 1, 3).reshape(SEQS * H, L, HD)


def from_heads(member):
    return member.reshape(SEQS, H, L, HD).transpose(0, 2, 1, 3).reshape(SEQS, L, D)


def reference(queries, key_rows, value_rows, out_grad, moe_input, routes, route_gates, up_weight, down_weight):
    query_parts, key_parts, value_parts = lax.map(head_back, (to_heads(queries), to_heads(key_rows), to_heads(value_rows), to_heads(out_grad)))
    flat_routes = routes.reshape(-1).astype(jnp.int32)
    route_total = flat_routes.shape[0]
    expert_most = SEQS * N_CTX * CAP
    zero_row = jnp.zeros((1, D), jnp.bfloat16)
    padded_inputs = jnp.concatenate([moe_input.reshape(SEQS * L, D), zero_row], axis=0)
    padded_grads = jnp.concatenate([out_grad.reshape(SEQS * L, D), zero_row], axis=0)
    padded_gates = jnp.concatenate([route_gates.reshape(-1), jnp.zeros((1,), jnp.float32)])

    def one_expert(carried, expert):
        chosen = jnp.nonzero(flat_routes == expert, size=expert_most, fill_value=route_total)[0].astype(jnp.int32)
        token_index = (chosen // TOPK).astype(jnp.int32)
        rows_in = padded_inputs[token_index]
        gate_values = padded_gates[chosen]
        gated_rows = (gate_values[:, None] * padded_grads[token_index].astype(jnp.float32)).astype(jnp.bfloat16)
        up_matrix = up_weight[expert]
        down_matrix = down_weight[expert]
        preact = jnp.dot(rows_in, up_matrix, preferred_element_type=jnp.float32)
        sigmoid = jax.nn.sigmoid(preact)
        slopes = sigmoid * (1.0 + preact * (1.0 - sigmoid))
        back_grad = jnp.dot(gated_rows, down_matrix.T, preferred_element_type=jnp.float32)
        hidden_grad = (back_grad * slopes).astype(jnp.bfloat16)
        route_grad = jnp.dot(hidden_grad, up_matrix.T, preferred_element_type=jnp.float32).astype(jnp.bfloat16)
        carried = carried.at[token_index].add(route_grad.astype(jnp.float32))
        return carried, None

    initial = jnp.zeros((SEQS * L + 1, D), jnp.float32)
    summed, unused = lax.scan(one_expert, initial, jnp.arange(EXPERTS, dtype=jnp.int32))
    input_grad = summed[:-1].reshape(SEQS, L, D).astype(jnp.bfloat16)
    return (from_heads(query_parts), from_heads(key_parts), from_heads(value_parts), input_grad)
```

```python
import functools

import jax
import jax.numpy as jnp
from jax import lax
from jax.experimental import pallas as pl
from jax.experimental.pallas import tpu as pltpu
from jax.sharding import PartitionSpec as P

HD = 128
CAP = 24
VMEM_BYTES = 44 * 1024 * 1024
NT = (((1,), (1,)), ((), ()))
TN = (((0,), (0,)), ((), ()))


def dot_nt(left, right):
    return lax.dot_general(left, right, NT, preferred_element_type=jnp.float32)


def dot_tn(left, right):
    return lax.dot_general(left, right, TN, preferred_element_type=jnp.float32)


def dot_nn(left, right):
    return jnp.dot(left, right, preferred_element_type=jnp.float32)


def silu_slope(preact):
    sigmoid = jax.nn.sigmoid(preact)
    return sigmoid * (1.0 + preact * (1.0 - sigmoid))


def pack_kernel(group_ref, *refs):
    members, blocks = refs[:4], refs[4:]
    width = blocks[0].shape[2]
    for place, block in enumerate(blocks):
        first = pl.multiple_of(group_ref[place] * width, 128)
        for row, member in enumerate(members):
            block[row] = member[:, pl.ds(first, width)]


def pack_groups(group_ids, members, groups):
    bins, width = members[0].shape
    block = jax.ShapeDtypeStruct((4, bins, width // groups), jnp.bfloat16)
    return pl.pallas_call(
        pack_kernel,
        out_shape=[block] * groups,
        in_specs=[pl.BlockSpec(memory_space=pltpu.SMEM)]
        + [pl.BlockSpec(memory_space=pltpu.VMEM)] * 4,
        out_specs=[pl.BlockSpec(memory_space=pltpu.VMEM)] * groups,
        compiler_params=pltpu.CompilerParams(vmem_limit_bytes=VMEM_BYTES),
        cost_estimate=pl.CostEstimate(
            flops=0, bytes_accessed=16 * bins * width, transcendentals=0
        ),
        name="pack_groups",
    )(group_ids, *members)


def unpack_kernel(group_ref, *refs):
    blocks, outs = refs[:-3], refs[-3:]
    width = blocks[0].shape[2]
    for place, block in enumerate(blocks):
        first = pl.multiple_of(group_ref[place] * width, 128)
        for row, out in enumerate(outs):
            out[:, pl.ds(first, width)] = block[row]


def unpack_groups(group_ids, blocks):
    groups = len(blocks)
    bins, width = blocks[0].shape[1], blocks[0].shape[2] * groups
    out = jax.ShapeDtypeStruct((bins, width), jnp.bfloat16)
    return pl.pallas_call(
        unpack_kernel,
        out_shape=[out] * 3,
        in_specs=[pl.BlockSpec(memory_space=pltpu.SMEM)]
        + [pl.BlockSpec(memory_space=pltpu.VMEM)] * groups,
        out_specs=[pl.BlockSpec(memory_space=pltpu.VMEM)] * 3,
        compiler_params=pltpu.CompilerParams(vmem_limit_bytes=VMEM_BYTES),
        cost_estimate=pl.CostEstimate(
            flops=0, bytes_accessed=12 * bins * width, transcendentals=0
        ),
        name="unpack_groups",
    )(group_ids, *blocks)


def heads_kernel(*refs):
    count = len(refs) // 2
    blocks, outs = refs[:count], refs[count:]
    bins = blocks[0].shape[1]
    scale = HD ** (-0.5)
    query, key, value, grad = (
        jnp.concatenate([block[row] for block in blocks], axis=0) for row in range(4)
    )
    scores = dot_nt(key, query) * scale
    powers = jnp.exp(scores - jnp.max(scores, axis=0, keepdims=True))
    probs = powers * (1.0 / jnp.sum(powers, axis=0, keepdims=True))
    prob_grad = dot_nt(value, grad)
    row_delta = jnp.sum(probs * prob_grad, axis=0, keepdims=True)
    score_grad = (probs * (prob_grad - row_delta)).astype(jnp.bfloat16)
    results = (
        dot_tn(score_grad, key) * scale,
        dot_nn(score_grad, query) * scale,
        dot_nn(probs.astype(jnp.bfloat16), grad),
    )
    for row, result in enumerate(results):
        result = result.astype(jnp.bfloat16)
        for place, out in enumerate(outs):
            out[row] = result[place * bins : (place + 1) * bins]


def heads_back(blocks):
    groups = len(blocks)
    bins, width = blocks[0].shape[1:]
    rows = bins * groups
    heads = width // HD
    return pl.pallas_call(
        heads_kernel,
        grid=(heads,),
        out_shape=[jax.ShapeDtypeStruct((3, bins, width), jnp.bfloat16)] * groups,
        in_specs=[pl.BlockSpec((4, bins, HD), lambda h: (0, 0, h))] * groups,
        out_specs=[pl.BlockSpec((3, bins, HD), lambda h: (0, 0, h))] * groups,
        compiler_params=pltpu.CompilerParams(vmem_limit_bytes=VMEM_BYTES),
        cost_estimate=pl.CostEstimate(
            flops=20 * heads * rows * rows * HD,
            bytes_accessed=14 * rows * width,
            transcendentals=heads * rows * rows,
        ),
        name="heads_back",
    )(*blocks)


def attention_back(queries, key_rows, value_rows, out_grad):
    groups = lax.axis_size("ctx")
    me = lax.axis_index("ctx")
    group_ids = jnp.stack([me ^ place for place in range(groups)]).astype(jnp.int32)

    def exchange(block, place):
        if place == 0:
            return block
        return lax.ppermute(block, "ctx", [(i, i ^ place) for i in range(groups)])

    blocks = pack_groups(group_ids, (queries, key_rows, value_rows, out_grad), groups)
    blocks = [exchange(block, place) for place, block in enumerate(blocks)]
    results = heads_back(blocks)
    results = [exchange(block, place) for place, block in enumerate(results)]
    return unpack_groups(group_ids, results)


def expert_kernel(sources, top, meta_ref, *refs):
    token_refs, grad_refs = refs[:sources], refs[sources : 2 * sources]
    up_ref, down_ref = refs[2 * sources : 2 * sources + 2]
    out_refs = refs[2 * sources + 2 : 3 * sources + 2]
    pick_ref, token_rows, gated_rows, back_rows = refs[3 * sources + 2 :]
    bins = token_refs[0].shape[0]
    slots = sources * CAP
    experts = pick_ref.shape[0] // slots
    expert = pl.program_id(0)

    @pl.when(expert == 0)
    def _():
        earlier = lax.broadcasted_iota(jnp.int32, (bins, bins), 0)
        later = lax.broadcasted_iota(jnp.int32, (bins, bins), 1)
        before = (earlier < later).astype(jnp.bfloat16)
        slot = lax.broadcasted_iota(jnp.int32, (slots, bins), 0).astype(jnp.float32)
        gates = [jnp.zeros((slots, 1), jnp.float32)] * experts
        for source in range(sources):
            named = meta_ref[source, :top]
            weights = meta_ref[source, top:]
            hits = [(named == float(local)).astype(jnp.float32) for local in range(experts)]
            chosen = [jnp.sum(hit, axis=0, keepdims=True) for hit in hits]
            stacked = jnp.concatenate(chosen, axis=0)
            position = dot_nn(stacked.astype(jnp.bfloat16), before)
            for local in range(experts):
                place = jnp.where(
                    chosen[local] > 0.0, position[local : local + 1] + float(source * CAP), -1.0
                )
                pick = (slot == place).astype(jnp.float32)
                gate = jnp.sum(hits[local] * weights, axis=0, keepdims=True)
                gates[local] = gates[local] + jnp.sum(pick * gate, axis=1, keepdims=True)
                pick_ref[
                    local * slots : (local + 1) * slots, source * bins : (source + 1) * bins
                ] = pick.astype(jnp.bfloat16)
        picks = pick_ref[...]
        tokens = jnp.concatenate([ref[...] for ref in token_refs], axis=0)
        token_rows[...] = dot_nn(picks, tokens).astype(jnp.bfloat16)
        grads = jnp.concatenate([ref[...] for ref in grad_refs], axis=0)
        gate_column = jnp.concatenate(gates, axis=0)
        gated_rows[...] = (gate_column * dot_nn(picks, grads)).astype(jnp.bfloat16)

    rows = pl.ds(pl.multiple_of(expert * slots, 16), slots)
    preact = dot_nn(token_rows[rows, :], up_ref[0])
    back_grad = dot_nt(gated_rows[rows, :], down_ref[0])
    hidden_grad = (back_grad * silu_slope(preact)).astype(jnp.bfloat16)
    back_rows[rows, :] = dot_nt(hidden_grad, up_ref[0]).astype(jnp.bfloat16)

    @pl.when(expert == experts - 1)
    def _():
        sums = dot_tn(pick_ref[...], back_rows[...])
        for source, out in enumerate(out_refs):
            out[...] = sums[source * bins : (source + 1) * bins].astype(out.dtype)


def expert_back(meta, tokens, grads, up_weight, down_weight, top):
    sources = len(tokens)
    bins, width = tokens[0].shape
    experts, _, hidden = up_weight.shape
    slots = sources * CAP
    whole = pl.BlockSpec((bins, width), lambda e: (0, 0))
    return pl.pallas_call(
        functools.partial(expert_kernel, sources, top),
        grid=(experts,),
        out_shape=[
            jax.ShapeDtypeStruct((bins, width), jnp.bfloat16 if source % 2 else jnp.float32)
            for source in range(sources)
        ],
        in_specs=[pl.BlockSpec(meta.shape, lambda e: (0, 0, 0))]
        + [whole] * (2 * sources)
        + [
            pl.BlockSpec((1, width, hidden), lambda e: (e, 0, 0)),
            pl.BlockSpec((1, hidden, width), lambda e: (e, 0, 0)),
        ],
        out_specs=[whole] * sources,
        scratch_shapes=[
            pltpu.VMEM((experts * slots, sources * bins), jnp.bfloat16),
            pltpu.VMEM((experts * slots, width), jnp.bfloat16),
            pltpu.VMEM((experts * slots, width), jnp.bfloat16),
            pltpu.VMEM((experts * slots, width), jnp.bfloat16),
        ],
        compiler_params=pltpu.CompilerParams(vmem_limit_bytes=VMEM_BYTES),
        cost_estimate=pl.CostEstimate(
            flops=6 * experts * slots * width * hidden,
            bytes_accessed=4 * experts * width * hidden + 8 * sources * bins * width,
            transcendentals=experts * slots * hidden,
        ),
        name="expert_back",
    )(meta, *tokens, *grads, up_weight, down_weight)


def mixture_back(moe_input, out_grad, routes, route_gates, up_weight, down_weight):
    members = lax.axis_size("exp")
    me = lax.axis_index("exp")
    chips = members // 2
    top = routes.shape[1]
    first_expert = me * up_weight.shape[0]

    def swap(block):
        return lax.ppermute(block, "exp", [(i, i ^ 1) for i in range(members)])

    def hop(block, step):
        return lax.ppermute(
            block, "exp", [(i, (i + 2 * step) % members) for i in range(members)]
        )

    half = chips // 2
    offsets = [[0]]
    for distance in range(1, half):
        offsets.append([-distance, distance])
    offsets.append([half])

    meta = jnp.concatenate([routes.T.astype(jnp.float32), route_gates.T], axis=0)
    metas = lax.all_gather(meta, "exp")
    metas = metas.at[:, :top].add(-first_expert.astype(jnp.float32))
    order = jnp.stack(
        [
            (me + 2 * offset) % members ^ core
            for group in offsets
            for offset in group
            for core in range(2)
        ]
    )
    metas = metas[order]

    tokens, grads = {0: moe_input}, {0: out_grad}
    for distance in range(1, half):
        for sign in (1, -1):
            offset = -sign * distance
            tokens[offset] = hop(tokens[offset + sign], sign)
            grads[offset] = hop(grads[offset + sign], sign)
    tokens[half] = hop(tokens[1 - half], 1)
    grads[half] = hop(grads[half - 1], -1)

    total = None
    done = 0
    arrived = []
    for group in offsets:
        group_tokens, group_grads = [], []
        for offset in group:
            group_tokens += [tokens[offset], swap(tokens[offset])]
            group_grads += [grads[offset], swap(grads[offset])]
        count = len(group_tokens)
        sums = expert_back(
            metas[done : done + count], group_tokens, group_grads, up_weight, down_weight, top
        )
        done += count
        for place, offset in enumerate(group):
            both = sums[2 * place] + swap(sums[2 * place + 1]).astype(jnp.float32)
            if offset == 0:
                total = both
            else:
                arrived.append(hop(both.astype(jnp.bfloat16), offset))
    for part in arrived:
        total = total + part.astype(jnp.float32)
    return total.astype(jnp.bfloat16)


def per_device(
    queries, key_rows, value_rows, out_grad, moe_input, routes, route_gates, up_weight, down_weight
):
    query_grad, key_grad, value_grad = attention_back(
        queries[0], key_rows[0], value_rows[0], out_grad[0]
    )
    input_grad = mixture_back(
        moe_input[0], out_grad[0], routes[0], route_gates[0], up_weight, down_weight
    )
    return (query_grad[None], key_grad[None], value_grad[None], input_grad[None])


def solution(mesh):
    rows = P("exp", "ctx", None)
    experts = P("exp", None, None)
    return jax.shard_map(
        per_device,
        mesh=mesh,
        in_specs=(rows,) * 7 + (experts,) * 2,
        out_specs=(rows,) * 4,
        check_vma=False,
    )
```

```python
import functools

import jax
import jax.numpy as jnp
from jax import lax
from jax.experimental import pallas as pl
from jax.experimental.pallas import tpu as pltpu
from jax.sharding import PartitionSpec as P

HD = 128
CAP = 24
NOTES = 16
VMEM_BYTES = 44 * 1024 * 1024
NT = (((1,), (1,)), ((), ()))
TN = (((0,), (0,)), ((), ()))


def dot_nt(left, right):
    return lax.dot_general(left, right, NT, preferred_element_type=jnp.float32)


def dot_tn(left, right):
    return lax.dot_general(left, right, TN, preferred_element_type=jnp.float32)


def dot_nn(left, right):
    return jnp.dot(left, right, preferred_element_type=jnp.float32)


def silu_slope(preact):
    sigmoid = jax.nn.sigmoid(preact)
    return sigmoid * (1.0 + preact * (1.0 - sigmoid))


def pack_kernel(*refs):
    *members, packed = refs
    groups, _, _, width = packed.shape
    for group in range(groups):
        for row, member in enumerate(members):
            packed[group, row] = member[:, group * width : (group + 1) * width]


def pack_groups(members, groups):
    bins, width = members[0].shape
    return pl.pallas_call(
        pack_kernel,
        out_shape=jax.ShapeDtypeStruct((groups, 4, bins, width // groups), jnp.bfloat16),
        compiler_params=pltpu.CompilerParams(vmem_limit_bytes=VMEM_BYTES),
        cost_estimate=pl.CostEstimate(
            flops=0, bytes_accessed=16 * bins * width, transcendentals=0
        ),
        name="pack_groups",
    )(*members)


def unpack_kernel(packed, *outs):
    groups, _, _, width = packed.shape
    for group in range(groups):
        for row, out in enumerate(outs):
            out[:, group * width : (group + 1) * width] = packed[group, row]


def unpack_groups(packed):
    groups, count, bins, width = packed.shape
    out = jax.ShapeDtypeStruct((bins, width * groups), jnp.bfloat16)
    return pl.pallas_call(
        unpack_kernel,
        out_shape=[out] * count,
        compiler_params=pltpu.CompilerParams(vmem_limit_bytes=VMEM_BYTES),
        cost_estimate=pl.CostEstimate(
            flops=0, bytes_accessed=12 * bins * width * groups, transcendentals=0
        ),
        name="unpack_groups",
    )(packed)


def heads_kernel(packed, out):
    groups, _, bins, _ = packed.shape
    rows = groups * bins
    scale = HD ** (-0.5)
    query, key, value, grad = (packed[:, row].reshape(rows, HD) for row in range(4))
    scores = dot_nt(key, query) * scale
    powers = jnp.exp(scores - jnp.max(scores, axis=0, keepdims=True))
    probs = powers * (1.0 / jnp.sum(powers, axis=0, keepdims=True))
    prob_grad = dot_nt(value, grad)
    row_delta = jnp.sum(probs * prob_grad, axis=0, keepdims=True)
    score_grad = (probs * (prob_grad - row_delta)).astype(jnp.bfloat16)
    results = (
        dot_tn(score_grad, key) * scale,
        dot_nn(score_grad, query) * scale,
        dot_nn(probs.astype(jnp.bfloat16), grad),
    )
    for row, result in enumerate(results):
        out[:, row] = result.astype(jnp.bfloat16).reshape(groups, bins, HD)


def heads_back(packed):
    groups, _, bins, width = packed.shape
    rows = bins * groups
    heads = width // HD
    return pl.pallas_call(
        heads_kernel,
        grid=(heads,),
        out_shape=jax.ShapeDtypeStruct((groups, 3, bins, width), jnp.bfloat16),
        in_specs=[pl.BlockSpec((groups, 4, bins, HD), lambda h: (0, 0, 0, h))],
        out_specs=pl.BlockSpec((groups, 3, bins, HD), lambda h: (0, 0, 0, h)),
        compiler_params=pltpu.CompilerParams(vmem_limit_bytes=VMEM_BYTES),
        cost_estimate=pl.CostEstimate(
            flops=20 * heads * rows * rows * HD,
            bytes_accessed=14 * rows * width,
            transcendentals=heads * rows * rows,
        ),
        name="heads_back",
    )(packed)


def exchange(packed):
    return lax.all_to_all(packed, "ctx", split_axis=0, concat_axis=0, tiled=True)


def block_kernel(tokens_ref, grads_ref, routes_ref, gates_ref, block_ref):
    bins, width = tokens_ref.shape
    block_ref[:bins] = tokens_ref[...]
    block_ref[bins : 2 * bins] = grads_ref[...]
    block_ref[2 * bins :] = jnp.zeros((NOTES, width), jnp.bfloat16)
    diagonal = lax.broadcasted_iota(jnp.int32, (bins, bins), 0) == lax.broadcasted_iota(
        jnp.int32, (bins, bins), 1
    )
    diagonal = diagonal.astype(jnp.bfloat16)
    rest = gates_ref[...]
    pieces = [(routes_ref[...] + 1).astype(jnp.float32).astype(jnp.bfloat16)]
    for _ in range(3):
        piece = rest.astype(jnp.bfloat16)
        rest = rest - piece.astype(jnp.float32)
        pieces.append(piece)
    notes = jnp.concatenate([dot_tn(piece, diagonal) for piece in pieces], axis=0)
    block_ref[2 * bins : 2 * bins + notes.shape[0], :bins] = notes.astype(jnp.bfloat16)


def make_block(tokens, grads, routes, gates):
    bins, width = tokens.shape
    return pl.pallas_call(
        block_kernel,
        out_shape=jax.ShapeDtypeStruct((2 * bins + NOTES, width), jnp.bfloat16),
        compiler_params=pltpu.CompilerParams(vmem_limit_bytes=VMEM_BYTES),
        cost_estimate=pl.CostEstimate(
            flops=0, bytes_accessed=8 * bins * width, transcendentals=0
        ),
        name="make_block",
    )(tokens, grads, routes, gates)


def expert_kernel(sources, top, base_ref, *refs):
    block_refs = refs[:sources]
    up_ref, down_ref = refs[sources : sources + 2]
    keep_refs = refs[sources + 2 : -5]
    give_ref, pick_ref, token_rows, gated_rows, back_rows = refs[-5:]
    bins = keep_refs[0].shape[0]
    slots = sources * CAP
    experts = pick_ref.shape[0] // slots
    expert = pl.program_id(0)

    @pl.when(expert == 0)
    def _():
        earlier = lax.broadcasted_iota(jnp.int32, (bins, bins), 0)
        later = lax.broadcasted_iota(jnp.int32, (bins, bins), 1)
        before = (earlier < later).astype(jnp.bfloat16)
        slot = lax.broadcasted_iota(jnp.int32, (slots, bins), 0).astype(jnp.float32)
        base = base_ref[0].astype(jnp.float32)
        gates = [jnp.zeros((slots, 1), jnp.float32)] * experts
        for source, block in enumerate(block_refs):
            notes = block[2 * bins :, :bins].astype(jnp.float32)
            named = notes[:top] - base
            weights = notes[top : 2 * top] + notes[2 * top : 3 * top] + notes[3 * top : 4 * top]
            hits = [(named == float(local + 1)).astype(jnp.float32) for local in range(experts)]
            chosen = [jnp.sum(hit, axis=0, keepdims=True) for hit in hits]
            stacked = jnp.concatenate(chosen, axis=0)
            position = dot_nn(stacked.astype(jnp.bfloat16), before)
            for local in range(experts):
                place = jnp.where(
                    chosen[local] > 0.0, position[local : local + 1] + float(source * CAP), -1.0
                )
                pick = (slot == place).astype(jnp.float32)
                gate = jnp.sum(hits[local] * weights, axis=0, keepdims=True)
                gates[local] = gates[local] + jnp.sum(pick * gate, axis=1, keepdims=True)
                pick_ref[
                    local * slots : (local + 1) * slots, source * bins : (source + 1) * bins
                ] = pick.astype(jnp.bfloat16)
        picks = pick_ref[...]
        tokens = jnp.concatenate([block[:bins] for block in block_refs], axis=0)
        token_rows[...] = dot_nn(picks, tokens).astype(jnp.bfloat16)
        grads = jnp.concatenate([block[bins : 2 * bins] for block in block_refs], axis=0)
        gate_column = jnp.concatenate(gates, axis=0)
        gated_rows[...] = (gate_column * dot_nn(picks, grads)).astype(jnp.bfloat16)

    rows = pl.ds(pl.multiple_of(expert * slots, 16), slots)
    preact = dot_nn(token_rows[rows, :], up_ref[0])
    back_grad = dot_nt(gated_rows[rows, :], down_ref[0])
    hidden_grad = (back_grad * silu_slope(preact)).astype(jnp.bfloat16)
    back_rows[rows, :] = dot_nt(hidden_grad, up_ref[0]).astype(jnp.bfloat16)

    @pl.when(expert == experts - 1)
    def _():
        sums = dot_tn(pick_ref[...], back_rows[...])
        for pair, keep in enumerate(keep_refs):
            mine, other = 2 * pair * bins, (2 * pair + 1) * bins
            keep[...] = sums[mine : mine + bins]
            give_ref[pair * bins : (pair + 1) * bins] = sums[other : other + bins].astype(
                jnp.bfloat16
            )


def expert_back(base, blocks, up_weight, down_weight, bins, top):
    sources = len(blocks)
    experts, width, hidden = up_weight.shape
    slots = sources * CAP
    pairs = sources // 2
    return pl.pallas_call(
        functools.partial(expert_kernel, sources, top),
        grid=(experts,),
        out_shape=[jax.ShapeDtypeStruct((bins, width), jnp.float32)] * pairs
        + [jax.ShapeDtypeStruct((pairs * bins, width), jnp.bfloat16)],
        in_specs=[pl.BlockSpec(memory_space=pltpu.SMEM)]
        + [pl.BlockSpec(block.shape, lambda e: (0, 0)) for block in blocks]
        + [
            pl.BlockSpec((1, width, hidden), lambda e: (e, 0, 0)),
            pl.BlockSpec((1, hidden, width), lambda e: (e, 0, 0)),
        ],
        out_specs=[pl.BlockSpec((bins, width), lambda e: (0, 0))] * pairs
        + [pl.BlockSpec((pairs * bins, width), lambda e: (0, 0))],
        scratch_shapes=[
            pltpu.VMEM((experts * slots, sources * bins), jnp.bfloat16),
            pltpu.VMEM((experts * slots, width), jnp.bfloat16),
            pltpu.VMEM((experts * slots, width), jnp.bfloat16),
            pltpu.VMEM((experts * slots, width), jnp.bfloat16),
        ],
        compiler_params=pltpu.CompilerParams(vmem_limit_bytes=VMEM_BYTES),
        cost_estimate=pl.CostEstimate(
            flops=6 * experts * slots * width * hidden,
            bytes_accessed=4 * experts * width * hidden + 8 * sources * bins * width,
            transcendentals=experts * slots * hidden,
        ),
        name="expert_back",
    )(base, *blocks, up_weight, down_weight)


def per_device(
    queries, key_rows, value_rows, out_grad, moe_input, routes, route_gates, up_weight, down_weight
):
    members = lax.axis_size("exp")
    me = lax.axis_index("exp")
    groups = lax.axis_size("ctx")
    chips = members // 2
    half = chips // 2
    _, bins, top = routes.shape
    base = (me * up_weight.shape[0]).astype(jnp.int32).reshape(1)

    def swap(block):
        return lax.ppermute(block, "exp", [(i, i ^ 1) for i in range(members)])

    def move(block, pairs):
        wide = [(2 * a + core, 2 * b + core) for a, b in pairs for core in range(2)]
        return lax.ppermute(block, "exp", wide)

    def line(distance, sign):
        return [(i, i + sign * distance) for i in range(chips) if 0 <= i + sign * distance < chips]

    def work(*arrivals):
        blocks = []
        for _, _, block in arrivals:
            blocks += [block, swap(block)]
        *kept, give = expert_back(base, blocks, up_weight, down_weight, bins, top)
        return arrivals, kept, swap(give)

    def send_back(arrivals, kept, given):
        parts = []
        for place, (kind, distance, _) in enumerate(arrivals):
            both = kept[place] + given[place * bins : (place + 1) * bins].astype(jnp.float32)
            if distance > 0:
                pairs = []
                if kind != "after":
                    pairs += line(distance, -1)
                if kind != "before":
                    pairs += line(distance, 1)
                both = move(both.astype(jnp.bfloat16), pairs)
            parts.append(both)
        return parts

    own = make_block(moe_input[0], out_grad[0], routes[0], route_gates[0])
    packed = pack_groups((queries[0], key_rows[0], value_rows[0], out_grad[0]), groups)
    heads = exchange(packed)
    parts, results = [], None
    arrivals, kept, given = work(("own", 0, own))
    right, left = own, own
    for d in range(1, half + 1):
        right = move(right, [(i, i + 1) for i in range(d - 1, chips - 1)])
        left = move(left, [(i, i - 1) for i in range(1, chips - d + 1)])
        right, left, kept, results = lax.optimization_barrier((right, left, kept, results))
        parts += send_back(arrivals, kept, given)
        arrivals = []
        if results is None:
            results = heads_back(heads)
        if d < half:
            arrivals, kept, given = work(("before", d, right), ("after", d, left))
    far = jnp.where(me >= 2 * half, right, left)
    outs = unpack_groups(exchange(results))
    for d in range(half, chips):
        if d > half:
            inward = [(i - 1, i) for i in range(d, chips)] + [(i + 1, i) for i in range(chips - d)]
            far, kept, given, parts, outs = lax.optimization_barrier(
                (move(far, inward), kept, given, parts, outs)
            )
            parts += send_back(arrivals, kept, given)
        arrivals, kept, given = work(("far", d, far))
    parts += send_back(arrivals, kept, given)
    input_grad = functools.reduce(jnp.add, [part.astype(jnp.float32) for part in parts])
    return tuple(out[None] for out in outs) + (input_grad.astype(jnp.bfloat16)[None],)


def solution(mesh):
    rows = P("exp", "ctx", None)
    experts = P("exp", None, None)
    return jax.shard_map(
        per_device,
        mesh=mesh,
        in_specs=(rows,) * 7 + (experts,) * 2,
        out_specs=(rows,) * 4,
        check_vma=False,
    )
```

```python
import functools

import jax
import jax.numpy as jnp
from jax import lax
from jax.experimental import pallas as pl
from jax.experimental.pallas import tpu as pltpu
from jax.sharding import PartitionSpec as P

HD = 128
CAP = 24
NOTES = 16
PARTS = 4
VMEM_BYTES = 36 * 1024 * 1024
VMEM_EXPERTS = 52 * 1024 * 1024
VMEM_MOST = 36 * 1024 * 1024
NT = (((1,), (1,)), ((), ()))
TN = (((0,), (0,)), ((), ()))


def dot_nt(left, right):
    return lax.dot_general(left, right, NT, preferred_element_type=jnp.float32)


def dot_tn(left, right):
    return lax.dot_general(left, right, TN, preferred_element_type=jnp.float32)


def dot_nn(left, right):
    return jnp.dot(left, right, preferred_element_type=jnp.float32)


def silu_slope(preact):
    sigmoid = jax.nn.sigmoid(preact)
    return sigmoid * (1.0 + preact * (1.0 - sigmoid))


def pack_kernel(*refs):
    *members, packed = refs
    groups, _, _, width = packed.shape
    for group in range(groups):
        for row, member in enumerate(members):
            packed[group, row] = member[:, group * width : (group + 1) * width]


def pack_groups(members, groups):
    bins, width = members[0].shape
    return pl.pallas_call(
        pack_kernel,
        out_shape=jax.ShapeDtypeStruct((groups, 4, bins, width // groups), jnp.bfloat16),
        compiler_params=pltpu.CompilerParams(vmem_limit_bytes=VMEM_BYTES),
        cost_estimate=pl.CostEstimate(
            flops=0, bytes_accessed=16 * bins * width, transcendentals=0
        ),
        name="pack_groups",
    )(*members)


def unpack_kernel(packed, *outs):
    groups, _, _, width = packed.shape
    for group in range(groups):
        for row, out in enumerate(outs):
            out[:, group * width : (group + 1) * width] = packed[group, row]


def unpack_groups(packed):
    groups, count, bins, width = packed.shape
    out = jax.ShapeDtypeStruct((bins, width * groups), jnp.bfloat16)
    return pl.pallas_call(
        unpack_kernel,
        out_shape=[out] * count,
        compiler_params=pltpu.CompilerParams(vmem_limit_bytes=VMEM_BYTES),
        cost_estimate=pl.CostEstimate(
            flops=0, bytes_accessed=12 * bins * width * groups, transcendentals=0
        ),
        name="unpack_groups",
    )(packed)


def heads_kernel(packed, out):
    groups, _, bins, _ = packed.shape
    rows = groups * bins
    scale = HD ** (-0.5)
    query, key, value, grad = (packed[:, row].reshape(rows, HD) for row in range(4))
    scores = dot_nt(key, query) * scale
    powers = jnp.exp(scores - jnp.max(scores, axis=0, keepdims=True))
    probs = powers * (1.0 / jnp.sum(powers, axis=0, keepdims=True))
    prob_grad = dot_nt(value, grad)
    row_delta = jnp.sum(probs * prob_grad, axis=0, keepdims=True)
    score_grad = (probs * (prob_grad - row_delta)).astype(jnp.bfloat16)
    results = (
        dot_tn(score_grad, key) * scale,
        dot_nn(score_grad, query) * scale,
        dot_nn(probs.astype(jnp.bfloat16), grad),
    )
    for row, result in enumerate(results):
        out[:, row] = result.astype(jnp.bfloat16).reshape(groups, bins, HD)


def heads_back(packed):
    groups, _, bins, width = packed.shape
    rows = bins * groups
    heads = width // HD
    return pl.pallas_call(
        heads_kernel,
        grid=(heads,),
        out_shape=jax.ShapeDtypeStruct((groups, 3, bins, width), jnp.bfloat16),
        in_specs=[pl.BlockSpec((groups, 4, bins, HD), lambda h: (0, 0, 0, h))],
        out_specs=pl.BlockSpec((groups, 3, bins, HD), lambda h: (0, 0, 0, h)),
        compiler_params=pltpu.CompilerParams(vmem_limit_bytes=VMEM_BYTES),
        cost_estimate=pl.CostEstimate(
            flops=20 * heads * rows * rows * HD,
            bytes_accessed=14 * rows * width,
            transcendentals=heads * rows * rows,
        ),
        name="heads_back",
    )(packed)


def exchange(packed):
    return lax.all_to_all(packed, "ctx", split_axis=0, concat_axis=0, tiled=True)


def block_kernel(tokens_ref, grads_ref, routes_ref, gates_ref, block_ref, sems):
    bins, width = tokens_ref.shape
    rows = bins // 2
    copies = [
        pltpu.make_async_copy(
            ref.at[pl.ds(part * rows, rows)],
            block_ref.at[pl.ds((2 * place + part) * rows, rows)],
            sems.at[2 * place + part],
        )
        for place, ref in enumerate((tokens_ref, grads_ref))
        for part in range(2)
    ]
    for copy in copies:
        copy.start()
    rest = gates_ref[...]
    pieces = [(routes_ref[...] + 1).astype(jnp.float32)]
    for _ in range(3):
        piece = rest.astype(jnp.bfloat16).astype(jnp.float32)
        rest = rest - piece
        pieces.append(piece)
    notes = jnp.concatenate(pieces, axis=0).astype(jnp.bfloat16)
    block_ref[2 * bins :, bins:] = jnp.zeros((NOTES, width - bins), jnp.bfloat16)
    block_ref[2 * bins :, :bins] = notes
    for copy in copies:
        copy.wait()


def make_block(tokens, grads, routes, gates):
    bins, width = tokens.shape
    return pl.pallas_call(
        block_kernel,
        out_shape=jax.ShapeDtypeStruct((2 * bins + NOTES, width), jnp.bfloat16),
        in_specs=[pl.BlockSpec(memory_space=pltpu.HBM)] * 2
        + [pl.BlockSpec(memory_space=pltpu.VMEM)] * 2,
        out_specs=pl.BlockSpec(memory_space=pltpu.VMEM),
        scratch_shapes=[pltpu.SemaphoreType.DMA((4,))],
        compiler_params=pltpu.CompilerParams(vmem_limit_bytes=VMEM_MOST),
        cost_estimate=pl.CostEstimate(
            flops=0, bytes_accessed=8 * bins * width, transcendentals=0
        ),
        name="make_block",
    )(tokens, grads, routes.T, gates.T)


def expert_kernel(sources, top, base_ref, *refs):
    block_refs = refs[:sources]
    up_hbm, down_hbm = refs[sources : sources + 2]
    keep_refs = refs[sources + 2 : -8]
    give_ref, pick_ref, token_rows, gated_rows, back_rows, up_ref, down_ref, sems = refs[-8:]
    bins = keep_refs[0].shape[0]
    slots = sources * CAP
    experts = pick_ref.shape[0] // slots

    def copies(expert):
        place = expert % 2
        return [
            pltpu.make_async_copy(
                hbm.at[expert, pl.ds(part * (hbm.shape[1] // PARTS), hbm.shape[1] // PARTS)],
                vmem.at[place, pl.ds(part * (hbm.shape[1] // PARTS), hbm.shape[1] // PARTS)],
                sems.at[place, PARTS * which + part],
            )
            for which, (hbm, vmem) in enumerate(((up_hbm, up_ref), (down_hbm, down_ref)))
            for part in range(PARTS)
        ]

    for copy in copies(0):
        copy.start()

    def pick_rows():
        earlier = lax.broadcasted_iota(jnp.int32, (bins, bins), 0)
        later = lax.broadcasted_iota(jnp.int32, (bins, bins), 1)
        before = (earlier < later).astype(jnp.bfloat16)
        slot = lax.broadcasted_iota(jnp.int32, (slots, bins), 0).astype(jnp.float32)
        base = base_ref[0].astype(jnp.float32)
        gates = [jnp.zeros((slots, 1), jnp.float32)] * experts
        for source, block in enumerate(block_refs):
            notes = block[2 * bins :, :bins].astype(jnp.float32)
            named = notes[:top] - base
            weights = notes[top : 2 * top] + notes[2 * top : 3 * top] + notes[3 * top : 4 * top]
            hits = [(named == float(local + 1)).astype(jnp.float32) for local in range(experts)]
            chosen = [jnp.sum(hit, axis=0, keepdims=True) for hit in hits]
            stacked = jnp.concatenate(chosen, axis=0)
            position = dot_nn(stacked.astype(jnp.bfloat16), before)
            for local in range(experts):
                place = jnp.where(
                    chosen[local] > 0.0, position[local : local + 1] + float(source * CAP), -1.0
                )
                pick = (slot == place).astype(jnp.float32)
                gate = jnp.sum(hits[local] * weights, axis=0, keepdims=True)
                gates[local] = gates[local] + jnp.sum(pick * gate, axis=1, keepdims=True)
                pick_ref[
                    local * slots : (local + 1) * slots, source * bins : (source + 1) * bins
                ] = pick.astype(jnp.bfloat16)
        picks = pick_ref[...]
        tokens = jnp.concatenate([block[:bins] for block in block_refs], axis=0)
        token_rows[...] = dot_nn(picks, tokens).astype(jnp.bfloat16)
        grads = jnp.concatenate([block[bins : 2 * bins] for block in block_refs], axis=0)
        gate_column = jnp.concatenate(gates, axis=0)
        gated_rows[...] = (gate_column * dot_nn(picks, grads)).astype(jnp.bfloat16)

    pick_rows()

    @pl.loop(0, experts)
    def _(expert):
        @pl.when(expert + 1 < experts)
        def _():
            for copy in copies(expert + 1):
                copy.start()

        for copy in copies(expert):
            copy.wait()
        place = expert % 2
        rows = pl.ds(pl.multiple_of(expert * slots, 16), slots)
        preact = dot_nn(token_rows[rows, :], up_ref[place])
        back_grad = dot_nt(gated_rows[rows, :], down_ref[place])
        hidden_grad = (back_grad * silu_slope(preact)).astype(jnp.bfloat16)
        back_rows[rows, :] = dot_nt(hidden_grad, up_ref[place]).astype(jnp.bfloat16)

    sums = dot_tn(pick_ref[...], back_rows[...])
    for pair, keep in enumerate(keep_refs):
        mine, other = 2 * pair * bins, (2 * pair + 1) * bins
        keep[...] = sums[mine : mine + bins].astype(jnp.bfloat16)
        give_ref[pair * bins : (pair + 1) * bins] = sums[other : other + bins].astype(jnp.bfloat16)


def expert_back(base, blocks, up_weight, down_weight, bins, top):
    sources = len(blocks)
    experts, width, hidden = up_weight.shape
    slots = sources * CAP
    pairs = sources // 2
    return pl.pallas_call(
        functools.partial(expert_kernel, sources, top),
        out_shape=[jax.ShapeDtypeStruct((bins, width), jnp.bfloat16)] * pairs
        + [jax.ShapeDtypeStruct((pairs * bins, width), jnp.bfloat16)],
        in_specs=[pl.BlockSpec(memory_space=pltpu.SMEM)]
        + [pl.BlockSpec(memory_space=pltpu.VMEM)] * sources
        + [pl.BlockSpec(memory_space=pltpu.HBM)] * 2,
        out_specs=[pl.BlockSpec(memory_space=pltpu.VMEM)] * (pairs + 1),
        scratch_shapes=[
            pltpu.VMEM((experts * slots, sources * bins), jnp.bfloat16),
            pltpu.VMEM((experts * slots, width), jnp.bfloat16),
            pltpu.VMEM((experts * slots, width), jnp.bfloat16),
            pltpu.VMEM((experts * slots, width), jnp.bfloat16),
            pltpu.VMEM((2, width, hidden), jnp.bfloat16),
            pltpu.VMEM((2, hidden, width), jnp.bfloat16),
            pltpu.SemaphoreType.DMA((2, 2 * PARTS)),
        ],
        compiler_params=pltpu.CompilerParams(vmem_limit_bytes=VMEM_EXPERTS),
        cost_estimate=pl.CostEstimate(
            flops=12 * experts * max(slots, 256) * width * hidden,
            bytes_accessed=4 * experts * width * hidden + 8 * sources * bins * width,
            transcendentals=experts * slots * hidden,
        ),
        name="expert_back",
    )(base, *blocks, up_weight, down_weight)


def per_device(
    queries, key_rows, value_rows, out_grad, moe_input, routes, route_gates, up_weight, down_weight
):
    members = lax.axis_size("exp")
    me = lax.axis_index("exp")
    groups = lax.axis_size("ctx")
    chips = members // 2
    half = chips // 2
    _, bins, top = routes.shape
    base = (me * up_weight.shape[0]).astype(jnp.int32).reshape(1)

    def swap(block):
        return lax.ppermute(block, "exp", [(i, i ^ 1) for i in range(members)])

    def move(block, pairs):
        wide = [(2 * a + core, 2 * b + core) for a, b in pairs for core in range(2)]
        return lax.ppermute(block, "exp", wide)

    def line(distance, sign):
        return [(i, i + sign * distance) for i in range(chips) if 0 <= i + sign * distance < chips]

    def work(*arrivals):
        blocks = []
        for _, _, block in arrivals:
            blocks += [block, swap(block)]
        *kept, give = expert_back(base, blocks, up_weight, down_weight, bins, top)
        return arrivals, kept, swap(give)

    def send_back(arrivals, sums):
        parts = []
        for (kind, distance, _), both in zip(arrivals, sums):
            pairs = []
            if kind != "after":
                pairs += line(distance, -1)
            if kind != "before":
                pairs += line(distance, 1)
            parts.append(move(both, pairs))
        return parts

    def both_cores(kept, given):
        return [
            (own.astype(jnp.float32) + given[place * bins : (place + 1) * bins]).astype(
                jnp.bfloat16
            )
            for place, own in enumerate(kept)
        ]

    barrier = lax.optimization_barrier
    own = make_block(moe_input[0], out_grad[0], routes[0], route_gates[0])
    packed = pack_groups((queries[0], key_rows[0], value_rows[0], out_grad[0]), groups)
    heads = exchange(packed)
    parts = []
    right, left = own, own
    arrivals, kept, given = work(("own", 0, barrier((own, packed))[0]))
    for d in range(1, half + 1):
        right = move(right, [(i, i + 1) for i in range(d - 1, chips - 1)])
        left = move(left, [(i, i - 1) for i in range(1, chips - d + 1)])
        right, left, kept, given = barrier((right, left, kept, given))
        if d == 1:
            total = kept[0].astype(jnp.float32) + given
            results = heads_back(heads)
        else:
            parts += send_back(arrivals, both_cores(kept, given))
        if d < half:
            right, left, results = barrier((right, left, results))
            arrivals, kept, given = work(("before", d, right), ("after", d, left))
    far = jnp.where(me >= 2 * half, right, left)
    arrivals, kept, given = work(("far", half, far))
    for d in range(half + 1, chips):
        inward = [(i - 1, i) for i in range(d, chips)] + [(i + 1, i) for i in range(chips - d)]
        far, kept, given, results = barrier((move(far, inward), kept, given, results))
        sums = both_cores(kept, given)
        far, total, sums, parts = barrier((far, total, sums, parts))
        for part in parts:
            total = total + part
        parts = send_back(arrivals, sums)
        arrivals, kept, given = work(("far", d, far))
        kept, given, parts = barrier((kept, given, parts))
    outs = unpack_groups(exchange(results))
    for part in parts + send_back(arrivals, both_cores(kept, given)):
        total = total + part
    return tuple(out[None] for out in outs) + (total.astype(jnp.bfloat16)[None],)


def solution(mesh):
    rows = P("exp", "ctx", None)
    experts = P("exp", None, None)
    return jax.shard_map(
        per_device,
        mesh=mesh,
        in_specs=(rows,) * 7 + (experts,) * 2,
        out_specs=(rows,) * 4,
        check_vma=False,
    )
```

```python
import functools

import jax
import jax.numpy as jnp
from jax import lax
from jax.experimental import pallas as pl
from jax.experimental.pallas import tpu as pltpu
from jax.sharding import PartitionSpec as P

HD = 128
CAP = 24
NOTES = 16
PARTS = 4
VMEM_BYTES = 36 * 1024 * 1024
VMEM_EXPERTS = 45 * 1024 * 1024
NT = (((1,), (1,)), ((), ()))
TN = (((0,), (0,)), ((), ()))


def dot_nt(left, right):
    return lax.dot_general(left, right, NT, preferred_element_type=jnp.float32)


def dot_tn(left, right):
    return lax.dot_general(left, right, TN, preferred_element_type=jnp.float32)


def dot_nn(left, right):
    return jnp.dot(left, right, preferred_element_type=jnp.float32)


def silu_slope(preact):
    sigmoid = jax.nn.sigmoid(preact)
    return sigmoid * (1.0 + preact * (1.0 - sigmoid))


def pack_kernel(*refs):
    *members, packed = refs
    groups, _, _, width = packed.shape
    for group in range(groups):
        for row, member in enumerate(members):
            packed[group, row] = member[:, group * width : (group + 1) * width]


def pack_groups(members, groups):
    bins, width = members[0].shape
    return pl.pallas_call(
        pack_kernel,
        out_shape=jax.ShapeDtypeStruct((groups, 4, bins, width // groups), jnp.bfloat16),
        compiler_params=pltpu.CompilerParams(vmem_limit_bytes=VMEM_BYTES),
        cost_estimate=pl.CostEstimate(
            flops=0, bytes_accessed=16 * bins * width, transcendentals=0
        ),
        name="pack_groups",
    )(*members)


def unpack_kernel(packed, *outs):
    groups, _, _, width = packed.shape
    for group in range(groups):
        for row, out in enumerate(outs):
            out[:, group * width : (group + 1) * width] = packed[group, row]


def unpack_groups(packed):
    groups, count, bins, width = packed.shape
    out = jax.ShapeDtypeStruct((bins, width * groups), jnp.bfloat16)
    return pl.pallas_call(
        unpack_kernel,
        out_shape=[out] * count,
        compiler_params=pltpu.CompilerParams(vmem_limit_bytes=VMEM_BYTES),
        cost_estimate=pl.CostEstimate(
            flops=0, bytes_accessed=12 * bins * width * groups, transcendentals=0
        ),
        name="unpack_groups",
    )(packed)


def heads_kernel(packed, out):
    groups, _, bins, _ = packed.shape
    rows = groups * bins
    scale = HD ** (-0.5)
    query, key, value, grad = (packed[:, row].reshape(rows, HD) for row in range(4))
    scores = dot_nt(key, query) * scale
    powers = jnp.exp(scores - jnp.max(scores, axis=0, keepdims=True))
    probs = powers * (1.0 / jnp.sum(powers, axis=0, keepdims=True))
    prob_grad = dot_nt(value, grad)
    row_delta = jnp.sum(probs * prob_grad, axis=0, keepdims=True)
    score_grad = (probs * (prob_grad - row_delta)).astype(jnp.bfloat16)
    results = (
        dot_tn(score_grad, key) * scale,
        dot_nn(score_grad, query) * scale,
        dot_nn(probs.astype(jnp.bfloat16), grad),
    )
    for row, result in enumerate(results):
        out[:, row] = result.astype(jnp.bfloat16).reshape(groups, bins, HD)


def heads_back(packed):
    groups, _, bins, width = packed.shape
    rows = bins * groups
    heads = width // HD
    return pl.pallas_call(
        heads_kernel,
        grid=(heads,),
        out_shape=jax.ShapeDtypeStruct((groups, 3, bins, width), jnp.bfloat16),
        in_specs=[pl.BlockSpec((groups, 4, bins, HD), lambda h: (0, 0, 0, h))],
        out_specs=pl.BlockSpec((groups, 3, bins, HD), lambda h: (0, 0, 0, h)),
        compiler_params=pltpu.CompilerParams(vmem_limit_bytes=VMEM_BYTES),
        cost_estimate=pl.CostEstimate(
            flops=20 * heads * rows * rows * HD,
            bytes_accessed=14 * rows * width,
            transcendentals=heads * rows * rows,
        ),
        name="heads_back",
    )(packed)


def exchange(packed):
    return lax.all_to_all(packed, "ctx", split_axis=0, concat_axis=0, tiled=True)


def rows_kernel(tokens_ref, routes_ref, gates_ref, rows_ref):
    bins, width = tokens_ref.shape
    rows_ref[:bins] = tokens_ref[...]
    rest = gates_ref[...]
    pieces = [(routes_ref[...] + 1).astype(jnp.float32)]
    for _ in range(3):
        piece = rest.astype(jnp.bfloat16).astype(jnp.float32)
        rest = rest - piece
        pieces.append(piece)
    rows_ref[bins:, bins:] = jnp.zeros((NOTES, width - bins), jnp.bfloat16)
    rows_ref[bins:, :bins] = jnp.concatenate(pieces, axis=0).astype(jnp.bfloat16)


def add_notes(tokens, routes, gates):
    bins, width = tokens.shape
    return pl.pallas_call(
        rows_kernel,
        out_shape=jax.ShapeDtypeStruct((bins + NOTES, width), jnp.bfloat16),
        compiler_params=pltpu.CompilerParams(vmem_limit_bytes=VMEM_BYTES),
        cost_estimate=pl.CostEstimate(
            flops=0, bytes_accessed=4 * bins * width, transcendentals=0
        ),
        name="add_notes",
    )(tokens, routes.T, gates.T)


def expert_kernel(sources, top, base_ref, *refs):
    token_refs, grad_refs = refs[:sources], refs[sources : 2 * sources]
    up_hbm, down_hbm = refs[2 * sources : 2 * sources + 2]
    keep_refs = refs[2 * sources + 2 : -8]
    give_ref, pick_ref, token_rows, gated_rows, back_rows, up_ref, down_ref, sems = refs[-8:]
    bins = keep_refs[0].shape[0]
    slots = sources * CAP
    experts = pick_ref.shape[0] // slots

    def copies(expert):
        place = expert % 2
        return [
            pltpu.make_async_copy(
                hbm.at[expert, pl.ds(part * (hbm.shape[1] // PARTS), hbm.shape[1] // PARTS)],
                vmem.at[place, pl.ds(part * (hbm.shape[1] // PARTS), hbm.shape[1] // PARTS)],
                sems.at[place, PARTS * which + part],
            )
            for which, (hbm, vmem) in enumerate(((up_hbm, up_ref), (down_hbm, down_ref)))
            for part in range(PARTS)
        ]

    for copy in copies(0):
        copy.start()

    def pick_rows():
        earlier = lax.broadcasted_iota(jnp.int32, (bins, bins), 0)
        later = lax.broadcasted_iota(jnp.int32, (bins, bins), 1)
        before = (earlier < later).astype(jnp.bfloat16)
        slot = lax.broadcasted_iota(jnp.int32, (slots, bins), 0).astype(jnp.float32)
        base = base_ref[0].astype(jnp.float32)
        gates = [jnp.zeros((slots, 1), jnp.float32)] * experts
        for source, token_ref in enumerate(token_refs):
            notes = token_ref[bins:, :bins].astype(jnp.float32)
            named = notes[:top] - base
            weights = notes[top : 2 * top] + notes[2 * top : 3 * top] + notes[3 * top : 4 * top]
            hits = [(named == float(local + 1)).astype(jnp.float32) for local in range(experts)]
            chosen = [jnp.sum(hit, axis=0, keepdims=True) for hit in hits]
            stacked = jnp.concatenate(chosen, axis=0)
            position = dot_nn(stacked.astype(jnp.bfloat16), before)
            for local in range(experts):
                place = jnp.where(
                    chosen[local] > 0.0, position[local : local + 1] + float(source * CAP), -1.0
                )
                pick = (slot == place).astype(jnp.float32)
                gate = jnp.sum(hits[local] * weights, axis=0, keepdims=True)
                gates[local] = gates[local] + jnp.sum(pick * gate, axis=1, keepdims=True)
                pick_ref[
                    local * slots : (local + 1) * slots, source * bins : (source + 1) * bins
                ] = pick.astype(jnp.bfloat16)
        picks = pick_ref[...]
        tokens = jnp.concatenate([ref[:bins] for ref in token_refs], axis=0)
        token_rows[...] = dot_nn(picks, tokens).astype(jnp.bfloat16)
        grads = jnp.concatenate([ref[...] for ref in grad_refs], axis=0)
        gate_column = jnp.concatenate(gates, axis=0)
        gated_rows[...] = (gate_column * dot_nn(picks, grads)).astype(jnp.bfloat16)

    pick_rows()

    @pl.loop(0, experts)
    def _(expert):
        @pl.when(expert + 1 < experts)
        def _():
            for copy in copies(expert + 1):
                copy.start()

        for copy in copies(expert):
            copy.wait()
        place = expert % 2
        rows = pl.ds(pl.multiple_of(expert * slots, 16), slots)
        preact = dot_nn(token_rows[rows, :], up_ref[place])
        back_grad = dot_nt(gated_rows[rows, :], down_ref[place])
        hidden_grad = (back_grad * silu_slope(preact)).astype(jnp.bfloat16)
        back_rows[rows, :] = dot_nt(hidden_grad, up_ref[place]).astype(jnp.bfloat16)

    sums = dot_tn(pick_ref[...], back_rows[...])
    for pair, keep in enumerate(keep_refs):
        mine, other = 2 * pair * bins, (2 * pair + 1) * bins
        keep[...] = sums[mine : mine + bins].astype(jnp.bfloat16)
        give_ref[pair * bins : (pair + 1) * bins] = sums[other : other + bins].astype(jnp.bfloat16)


def expert_back(base, tokens, grads, up_weight, down_weight, top):
    sources = len(tokens)
    bins = grads[0].shape[0]
    experts, width, hidden = up_weight.shape
    slots = sources * CAP
    pairs = sources // 2
    return pl.pallas_call(
        functools.partial(expert_kernel, sources, top),
        out_shape=[jax.ShapeDtypeStruct((bins, width), jnp.bfloat16)] * pairs
        + [jax.ShapeDtypeStruct((pairs * bins, width), jnp.bfloat16)],
        in_specs=[pl.BlockSpec(memory_space=pltpu.SMEM)]
        + [pl.BlockSpec(memory_space=pltpu.VMEM)] * (2 * sources)
        + [pl.BlockSpec(memory_space=pltpu.HBM)] * 2,
        out_specs=[pl.BlockSpec(memory_space=pltpu.VMEM)] * (pairs + 1),
        scratch_shapes=[
            pltpu.VMEM((experts * slots, sources * bins), jnp.bfloat16),
            pltpu.VMEM((experts * slots, width), jnp.bfloat16),
            pltpu.VMEM((experts * slots, width), jnp.bfloat16),
            pltpu.VMEM((experts * slots, width), jnp.bfloat16),
            pltpu.VMEM((2, width, hidden), jnp.bfloat16),
            pltpu.VMEM((2, hidden, width), jnp.bfloat16),
            pltpu.SemaphoreType.DMA((2, 2 * PARTS)),
        ],
        compiler_params=pltpu.CompilerParams(vmem_limit_bytes=VMEM_EXPERTS),
        cost_estimate=pl.CostEstimate(
            flops=12 * experts * max(slots, 256) * width * hidden,
            bytes_accessed=4 * experts * width * hidden + 8 * sources * bins * width,
            transcendentals=experts * slots * hidden,
        ),
        name="expert_back",
    )(base, *tokens, *grads, up_weight, down_weight)


def per_device(
    queries, key_rows, value_rows, out_grad, moe_input, routes, route_gates, up_weight, down_weight
):
    members = lax.axis_size("exp")
    me = lax.axis_index("exp")
    groups = lax.axis_size("ctx")
    chips = members // 2
    half = chips // 2
    _, bins, top = routes.shape
    base = (me * up_weight.shape[0]).astype(jnp.int32).reshape(1)

    def swap(block):
        return lax.ppermute(block, "exp", [(i, i ^ 1) for i in range(members)])

    def hop(block, step):
        return lax.ppermute(
            block, "exp", [(i, (i + 2 * step) % members) for i in range(members)]
        )

    def work(tokens, grads):
        all_tokens, all_grads = [], []
        for token_rows, grad_rows in zip(tokens, grads):
            all_tokens += [token_rows, swap(token_rows)]
            all_grads += [grad_rows, swap(grad_rows)]
        *kept, give = expert_back(base, all_tokens, all_grads, up_weight, down_weight, top)
        return kept, give

    def both_cores(kept, given):
        return [
            (own.astype(jnp.float32) + given[place * bins : (place + 1) * bins]).astype(
                jnp.bfloat16
            )
            for place, own in enumerate(kept)
        ]

    barrier = lax.optimization_barrier
    grads = out_grad[0]
    tokens = add_notes(moe_input[0], routes[0], route_gates[0])
    left_grads, right_grads = hop(grads, -1), hop(grads, 1)
    right_tokens, left_tokens = hop(tokens, 1), hop(tokens, -1)
    packed = pack_groups((queries[0], key_rows[0], value_rows[0], grads), groups)
    heads = exchange(packed)
    kept, give = work([tokens], [grads])
    given = swap(give)
    right_tokens, left_grads, kept, given = barrier((right_tokens, left_grads, kept, given))
    total = kept[0].astype(jnp.float32) + given
    heads, right_tokens, left_grads = barrier((heads, right_tokens, left_grads))
    results = heads_back(heads)
    distances, parts, sums, arrived = [], [], [], []
    for d in range(1, half + 1):
        if d < half:
            near = (right_tokens, left_tokens, right_grads, left_grads)
            steps = [-d, d]
        else:
            near = (right_tokens, left_grads)
            steps = [half]
        if d > 1:
            near, kept, given, results = barrier((near, kept, given, results))
            sums = both_cores(kept, given)
            near, sums = barrier((near, sums))
            arrived = [hop(part, step) for part, step in zip(sums, distances)]
        else:
            near, results = barrier((near, results))
            results = exchange(results)
        if d < half:
            right_tokens, left_tokens, right_grads, left_grads = near
            kept, give = work([right_tokens, left_tokens], [right_grads, left_grads])
            right_tokens = hop(right_tokens, 1)
            left_grads = hop(left_grads, -1)
            if d + 1 < half:
                left_tokens = hop(left_tokens, -1)
                right_grads = hop(right_grads, 1)
        else:
            right_tokens, left_grads = near
            kept, give = work([right_tokens], [left_grads])
        give, arrived = barrier((give, arrived))
        parts += arrived
        given = swap(give)
        distances = steps
    outs = unpack_groups(results)
    for part, step in zip(both_cores(kept, given), distances):
        parts.append(hop(part, step))
    for part in parts:
        total = total + part
    return tuple(out[None] for out in outs) + (total.astype(jnp.bfloat16)[None],)


def solution(mesh):
    rows = P("exp", "ctx", None)
    experts = P("exp", None, None)
    return jax.shard_map(
        per_device,
        mesh=mesh,
        in_specs=(rows,) * 7 + (experts,) * 2,
        out_specs=(rows,) * 4,
        check_vma=False,
    )
```

```python
import functools

import jax
import jax.numpy as jnp
from jax import lax
from jax.experimental import pallas as pl
from jax.experimental.pallas import tpu as pltpu
from jax.sharding import PartitionSpec as P

HD = 128
CAP = 24
NOTES = 16
PARTS = 4
VMEM_BYTES = 36 * 1024 * 1024
VMEM_EXPERTS = 45 * 1024 * 1024
SMALL = pl.CostEstimate(flops=1, bytes_accessed=1, transcendentals=0)
NT = (((1,), (1,)), ((), ()))
TN = (((0,), (0,)), ((), ()))


def dot_nt(left, right):
    return lax.dot_general(left, right, NT, preferred_element_type=jnp.float32)


def dot_tn(left, right):
    return lax.dot_general(left, right, TN, preferred_element_type=jnp.float32)


def dot_nn(left, right):
    return jnp.dot(left, right, preferred_element_type=jnp.float32)


def silu_slope(preact):
    sigmoid = jax.nn.sigmoid(preact)
    return sigmoid * (1.0 + preact * (1.0 - sigmoid))


def pack_kernel(*refs):
    *members, packed = refs
    groups, _, _, width = packed.shape
    for group in range(groups):
        for row, member in enumerate(members):
            packed[group, row] = member[:, group * width : (group + 1) * width]


def pack_groups(members, groups):
    bins, width = members[0].shape
    return pl.pallas_call(
        pack_kernel,
        out_shape=jax.ShapeDtypeStruct((groups, 4, bins, width // groups), jnp.bfloat16),
        compiler_params=pltpu.CompilerParams(vmem_limit_bytes=VMEM_BYTES),
        cost_estimate=SMALL,
        name="pack_groups",
    )(*members)


def unpack_kernel(packed, *outs):
    groups, _, _, width = packed.shape
    for group in range(groups):
        for row, out in enumerate(outs):
            out[:, group * width : (group + 1) * width] = packed[group, row]


def unpack_groups(packed):
    groups, count, bins, width = packed.shape
    out = jax.ShapeDtypeStruct((bins, width * groups), jnp.bfloat16)
    return pl.pallas_call(
        unpack_kernel,
        out_shape=[out] * count,
        compiler_params=pltpu.CompilerParams(vmem_limit_bytes=VMEM_BYTES),
        cost_estimate=SMALL,
        name="unpack_groups",
    )(packed)


def heads_kernel(packed, out):
    groups, _, bins, _ = packed.shape
    rows = groups * bins
    scale = HD ** (-0.5)
    query, key, value, grad = (packed[:, row].reshape(rows, HD) for row in range(4))
    scores = dot_nt(key, query) * scale
    powers = jnp.exp(scores - jnp.max(scores, axis=0, keepdims=True))
    probs = powers * (1.0 / jnp.sum(powers, axis=0, keepdims=True))
    prob_grad = dot_nt(value, grad)
    row_delta = jnp.sum(probs * prob_grad, axis=0, keepdims=True)
    score_grad = (probs * (prob_grad - row_delta)).astype(jnp.bfloat16)
    results = (
        dot_tn(score_grad, key) * scale,
        dot_nn(score_grad, query) * scale,
        dot_nn(probs.astype(jnp.bfloat16), grad),
    )
    for row, result in enumerate(results):
        out[:, row] = result.astype(jnp.bfloat16).reshape(groups, bins, HD)


def heads_back(packed):
    groups, _, bins, width = packed.shape
    rows = bins * groups
    heads = width // HD
    return pl.pallas_call(
        heads_kernel,
        grid=(heads,),
        out_shape=jax.ShapeDtypeStruct((groups, 3, bins, width), jnp.bfloat16),
        in_specs=[pl.BlockSpec((groups, 4, bins, HD), lambda h: (0, 0, 0, h))],
        out_specs=pl.BlockSpec((groups, 3, bins, HD), lambda h: (0, 0, 0, h)),
        compiler_params=pltpu.CompilerParams(vmem_limit_bytes=VMEM_BYTES),
        cost_estimate=SMALL,
        name="heads_back",
    )(packed)


def exchange(packed):
    return lax.all_to_all(packed, "ctx", split_axis=0, concat_axis=0, tiled=True)


def rows_kernel(tokens_ref, routes_ref, gates_ref, rows_ref):
    bins, width = tokens_ref.shape
    rows_ref[:bins] = tokens_ref[...]
    rest = gates_ref[...]
    pieces = [(routes_ref[...] + 1).astype(jnp.float32)]
    for _ in range(3):
        piece = rest.astype(jnp.bfloat16).astype(jnp.float32)
        rest = rest - piece
        pieces.append(piece)
    rows_ref[bins:, bins:] = jnp.zeros((NOTES, width - bins), jnp.bfloat16)
    rows_ref[bins:, :bins] = jnp.concatenate(pieces, axis=0).astype(jnp.bfloat16)


def add_notes(tokens, routes, gates):
    bins, width = tokens.shape
    return pl.pallas_call(
        rows_kernel,
        out_shape=jax.ShapeDtypeStruct((bins + NOTES, width), jnp.bfloat16),
        compiler_params=pltpu.CompilerParams(vmem_limit_bytes=VMEM_BYTES),
        cost_estimate=SMALL,
        name="add_notes",
    )(tokens, routes.T, gates.T)


def expert_kernel(sources, top, base_ref, *refs):
    token_refs, grad_refs = refs[:sources], refs[sources : 2 * sources]
    up_hbm, down_hbm = refs[2 * sources : 2 * sources + 2]
    keep_refs = refs[2 * sources + 2 : -8]
    give_ref, pick_ref, token_rows, gated_rows, back_rows, up_ref, down_ref, sems = refs[-8:]
    bins = keep_refs[0].shape[0]
    slots = sources * CAP
    experts = pick_ref.shape[0] // slots

    def copies(expert):
        place = expert % 2
        return [
            pltpu.make_async_copy(
                hbm.at[expert, pl.ds(part * (hbm.shape[1] // PARTS), hbm.shape[1] // PARTS)],
                vmem.at[place, pl.ds(part * (hbm.shape[1] // PARTS), hbm.shape[1] // PARTS)],
                sems.at[place, PARTS * which + part],
            )
            for which, (hbm, vmem) in enumerate(((up_hbm, up_ref), (down_hbm, down_ref)))
            for part in range(PARTS)
        ]

    for copy in copies(0):
        copy.start()

    def pick_rows():
        earlier = lax.broadcasted_iota(jnp.int32, (bins, bins), 0)
        later = lax.broadcasted_iota(jnp.int32, (bins, bins), 1)
        before = (earlier < later).astype(jnp.bfloat16)
        slot = lax.broadcasted_iota(jnp.int32, (slots, bins), 0).astype(jnp.float32)
        base = base_ref[0].astype(jnp.float32)
        gates = [jnp.zeros((slots, 1), jnp.float32)] * experts
        for source, token_ref in enumerate(token_refs):
            notes = token_ref[bins:, :bins].astype(jnp.float32)
            named = notes[:top] - base
            weights = notes[top : 2 * top] + notes[2 * top : 3 * top] + notes[3 * top : 4 * top]
            hits = [(named == float(local + 1)).astype(jnp.float32) for local in range(experts)]
            chosen = [jnp.sum(hit, axis=0, keepdims=True) for hit in hits]
            stacked = jnp.concatenate(chosen, axis=0)
            position = dot_nn(stacked.astype(jnp.bfloat16), before)
            for local in range(experts):
                place = jnp.where(
                    chosen[local] > 0.0, position[local : local + 1] + float(source * CAP), -1.0
                )
                pick = (slot == place).astype(jnp.float32)
                gate = jnp.sum(hits[local] * weights, axis=0, keepdims=True)
                gates[local] = gates[local] + jnp.sum(pick * gate, axis=1, keepdims=True)
                pick_ref[
                    local * slots : (local + 1) * slots, source * bins : (source + 1) * bins
                ] = pick.astype(jnp.bfloat16)
        picks = pick_ref[...]
        tokens = jnp.concatenate([ref[:bins] for ref in token_refs], axis=0)
        token_rows[...] = dot_nn(picks, tokens).astype(jnp.bfloat16)
        grads = jnp.concatenate([ref[...] for ref in grad_refs], axis=0)
        gate_column = jnp.concatenate(gates, axis=0)
        gated_rows[...] = (gate_column * dot_nn(picks, grads)).astype(jnp.bfloat16)

    pick_rows()

    @pl.loop(0, experts)
    def _(expert):
        @pl.when(expert + 1 < experts)
        def _():
            for copy in copies(expert + 1):
                copy.start()

        for copy in copies(expert):
            copy.wait()
        place = expert % 2
        rows = pl.ds(pl.multiple_of(expert * slots, 16), slots)
        preact = dot_nn(token_rows[rows, :], up_ref[place])
        back_grad = dot_nt(gated_rows[rows, :], down_ref[place])
        hidden_grad = (back_grad * silu_slope(preact)).astype(jnp.bfloat16)
        back_rows[rows, :] = dot_nt(hidden_grad, up_ref[place]).astype(jnp.bfloat16)

    sums = dot_tn(pick_ref[...], back_rows[...])
    for pair, keep in enumerate(keep_refs):
        mine, other = 2 * pair * bins, (2 * pair + 1) * bins
        keep[...] = sums[mine : mine + bins].astype(jnp.bfloat16)
        give_ref[pair * bins : (pair + 1) * bins] = sums[other : other + bins].astype(jnp.bfloat16)


def expert_back(base, tokens, grads, up_weight, down_weight, top):
    sources = len(tokens)
    bins = grads[0].shape[0]
    experts, width, hidden = up_weight.shape
    slots = sources * CAP
    pairs = sources // 2
    return pl.pallas_call(
        functools.partial(expert_kernel, sources, top),
        out_shape=[jax.ShapeDtypeStruct((bins, width), jnp.bfloat16)] * pairs
        + [jax.ShapeDtypeStruct((pairs * bins, width), jnp.bfloat16)],
        in_specs=[pl.BlockSpec(memory_space=pltpu.SMEM)]
        + [pl.BlockSpec(memory_space=pltpu.VMEM)] * (2 * sources)
        + [pl.BlockSpec(memory_space=pltpu.HBM)] * 2,
        out_specs=[pl.BlockSpec(memory_space=pltpu.VMEM)] * (pairs + 1),
        scratch_shapes=[
            pltpu.VMEM((experts * slots, sources * bins), jnp.bfloat16),
            pltpu.VMEM((experts * slots, width), jnp.bfloat16),
            pltpu.VMEM((experts * slots, width), jnp.bfloat16),
            pltpu.VMEM((experts * slots, width), jnp.bfloat16),
            pltpu.VMEM((2, width, hidden), jnp.bfloat16),
            pltpu.VMEM((2, hidden, width), jnp.bfloat16),
            pltpu.SemaphoreType.DMA((2, 2 * PARTS)),
        ],
        compiler_params=pltpu.CompilerParams(vmem_limit_bytes=VMEM_EXPERTS),
        cost_estimate=SMALL,
        name="expert_back",
    )(base, *tokens, *grads, up_weight, down_weight)


def per_device(
    queries, key_rows, value_rows, out_grad, moe_input, routes, route_gates, up_weight, down_weight
):
    members = lax.axis_size("exp")
    me = lax.axis_index("exp")
    groups = lax.axis_size("ctx")
    chips = members // 2
    half = chips // 2
    _, bins, top = routes.shape
    base = (me * up_weight.shape[0]).astype(jnp.int32).reshape(1)

    def swap(block):
        return lax.ppermute(block, "exp", [(i, i ^ 1) for i in range(members)])

    def hop(block, step):
        return lax.ppermute(
            block, "exp", [(i, (i + 2 * step) % members) for i in range(members)]
        )

    def work(tokens, grads):
        all_tokens, all_grads = [], []
        for token_rows, grad_rows in zip(tokens, grads):
            all_tokens += [token_rows, swap(token_rows)]
            all_grads += [grad_rows, swap(grad_rows)]
        *kept, give = expert_back(base, all_tokens, all_grads, up_weight, down_weight, top)
        return kept, give

    def both_cores(kept, given):
        return [
            (own.astype(jnp.float32) + given[place * bins : (place + 1) * bins]).astype(
                jnp.bfloat16
            )
            for place, own in enumerate(kept)
        ]

    barrier = lax.optimization_barrier
    grads = out_grad[0]
    tokens = add_notes(moe_input[0], routes[0], route_gates[0])
    left_grads, right_grads = hop(grads, -1), hop(grads, 1)
    right_tokens, left_tokens = hop(tokens, 1), hop(tokens, -1)
    packed = pack_groups((queries[0], key_rows[0], value_rows[0], grads), groups)
    heads = exchange(packed)
    kept, give = work([tokens], [grads])
    given = swap(give)
    right_tokens, left_grads, kept, given = barrier((right_tokens, left_grads, kept, given))
    total = kept[0].astype(jnp.float32) + given
    heads, right_tokens, left_grads = barrier((heads, right_tokens, left_grads))
    results = heads_back(heads)
    distances, parts, sums, arrived = [], [], [], []
    for d in range(1, half + 1):
        if d < half:
            near = (right_tokens, left_tokens, right_grads, left_grads)
            steps = [-d, d]
        else:
            near = (right_tokens, left_grads)
            steps = [half]
        if d > 1:
            near, kept, given, results = barrier((near, kept, given, results))
            sums = both_cores(kept, given)
            near, sums = barrier((near, sums))
            arrived = [hop(part, step) for part, step in zip(sums, distances)]
        else:
            near, results = barrier((near, results))
            results = exchange(results)
        if d < half:
            right_tokens, left_tokens, right_grads, left_grads = near
            kept, give = work([right_tokens, left_tokens], [right_grads, left_grads])
            right_tokens = hop(right_tokens, 1)
            left_grads = hop(left_grads, -1)
            if d + 1 < half:
                left_tokens = hop(left_tokens, -1)
                right_grads = hop(right_grads, 1)
        else:
            right_tokens, left_grads = near
            kept, give = work([right_tokens], [left_grads])
        give, arrived = barrier((give, arrived))
        parts += arrived
        given = swap(give)
        distances = steps
    outs = unpack_groups(results)
    for part, step in zip(both_cores(kept, given), distances):
        parts.append(hop(part, step))
    for part in parts:
        total = total + part
    return tuple(out[None] for out in outs) + (total.astype(jnp.bfloat16)[None],)


def solution(mesh):
    rows = P("exp", "ctx", None)
    experts = P("exp", None, None)
    return jax.shard_map(
        per_device,
        mesh=mesh,
        in_specs=(rows,) * 7 + (experts,) * 2,
        out_specs=(rows,) * 4,
        check_vma=False,
    )
```

```python
import functools

import jax
import jax.numpy as jnp
from jax import lax
from jax.experimental import pallas as pl
from jax.experimental.pallas import tpu as pltpu
from jax.sharding import PartitionSpec as P

HD = 128
CAP = 24
NOTES = 16
PARTS = 4
VMEM_BYTES = 36 * 1024 * 1024
VMEM_EXPERTS = 45 * 1024 * 1024
SMALL = pl.CostEstimate(flops=1, bytes_accessed=1, transcendentals=0)
LARGE = pl.CostEstimate(flops=30 * 10**9, bytes_accessed=50 * 10**6, transcendentals=0)
NT = (((1,), (1,)), ((), ()))
TN = (((0,), (0,)), ((), ()))


def dot_nt(left, right):
    return lax.dot_general(left, right, NT, preferred_element_type=jnp.float32)


def dot_tn(left, right):
    return lax.dot_general(left, right, TN, preferred_element_type=jnp.float32)


def dot_nn(left, right):
    return jnp.dot(left, right, preferred_element_type=jnp.float32)


def silu_slope(preact):
    sigmoid = jax.nn.sigmoid(preact)
    return sigmoid * (1.0 + preact * (1.0 - sigmoid))


def pack_kernel(group_ref, *refs):
    members, blocks = refs[:4], refs[4:]
    width = blocks[0].shape[2]
    for place, block in enumerate(blocks):
        first = pl.multiple_of(group_ref[place] * width, 128)
        for row, member in enumerate(members):
            block[row] = member[:, pl.ds(first, width)]


def pack_groups(group_ids, members, groups):
    bins, width = members[0].shape
    block = jax.ShapeDtypeStruct((4, bins, width // groups), jnp.bfloat16)
    return pl.pallas_call(
        pack_kernel,
        out_shape=[block] * groups,
        in_specs=[pl.BlockSpec(memory_space=pltpu.SMEM)]
        + [pl.BlockSpec(memory_space=pltpu.VMEM)] * 4,
        out_specs=[pl.BlockSpec(memory_space=pltpu.VMEM)] * groups,
        compiler_params=pltpu.CompilerParams(vmem_limit_bytes=VMEM_BYTES),
        cost_estimate=SMALL,
        name="pack_groups",
    )(group_ids, *members)


def unpack_kernel(group_ref, *refs):
    blocks, outs = refs[:-3], refs[-3:]
    width = blocks[0].shape[2]
    for place, block in enumerate(blocks):
        first = pl.multiple_of(group_ref[place] * width, 128)
        for row, out in enumerate(outs):
            out[:, pl.ds(first, width)] = block[row]


def unpack_groups(group_ids, blocks):
    groups = len(blocks)
    bins, width = blocks[0].shape[1], blocks[0].shape[2] * groups
    out = jax.ShapeDtypeStruct((bins, width), jnp.bfloat16)
    return pl.pallas_call(
        unpack_kernel,
        out_shape=[out] * 3,
        in_specs=[pl.BlockSpec(memory_space=pltpu.SMEM)]
        + [pl.BlockSpec(memory_space=pltpu.VMEM)] * groups,
        out_specs=[pl.BlockSpec(memory_space=pltpu.VMEM)] * 3,
        compiler_params=pltpu.CompilerParams(vmem_limit_bytes=VMEM_BYTES),
        cost_estimate=SMALL,
        name="unpack_groups",
    )(group_ids, *blocks)


def heads_kernel(*refs):
    count = len(refs) // 2
    blocks, outs = refs[:count], refs[count:]
    bins = blocks[0].shape[1]
    scale = HD ** (-0.5)
    query, key, value, grad = (
        jnp.concatenate([block[row] for block in blocks], axis=0) for row in range(4)
    )
    scores = dot_nt(key, query) * scale
    powers = jnp.exp(scores - jnp.max(scores, axis=0, keepdims=True))
    probs = powers * (1.0 / jnp.sum(powers, axis=0, keepdims=True))
    prob_grad = dot_nt(value, grad)
    row_delta = jnp.sum(probs * prob_grad, axis=0, keepdims=True)
    score_grad = (probs * (prob_grad - row_delta)).astype(jnp.bfloat16)
    results = (
        dot_tn(score_grad, key) * scale,
        dot_nn(score_grad, query) * scale,
        dot_nn(probs.astype(jnp.bfloat16), grad),
    )
    for row, result in enumerate(results):
        result = result.astype(jnp.bfloat16)
        for place, out in enumerate(outs):
            out[row] = result[place * bins : (place + 1) * bins]


def heads_back(blocks):
    groups = len(blocks)
    bins, width = blocks[0].shape[1:]
    rows = bins * groups
    heads = width // HD
    return pl.pallas_call(
        heads_kernel,
        grid=(heads,),
        out_shape=[jax.ShapeDtypeStruct((3, bins, width), jnp.bfloat16)] * groups,
        in_specs=[pl.BlockSpec((4, bins, HD), lambda h: (0, 0, h))] * groups,
        out_specs=[pl.BlockSpec((3, bins, HD), lambda h: (0, 0, h))] * groups,
        compiler_params=pltpu.CompilerParams(vmem_limit_bytes=VMEM_BYTES),
        cost_estimate=SMALL,
        name="heads_back",
    )(*blocks)


def exchange(blocks):
    groups = len(blocks)
    return [blocks[0]] + [
        lax.ppermute(blocks[place], "ctx", [(i, i ^ place) for i in range(groups)])
        for place in range(1, groups)
    ]


def block_kernel(tokens_ref, grads_ref, routes_ref, gates_ref, block_ref):
    bins, width = tokens_ref.shape
    block_ref[:bins] = tokens_ref[...]
    block_ref[bins : 2 * bins] = grads_ref[...]
    rest = gates_ref[...]
    pieces = [(routes_ref[...] + 1).astype(jnp.float32)]
    for _ in range(3):
        piece = rest.astype(jnp.bfloat16).astype(jnp.float32)
        rest = rest - piece
        pieces.append(piece)
    block_ref[2 * bins :, bins:] = jnp.zeros((NOTES, width - bins), jnp.bfloat16)
    block_ref[2 * bins :, :bins] = jnp.concatenate(pieces, axis=0).astype(jnp.bfloat16)


def make_block(tokens, grads, routes, gates):
    bins, width = tokens.shape
    return pl.pallas_call(
        block_kernel,
        out_shape=jax.ShapeDtypeStruct((2 * bins + NOTES, width), jnp.bfloat16),
        compiler_params=pltpu.CompilerParams(vmem_limit_bytes=VMEM_BYTES),
        cost_estimate=SMALL,
        name="make_block",
    )(tokens, grads, routes.T, gates.T)


def expert_kernel(sources, top, base_ref, *refs):
    block_refs = refs[:sources]
    up_hbm, down_hbm = refs[sources : sources + 2]
    keep_refs = refs[sources + 2 : -8]
    give_ref, pick_ref, token_rows, gated_rows, back_rows, up_ref, down_ref, sems = refs[-8:]
    bins = keep_refs[0].shape[0]
    slots = sources * CAP
    experts = pick_ref.shape[0] // slots

    def copies(expert):
        place = expert % 2
        return [
            pltpu.make_async_copy(
                hbm.at[expert, pl.ds(part * (hbm.shape[1] // PARTS), hbm.shape[1] // PARTS)],
                vmem.at[place, pl.ds(part * (hbm.shape[1] // PARTS), hbm.shape[1] // PARTS)],
                sems.at[place, PARTS * which + part],
            )
            for which, (hbm, vmem) in enumerate(((up_hbm, up_ref), (down_hbm, down_ref)))
            for part in range(PARTS)
        ]

    for copy in copies(0):
        copy.start()

    def pick_rows():
        earlier = lax.broadcasted_iota(jnp.int32, (bins, bins), 0)
        later = lax.broadcasted_iota(jnp.int32, (bins, bins), 1)
        before = (earlier < later).astype(jnp.bfloat16)
        slot = lax.broadcasted_iota(jnp.int32, (slots, bins), 0).astype(jnp.float32)
        base = base_ref[0].astype(jnp.float32)
        gates = [jnp.zeros((slots, 1), jnp.float32)] * experts
        for source, block in enumerate(block_refs):
            notes = block[2 * bins :, :bins].astype(jnp.float32)
            named = notes[:top] - base
            weights = notes[top : 2 * top] + notes[2 * top : 3 * top] + notes[3 * top : 4 * top]
            hits = [(named == float(local + 1)).astype(jnp.float32) for local in range(experts)]
            chosen = [jnp.sum(hit, axis=0, keepdims=True) for hit in hits]
            stacked = jnp.concatenate(chosen, axis=0)
            position = dot_nn(stacked.astype(jnp.bfloat16), before)
            for local in range(experts):
                place = jnp.where(
                    chosen[local] > 0.0, position[local : local + 1] + float(source * CAP), -1.0
                )
                pick = (slot == place).astype(jnp.float32)
                gate = jnp.sum(hits[local] * weights, axis=0, keepdims=True)
                gates[local] = gates[local] + jnp.sum(pick * gate, axis=1, keepdims=True)
                pick_ref[
                    local * slots : (local + 1) * slots, source * bins : (source + 1) * bins
                ] = pick.astype(jnp.bfloat16)
        picks = pick_ref[...]
        tokens = jnp.concatenate([block[:bins] for block in block_refs], axis=0)
        token_rows[...] = dot_nn(picks, tokens).astype(jnp.bfloat16)
        grads = jnp.concatenate([block[bins : 2 * bins] for block in block_refs], axis=0)
        gate_column = jnp.concatenate(gates, axis=0)
        gated_rows[...] = (gate_column * dot_nn(picks, grads)).astype(jnp.bfloat16)

    pick_rows()

    @pl.loop(0, experts)
    def _(expert):
        @pl.when(expert + 1 < experts)
        def _():
            for copy in copies(expert + 1):
                copy.start()

        for copy in copies(expert):
            copy.wait()
        place = expert % 2
        rows = pl.ds(pl.multiple_of(expert * slots, 16), slots)
        preact = dot_nn(token_rows[rows, :], up_ref[place])
        back_grad = dot_nt(gated_rows[rows, :], down_ref[place])
        hidden_grad = (back_grad * silu_slope(preact)).astype(jnp.bfloat16)
        back_rows[rows, :] = dot_nt(hidden_grad, up_ref[place]).astype(jnp.bfloat16)

    sums = dot_tn(pick_ref[...], back_rows[...])
    for pair, keep in enumerate(keep_refs):
        mine, other = 2 * pair * bins, (2 * pair + 1) * bins
        keep[...] = sums[mine : mine + bins].astype(jnp.bfloat16)
        give_ref[pair * bins : (pair + 1) * bins] = sums[other : other + bins].astype(jnp.bfloat16)


def expert_back(base, blocks, up_weight, down_weight, bins, top):
    sources = len(blocks)
    experts, width, hidden = up_weight.shape
    slots = sources * CAP
    pairs = sources // 2
    return pl.pallas_call(
        functools.partial(expert_kernel, sources, top),
        out_shape=[jax.ShapeDtypeStruct((bins, width), jnp.bfloat16)] * pairs
        + [jax.ShapeDtypeStruct((pairs * bins, width), jnp.bfloat16)],
        in_specs=[pl.BlockSpec(memory_space=pltpu.SMEM)]
        + [pl.BlockSpec(memory_space=pltpu.VMEM)] * sources
        + [pl.BlockSpec(memory_space=pltpu.HBM)] * 2,
        out_specs=[pl.BlockSpec(memory_space=pltpu.VMEM)] * (pairs + 1),
        scratch_shapes=[
            pltpu.VMEM((experts * slots, sources * bins), jnp.bfloat16),
            pltpu.VMEM((experts * slots, width), jnp.bfloat16),
            pltpu.VMEM((experts * slots, width), jnp.bfloat16),
            pltpu.VMEM((experts * slots, width), jnp.bfloat16),
            pltpu.VMEM((2, width, hidden), jnp.bfloat16),
            pltpu.VMEM((2, hidden, width), jnp.bfloat16),
            pltpu.SemaphoreType.DMA((2, 2 * PARTS)),
        ],
        compiler_params=pltpu.CompilerParams(vmem_limit_bytes=VMEM_EXPERTS),
        cost_estimate=LARGE,
        name="expert_back",
    )(base, *blocks, up_weight, down_weight)


def per_device(
    queries, key_rows, value_rows, out_grad, moe_input, routes, route_gates, up_weight, down_weight
):
    members = lax.axis_size("exp")
    me = lax.axis_index("exp")
    groups = lax.axis_size("ctx")
    chips = members // 2
    half = chips // 2
    _, bins, top = routes.shape
    base = (me * up_weight.shape[0]).astype(jnp.int32).reshape(1)

    def swap(block):
        return lax.ppermute(block, "exp", [(i, i ^ 1) for i in range(members)])

    def hop(block, step):
        return lax.ppermute(
            block, "exp", [(i, (i + 2 * step) % members) for i in range(members)]
        )

    def work(blocks):
        *kept, give = expert_back(base, blocks, up_weight, down_weight, bins, top)
        return kept, give

    def both_cores(kept, given):
        return [
            (own.astype(jnp.float32) + given[place * bins : (place + 1) * bins]).astype(
                jnp.bfloat16
            )
            for place, own in enumerate(kept)
        ]

    barrier = lax.optimization_barrier
    own = make_block(moe_input[0], out_grad[0], routes[0], route_gates[0])
    right, left = hop(own, 1), hop(own, -1)
    pair = [own, swap(own)]
    table = [[group ^ place for place in range(groups)] for group in range(groups)]
    group_ids = jnp.asarray(table, jnp.int32)[lax.axis_index("ctx")]
    rows = (queries[0], key_rows[0], value_rows[0], out_grad[0])
    packed = pack_groups(group_ids, rows, groups)
    pair, packed = barrier((pair, packed))
    heads = exchange(packed)
    kept, give = work(pair)
    heads, kept, give = barrier((heads, kept, give))
    results = heads_back(heads)
    right, kept, give, results = barrier((right, kept, give, results))
    total = kept[0].astype(jnp.float32) + swap(give)
    results = exchange(results)
    steps, parts, arrived = [], [], []
    for d in range(1, half + 1):
        blocks = [right, swap(right)]
        following = []
        if d < half:
            following.append(hop(right, 1))
            blocks += [left, swap(left)]
            if d + 1 < half:
                following.append(hop(left, -1))
        if d > 1:
            sums = both_cores(kept, swap(give))
            sums, blocks = barrier((sums, blocks))
            arrived = [hop(part, step) for part, step in zip(sums, steps)]
        kept, give = work(blocks)
        following, arrived, results, kept, give = barrier(
            (following, arrived, results, kept, give)
        )
        right, left = (following + [None, None])[:2]
        parts += arrived
        steps = [-d, d] if d < half else [half]
    outs = unpack_groups(group_ids, results)
    for part, step in zip(both_cores(kept, swap(give)), steps):
        parts.append(hop(part, step))
    for part in parts:
        total = total + part
    return tuple(out[None] for out in outs) + (total.astype(jnp.bfloat16)[None],)


def solution(mesh):
    rows = P("exp", "ctx", None)
    experts = P("exp", None, None)
    return jax.shard_map(
        per_device,
        mesh=mesh,
        in_specs=(rows,) * 7 + (experts,) * 2,
        out_specs=(rows,) * 4,
        check_vma=False,
    )
```

```python
import functools

import jax
import jax.numpy as jnp
from jax import lax
from jax.experimental import pallas as pl
from jax.experimental.pallas import tpu as pltpu
from jax.sharding import PartitionSpec as P

HD = 128
CAP = 24
NOTES = 16
PARTS = 4
VMEM_BYTES = 36 * 1024 * 1024
VMEM_EXPERTS = 45 * 1024 * 1024
def cost(units):
    return pl.CostEstimate(
        flops=units * 10**9, bytes_accessed=units * 10**6, transcendentals=0
    )


SMALL = cost(0)
OWN_COST, HEADS_COST, NEAR_COST, FAR_COST = 30, 5, 0, 30
NT = (((1,), (1,)), ((), ()))
TN = (((0,), (0,)), ((), ()))


def dot_nt(left, right):
    return lax.dot_general(left, right, NT, preferred_element_type=jnp.float32)


def dot_tn(left, right):
    return lax.dot_general(left, right, TN, preferred_element_type=jnp.float32)


def dot_nn(left, right):
    return jnp.dot(left, right, preferred_element_type=jnp.float32)


def silu_slope(preact):
    sigmoid = jax.nn.sigmoid(preact)
    return sigmoid * (1.0 + preact * (1.0 - sigmoid))


def pack_kernel(group_ref, *refs):
    members, blocks = refs[:4], refs[4:]
    width = blocks[0].shape[2]
    for place, block in enumerate(blocks):
        first = pl.multiple_of(group_ref[place] * width, 128)
        for row, member in enumerate(members):
            block[row] = member[:, pl.ds(first, width)]


def pack_groups(group_ids, members, groups):
    bins, width = members[0].shape
    block = jax.ShapeDtypeStruct((4, bins, width // groups), jnp.bfloat16)
    return pl.pallas_call(
        pack_kernel,
        out_shape=[block] * groups,
        in_specs=[pl.BlockSpec(memory_space=pltpu.SMEM)]
        + [pl.BlockSpec(memory_space=pltpu.VMEM)] * 4,
        out_specs=[pl.BlockSpec(memory_space=pltpu.VMEM)] * groups,
        compiler_params=pltpu.CompilerParams(vmem_limit_bytes=VMEM_BYTES),
        cost_estimate=SMALL,
        name="pack_groups",
    )(group_ids, *members)


def unpack_kernel(group_ref, *refs):
    blocks, outs = refs[:-3], refs[-3:]
    width = blocks[0].shape[2]
    for place, block in enumerate(blocks):
        first = pl.multiple_of(group_ref[place] * width, 128)
        for row, out in enumerate(outs):
            out[:, pl.ds(first, width)] = block[row]


def unpack_groups(group_ids, blocks):
    groups = len(blocks)
    bins, width = blocks[0].shape[1], blocks[0].shape[2] * groups
    out = jax.ShapeDtypeStruct((bins, width), jnp.bfloat16)
    return pl.pallas_call(
        unpack_kernel,
        out_shape=[out] * 3,
        in_specs=[pl.BlockSpec(memory_space=pltpu.SMEM)]
        + [pl.BlockSpec(memory_space=pltpu.VMEM)] * groups,
        out_specs=[pl.BlockSpec(memory_space=pltpu.VMEM)] * 3,
        compiler_params=pltpu.CompilerParams(vmem_limit_bytes=VMEM_BYTES),
        cost_estimate=SMALL,
        name="unpack_groups",
    )(group_ids, *blocks)


def heads_kernel(*refs):
    count = len(refs) // 2
    blocks, outs = refs[:count], refs[count:]
    bins = blocks[0].shape[1]
    scale = HD ** (-0.5)
    query, key, value, grad = (
        jnp.concatenate([block[row] for block in blocks], axis=0) for row in range(4)
    )
    scores = dot_nt(key, query) * scale
    powers = jnp.exp(scores - jnp.max(scores, axis=0, keepdims=True))
    probs = powers * (1.0 / jnp.sum(powers, axis=0, keepdims=True))
    prob_grad = dot_nt(value, grad)
    row_delta = jnp.sum(probs * prob_grad, axis=0, keepdims=True)
    score_grad = (probs * (prob_grad - row_delta)).astype(jnp.bfloat16)
    results = (
        dot_tn(score_grad, key) * scale,
        dot_nn(score_grad, query) * scale,
        dot_nn(probs.astype(jnp.bfloat16), grad),
    )
    for row, result in enumerate(results):
        result = result.astype(jnp.bfloat16)
        for place, out in enumerate(outs):
            out[row] = result[place * bins : (place + 1) * bins]


def heads_back(blocks):
    groups = len(blocks)
    bins, width = blocks[0].shape[1:]
    rows = bins * groups
    heads = width // HD
    return pl.pallas_call(
        heads_kernel,
        grid=(heads,),
        out_shape=[jax.ShapeDtypeStruct((3, bins, width), jnp.bfloat16)] * groups,
        in_specs=[pl.BlockSpec((4, bins, HD), lambda h: (0, 0, h))] * groups,
        out_specs=[pl.BlockSpec((3, bins, HD), lambda h: (0, 0, h))] * groups,
        compiler_params=pltpu.CompilerParams(vmem_limit_bytes=VMEM_BYTES),
        cost_estimate=cost(HEADS_COST),
        name="heads_back",
    )(*blocks)


def exchange(blocks):
    groups = len(blocks)
    return [blocks[0]] + [
        lax.ppermute(blocks[place], "ctx", [(i, i ^ place) for i in range(groups)])
        for place in range(1, groups)
    ]


def block_kernel(tokens_ref, grads_ref, routes_ref, gates_ref, block_ref):
    bins, width = tokens_ref.shape
    block_ref[:bins] = tokens_ref[...]
    block_ref[bins : 2 * bins] = grads_ref[...]
    rest = gates_ref[...]
    pieces = [(routes_ref[...] + 1).astype(jnp.float32)]
    for _ in range(3):
        piece = rest.astype(jnp.bfloat16).astype(jnp.float32)
        rest = rest - piece
        pieces.append(piece)
    block_ref[2 * bins :, bins:] = jnp.zeros((NOTES, width - bins), jnp.bfloat16)
    block_ref[2 * bins :, :bins] = jnp.concatenate(pieces, axis=0).astype(jnp.bfloat16)


def make_block(tokens, grads, routes, gates):
    bins, width = tokens.shape
    return pl.pallas_call(
        block_kernel,
        out_shape=jax.ShapeDtypeStruct((2 * bins + NOTES, width), jnp.bfloat16),
        compiler_params=pltpu.CompilerParams(vmem_limit_bytes=VMEM_BYTES),
        cost_estimate=SMALL,
        name="make_block",
    )(tokens, grads, routes.T, gates.T)


def expert_kernel(layout, pieces, top, base_ref, *refs):
    sources, count = len(layout), sum(layout)
    block_refs, refs = refs[:count], refs[count:]
    up_hbm, down_hbm = refs[:2]
    keep_refs = refs[2 : 2 + sources // 2]
    give_refs = refs[2 + sources // 2 : -7]
    pick_ref, token_rows, gated_rows, back_rows, up_ref, down_ref, sems = refs[-7:]
    bins = keep_refs[0].shape[0]
    slots = sources * CAP
    experts = pick_ref.shape[0] // slots

    def copies(expert):
        place = expert % 2
        return [
            pltpu.make_async_copy(
                hbm.at[expert, pl.ds(part * (hbm.shape[1] // PARTS), hbm.shape[1] // PARTS)],
                vmem.at[place, pl.ds(part * (hbm.shape[1] // PARTS), hbm.shape[1] // PARTS)],
                sems.at[place, PARTS * which + part],
            )
            for which, (hbm, vmem) in enumerate(((up_hbm, up_ref), (down_hbm, down_ref)))
            for part in range(PARTS)
        ]

    for copy in copies(0):
        copy.start()

    def pick_rows():
        blocks, first = [], 0
        for length in layout:
            members = [ref[...] for ref in block_refs[first : first + length]]
            blocks.append(jnp.concatenate(members, axis=0) if length > 1 else members[0])
            first += length
        earlier = lax.broadcasted_iota(jnp.int32, (bins, bins), 0)
        later = lax.broadcasted_iota(jnp.int32, (bins, bins), 1)
        before = (earlier < later).astype(jnp.bfloat16)
        slot = lax.broadcasted_iota(jnp.int32, (slots, bins), 0).astype(jnp.float32)
        base = base_ref[0].astype(jnp.float32)
        gates = [jnp.zeros((slots, 1), jnp.float32)] * experts
        for source, block in enumerate(blocks):
            notes = block[2 * bins :, :bins].astype(jnp.float32)
            named = notes[:top] - base
            weights = notes[top : 2 * top] + notes[2 * top : 3 * top] + notes[3 * top : 4 * top]
            hits = [(named == float(local + 1)).astype(jnp.float32) for local in range(experts)]
            chosen = [jnp.sum(hit, axis=0, keepdims=True) for hit in hits]
            stacked = jnp.concatenate(chosen, axis=0)
            position = dot_nn(stacked.astype(jnp.bfloat16), before)
            for local in range(experts):
                place = jnp.where(
                    chosen[local] > 0.0, position[local : local + 1] + float(source * CAP), -1.0
                )
                pick = (slot == place).astype(jnp.float32)
                gate = jnp.sum(hits[local] * weights, axis=0, keepdims=True)
                gates[local] = gates[local] + jnp.sum(pick * gate, axis=1, keepdims=True)
                pick_ref[
                    local * slots : (local + 1) * slots, source * bins : (source + 1) * bins
                ] = pick.astype(jnp.bfloat16)
        picks = pick_ref[...]
        tokens = jnp.concatenate([block[:bins] for block in blocks], axis=0)
        token_rows[...] = dot_nn(picks, tokens).astype(jnp.bfloat16)
        grads = jnp.concatenate([block[bins : 2 * bins] for block in blocks], axis=0)
        gate_column = jnp.concatenate(gates, axis=0)
        gated_rows[...] = (gate_column * dot_nn(picks, grads)).astype(jnp.bfloat16)

    pick_rows()

    @pl.loop(0, experts)
    def _(expert):
        @pl.when(expert + 1 < experts)
        def _():
            for copy in copies(expert + 1):
                copy.start()

        for copy in copies(expert):
            copy.wait()
        place = expert % 2
        rows = pl.ds(pl.multiple_of(expert * slots, 16), slots)
        preact = dot_nn(token_rows[rows, :], up_ref[place])
        back_grad = dot_nt(gated_rows[rows, :], down_ref[place])
        hidden_grad = (back_grad * silu_slope(preact)).astype(jnp.bfloat16)
        back_rows[rows, :] = dot_nt(hidden_grad, up_ref[place]).astype(jnp.bfloat16)

    sums = dot_tn(pick_ref[...], back_rows[...])
    for pair, keep in enumerate(keep_refs):
        mine, other = 2 * pair * bins, (2 * pair + 1) * bins
        keep[...] = sums[mine : mine + bins].astype(jnp.bfloat16)
        for piece in range(pieces):
            rows = bins // pieces
            give_refs[pair * pieces + piece][...] = sums[
                other + piece * rows : other + (piece + 1) * rows
            ].astype(jnp.bfloat16)


def expert_back(base, blocks, up_weight, down_weight, bins, top, units, pieces):
    sources = len(blocks)
    layout = [len(block) for block in blocks]
    experts, width, hidden = up_weight.shape
    slots = sources * CAP
    pairs = sources // 2
    return pl.pallas_call(
        functools.partial(expert_kernel, layout, pieces, top),
        out_shape=[jax.ShapeDtypeStruct((bins, width), jnp.bfloat16)] * pairs
        + [jax.ShapeDtypeStruct((bins // pieces, width), jnp.bfloat16)] * (pairs * pieces),
        in_specs=[pl.BlockSpec(memory_space=pltpu.SMEM)]
        + [pl.BlockSpec(memory_space=pltpu.VMEM)] * sum(layout)
        + [pl.BlockSpec(memory_space=pltpu.HBM)] * 2,
        out_specs=[pl.BlockSpec(memory_space=pltpu.VMEM)] * (pairs * (1 + pieces)),
        scratch_shapes=[
            pltpu.VMEM((experts * slots, sources * bins), jnp.bfloat16),
            pltpu.VMEM((experts * slots, width), jnp.bfloat16),
            pltpu.VMEM((experts * slots, width), jnp.bfloat16),
            pltpu.VMEM((experts * slots, width), jnp.bfloat16),
            pltpu.VMEM((2, width, hidden), jnp.bfloat16),
            pltpu.VMEM((2, hidden, width), jnp.bfloat16),
            pltpu.SemaphoreType.DMA((2, 2 * PARTS)),
        ],
        compiler_params=pltpu.CompilerParams(vmem_limit_bytes=VMEM_EXPERTS),
        cost_estimate=cost(units),
        name="expert_back",
    )(base, *[piece for block in blocks for piece in block], up_weight, down_weight)


def per_device(
    queries, key_rows, value_rows, out_grad, moe_input, routes, route_gates, up_weight, down_weight
):
    members = lax.axis_size("exp")
    me = lax.axis_index("exp")
    groups = lax.axis_size("ctx")
    chips = members // 2
    half = chips // 2
    _, bins, top = routes.shape
    base = (me * up_weight.shape[0]).astype(jnp.int32).reshape(1)

    def swap(block):
        return lax.ppermute(block, "exp", [(i, i ^ 1) for i in range(members)])

    def hop(block, step):
        return lax.ppermute(
            block, "exp", [(i, (i + 2 * step) % members) for i in range(members)]
        )

    def pair(block):
        return [[block], [swap(block)]]

    def pair_in_pieces(block):
        cuts = [0, bins // 2, bins, bins + bins // 2, block.shape[0]]
        return [[block], [swap(block[a:b]) for a, b in zip(cuts, cuts[1:])]]

    def work(blocks, units, pieces=1):
        outs = expert_back(base, blocks, up_weight, down_weight, bins, top, units, pieces)
        return outs[: len(blocks) // 2], outs[len(blocks) // 2 :]

    def both_cores(kept, given):
        pieces = len(given) // len(kept)
        return [
            (
                own.astype(jnp.float32)
                + jnp.concatenate(given[place * pieces : (place + 1) * pieces], axis=0)
            ).astype(jnp.bfloat16)
            for place, own in enumerate(kept)
        ]

    barrier = lax.optimization_barrier
    own = make_block(moe_input[0], out_grad[0], routes[0], route_gates[0])
    right, left = hop(own, 1), hop(own, -1)
    own_pair = pair(own)
    table = [[group ^ place for place in range(groups)] for group in range(groups)]
    group_ids = jnp.asarray(table, jnp.int32)[lax.axis_index("ctx")]
    rows = (queries[0], key_rows[0], value_rows[0], out_grad[0])
    packed = pack_groups(group_ids, rows, groups)
    own_pair, packed = barrier((own_pair, packed))
    heads = exchange(packed)
    kept, give = work(own_pair, OWN_COST)
    heads, kept, give, left = barrier((heads, kept, give, left))
    results = heads_back(heads)
    right, kept, give, results = barrier((right, kept, give, results))
    total = both_cores(kept, [swap(part) for part in give])[0].astype(jnp.float32)
    results = exchange(results)
    steps, parts, arrived = [], [], []
    for d in range(1, half):
        blocks = pair(left) + pair_in_pieces(right)
        following = [hop(left, -1)]
        if d + 1 < half:
            following.append(hop(right, 1))
        if d > 1:
            blocks, sums = barrier((blocks, sums))
            arrived = [hop(part, step) for part, step in zip(sums, steps)]
        kept, give = work(blocks, NEAR_COST)
        following, arrived, results, kept, give = barrier(
            (following, arrived, results, kept, give)
        )
        parts += arrived
        sums = both_cores(kept, [swap(part) for part in give])
        left, right = (following + [None])[:2]
        steps = [d, -d]
    blocks, sums = barrier((pair(left), sums))
    arrived = [hop(part, step) for part, step in zip(sums, steps)]
    kept, give = work(blocks, FAR_COST, 2)
    given = [swap(part) for part in give]
    kept, given, arrived = barrier((kept, given, arrived))
    parts += arrived
    for part in parts:
        total = total + part
    far = hop(both_cores(kept, given)[0], half)
    outs = unpack_groups(group_ids, results)
    total = total + far
    return tuple(out[None] for out in outs) + (total.astype(jnp.bfloat16)[None],)


def solution(mesh):
    rows = P("exp", "ctx", None)
    experts = P("exp", None, None)
    return jax.shard_map(
        per_device,
        mesh=mesh,
        in_specs=(rows,) * 7 + (experts,) * 2,
        out_specs=(rows,) * 4,
        check_vma=False,
    )
```

```python
import functools

import jax
import jax.numpy as jnp
from jax import lax
from jax.experimental import pallas as pl
from jax.experimental.pallas import tpu as pltpu
from jax.sharding import PartitionSpec as P

HD = 128
CAP = 24
NOTES = 16
PARTS = 4
VMEM_BYTES = 36 * 1024 * 1024
VMEM_EXPERTS = 45 * 1024 * 1024
def cost(units):
    return pl.CostEstimate(
        flops=units * 10**9, bytes_accessed=units * 10**6, transcendentals=0
    )


SMALL = cost(0)
OWN_COST, HEADS_COST, LEFT_COST, FAR_COST, RIGHT_COST = 30, 30, 0, 0, 30
NT = (((1,), (1,)), ((), ()))
TN = (((0,), (0,)), ((), ()))


def dot_nt(left, right):
    return lax.dot_general(left, right, NT, preferred_element_type=jnp.float32)


def dot_tn(left, right):
    return lax.dot_general(left, right, TN, preferred_element_type=jnp.float32)


def dot_nn(left, right):
    return jnp.dot(left, right, preferred_element_type=jnp.float32)


def silu_slope(preact):
    sigmoid = jax.nn.sigmoid(preact)
    return sigmoid * (1.0 + preact * (1.0 - sigmoid))


def pack_kernel(group_ref, *refs):
    members, blocks = refs[:4], refs[4:]
    width = blocks[0].shape[2]
    for place, block in enumerate(blocks):
        first = pl.multiple_of(group_ref[place] * width, 128)
        for row, member in enumerate(members):
            block[row] = member[:, pl.ds(first, width)]


def pack_groups(group_ids, members, groups):
    bins, width = members[0].shape
    block = jax.ShapeDtypeStruct((4, bins, width // groups), jnp.bfloat16)
    return pl.pallas_call(
        pack_kernel,
        out_shape=[block] * groups,
        in_specs=[pl.BlockSpec(memory_space=pltpu.SMEM)]
        + [pl.BlockSpec(memory_space=pltpu.VMEM)] * 4,
        out_specs=[pl.BlockSpec(memory_space=pltpu.VMEM)] * groups,
        compiler_params=pltpu.CompilerParams(vmem_limit_bytes=VMEM_BYTES),
        cost_estimate=SMALL,
        name="pack_groups",
    )(group_ids, *members)


def unpack_kernel(group_ref, *refs):
    blocks, outs = refs[:-3], refs[-3:]
    width = blocks[0].shape[2]
    for place, block in enumerate(blocks):
        first = pl.multiple_of(group_ref[place] * width, 128)
        for row, out in enumerate(outs):
            out[:, pl.ds(first, width)] = block[row]


def unpack_groups(group_ids, blocks):
    groups = len(blocks)
    bins, width = blocks[0].shape[1], blocks[0].shape[2] * groups
    out = jax.ShapeDtypeStruct((bins, width), jnp.bfloat16)
    return pl.pallas_call(
        unpack_kernel,
        out_shape=[out] * 3,
        in_specs=[pl.BlockSpec(memory_space=pltpu.SMEM)]
        + [pl.BlockSpec(memory_space=pltpu.VMEM)] * groups,
        out_specs=[pl.BlockSpec(memory_space=pltpu.VMEM)] * 3,
        compiler_params=pltpu.CompilerParams(vmem_limit_bytes=VMEM_BYTES),
        cost_estimate=SMALL,
        name="unpack_groups",
    )(group_ids, *blocks)


def heads_kernel(*refs):
    count = len(refs) // 2
    blocks, outs = refs[:count], refs[count:]
    bins = blocks[0].shape[1]
    scale = HD ** (-0.5)
    query, key, value, grad = (
        jnp.concatenate([block[row] for block in blocks], axis=0) for row in range(4)
    )
    scores = dot_nt(key, query) * scale
    powers = jnp.exp(scores - jnp.max(scores, axis=0, keepdims=True))
    probs = powers * (1.0 / jnp.sum(powers, axis=0, keepdims=True))
    prob_grad = dot_nt(value, grad)
    row_delta = jnp.sum(probs * prob_grad, axis=0, keepdims=True)
    score_grad = (probs * (prob_grad - row_delta)).astype(jnp.bfloat16)
    results = (
        dot_tn(score_grad, key) * scale,
        dot_nn(score_grad, query) * scale,
        dot_nn(probs.astype(jnp.bfloat16), grad),
    )
    for row, result in enumerate(results):
        result = result.astype(jnp.bfloat16)
        for place, out in enumerate(outs):
            out[row] = result[place * bins : (place + 1) * bins]


def heads_back(blocks):
    groups = len(blocks)
    bins, width = blocks[0].shape[1:]
    rows = bins * groups
    heads = width // HD
    return pl.pallas_call(
        heads_kernel,
        grid=(heads,),
        out_shape=[jax.ShapeDtypeStruct((3, bins, width), jnp.bfloat16)] * groups,
        in_specs=[pl.BlockSpec((4, bins, HD), lambda h: (0, 0, h))] * groups,
        out_specs=[pl.BlockSpec((3, bins, HD), lambda h: (0, 0, h))] * groups,
        compiler_params=pltpu.CompilerParams(vmem_limit_bytes=VMEM_BYTES),
        cost_estimate=cost(HEADS_COST),
        name="heads_back",
    )(*blocks)


def exchange(blocks):
    groups = len(blocks)
    return [blocks[0]] + [
        lax.ppermute(blocks[place], "ctx", [(i, i ^ place) for i in range(groups)])
        for place in range(1, groups)
    ]


def block_kernel(tokens_ref, grads_ref, routes_ref, gates_ref, block_ref, rows_ref):
    bins, width = tokens_ref.shape
    rest = gates_ref[...]
    pieces = [(routes_ref[...] + 1).astype(jnp.float32)]
    for _ in range(3):
        piece = rest.astype(jnp.bfloat16).astype(jnp.float32)
        rest = rest - piece
        pieces.append(piece)
    notes = jnp.concatenate(pieces, axis=0).astype(jnp.bfloat16)
    for out in (block_ref, rows_ref):
        out[:bins] = tokens_ref[...]
        out[bins : bins + NOTES, bins:] = jnp.zeros((NOTES, width - bins), jnp.bfloat16)
        out[bins : bins + NOTES, :bins] = notes
    block_ref[bins + NOTES :] = grads_ref[...]


def make_block(tokens, grads, routes, gates):
    bins, width = tokens.shape
    return pl.pallas_call(
        block_kernel,
        out_shape=[
            jax.ShapeDtypeStruct((2 * bins + NOTES, width), jnp.bfloat16),
            jax.ShapeDtypeStruct((bins + NOTES, width), jnp.bfloat16),
        ],
        compiler_params=pltpu.CompilerParams(vmem_limit_bytes=VMEM_BYTES),
        cost_estimate=SMALL,
        name="make_block",
    )(tokens, grads, routes.T, gates.T)


def expert_kernel(layout, pieces, top, base_ref, *refs):
    sources, count = len(layout), sum(layout)
    block_refs, refs = refs[:count], refs[count:]
    up_hbm, down_hbm = refs[:2]
    keep_refs = refs[2 : 2 + sources // 2]
    give_refs = refs[2 + sources // 2 : -7]
    pick_ref, token_rows, gated_rows, back_rows, up_ref, down_ref, sems = refs[-7:]
    bins = keep_refs[0].shape[0]
    slots = sources * CAP
    experts = pick_ref.shape[0] // slots

    def copies(expert):
        place = expert % 2
        return [
            pltpu.make_async_copy(
                hbm.at[expert, pl.ds(part * (hbm.shape[1] // PARTS), hbm.shape[1] // PARTS)],
                vmem.at[place, pl.ds(part * (hbm.shape[1] // PARTS), hbm.shape[1] // PARTS)],
                sems.at[place, PARTS * which + part],
            )
            for which, (hbm, vmem) in enumerate(((up_hbm, up_ref), (down_hbm, down_ref)))
            for part in range(PARTS)
        ]

    for copy in copies(0):
        copy.start()

    def pick_rows():
        blocks, first = [], 0
        for length in layout:
            members = [ref[...] for ref in block_refs[first : first + length]]
            blocks.append(jnp.concatenate(members, axis=0) if length > 1 else members[0])
            first += length
        earlier = lax.broadcasted_iota(jnp.int32, (bins, bins), 0)
        later = lax.broadcasted_iota(jnp.int32, (bins, bins), 1)
        before = (earlier < later).astype(jnp.bfloat16)
        slot = lax.broadcasted_iota(jnp.int32, (slots, bins), 0).astype(jnp.float32)
        base = base_ref[0].astype(jnp.float32)
        gates = [jnp.zeros((slots, 1), jnp.float32)] * experts
        for source, block in enumerate(blocks):
            notes = block[bins : bins + NOTES, :bins].astype(jnp.float32)
            named = notes[:top] - base
            weights = notes[top : 2 * top] + notes[2 * top : 3 * top] + notes[3 * top : 4 * top]
            hits = [(named == float(local + 1)).astype(jnp.float32) for local in range(experts)]
            chosen = [jnp.sum(hit, axis=0, keepdims=True) for hit in hits]
            stacked = jnp.concatenate(chosen, axis=0)
            position = dot_nn(stacked.astype(jnp.bfloat16), before)
            for local in range(experts):
                place = jnp.where(
                    chosen[local] > 0.0, position[local : local + 1] + float(source * CAP), -1.0
                )
                pick = (slot == place).astype(jnp.float32)
                gate = jnp.sum(hits[local] * weights, axis=0, keepdims=True)
                gates[local] = gates[local] + jnp.sum(pick * gate, axis=1, keepdims=True)
                pick_ref[
                    local * slots : (local + 1) * slots, source * bins : (source + 1) * bins
                ] = pick.astype(jnp.bfloat16)
        picks = pick_ref[...]
        tokens = jnp.concatenate([block[:bins] for block in blocks], axis=0)
        token_rows[...] = dot_nn(picks, tokens).astype(jnp.bfloat16)
        grads = jnp.concatenate([block[bins + NOTES :] for block in blocks], axis=0)
        gate_column = jnp.concatenate(gates, axis=0)
        gated_rows[...] = (gate_column * dot_nn(picks, grads)).astype(jnp.bfloat16)

    pick_rows()

    @pl.loop(0, experts)
    def _(expert):
        @pl.when(expert + 1 < experts)
        def _():
            for copy in copies(expert + 1):
                copy.start()

        for copy in copies(expert):
            copy.wait()
        place = expert % 2
        rows = pl.ds(pl.multiple_of(expert * slots, 16), slots)
        preact = dot_nn(token_rows[rows, :], up_ref[place])
        back_grad = dot_nt(gated_rows[rows, :], down_ref[place])
        hidden_grad = (back_grad * silu_slope(preact)).astype(jnp.bfloat16)
        back_rows[rows, :] = dot_nt(hidden_grad, up_ref[place]).astype(jnp.bfloat16)

    sums = dot_tn(pick_ref[...], back_rows[...])
    for pair, keep in enumerate(keep_refs):
        mine, other = 2 * pair * bins, (2 * pair + 1) * bins
        keep[...] = sums[mine : mine + bins].astype(jnp.bfloat16)
        for piece in range(pieces):
            rows = bins // pieces
            give_refs[pair * pieces + piece][...] = sums[
                other + piece * rows : other + (piece + 1) * rows
            ].astype(jnp.bfloat16)


def expert_back(base, blocks, up_weight, down_weight, bins, top, units, pieces):
    sources = len(blocks)
    layout = [len(block) for block in blocks]
    experts, width, hidden = up_weight.shape
    slots = sources * CAP
    pairs = sources // 2
    return pl.pallas_call(
        functools.partial(expert_kernel, layout, pieces, top),
        out_shape=[jax.ShapeDtypeStruct((bins, width), jnp.bfloat16)] * pairs
        + [jax.ShapeDtypeStruct((bins // pieces, width), jnp.bfloat16)] * (pairs * pieces),
        in_specs=[pl.BlockSpec(memory_space=pltpu.SMEM)]
        + [pl.BlockSpec(memory_space=pltpu.VMEM)] * sum(layout)
        + [pl.BlockSpec(memory_space=pltpu.HBM)] * 2,
        out_specs=[pl.BlockSpec(memory_space=pltpu.VMEM)] * (pairs * (1 + pieces)),
        scratch_shapes=[
            pltpu.VMEM((experts * slots, sources * bins), jnp.bfloat16),
            pltpu.VMEM((experts * slots, width), jnp.bfloat16),
            pltpu.VMEM((experts * slots, width), jnp.bfloat16),
            pltpu.VMEM((experts * slots, width), jnp.bfloat16),
            pltpu.VMEM((2, width, hidden), jnp.bfloat16),
            pltpu.VMEM((2, hidden, width), jnp.bfloat16),
            pltpu.SemaphoreType.DMA((2, 2 * PARTS)),
        ],
        compiler_params=pltpu.CompilerParams(vmem_limit_bytes=VMEM_EXPERTS),
        cost_estimate=cost(units),
        name="expert_back",
    )(base, *[piece for block in blocks for piece in block], up_weight, down_weight)


def per_device(
    queries, key_rows, value_rows, out_grad, moe_input, routes, route_gates, up_weight, down_weight
):
    members = lax.axis_size("exp")
    me = lax.axis_index("exp")
    groups = lax.axis_size("ctx")
    chips = members // 2
    half = chips // 2
    _, bins, top = routes.shape
    base = (me * up_weight.shape[0]).astype(jnp.int32).reshape(1)

    def swap(block):
        return lax.ppermute(block, "exp", [(i, i ^ 1) for i in range(members)])

    def hop(block, step):
        return lax.ppermute(
            block, "exp", [(i, (i + 2 * step) % members) for i in range(members)]
        )

    def pair(*pieces):
        return [list(pieces), [swap(piece) for piece in pieces]]

    def work(blocks, units, pieces=1):
        kept, *give = expert_back(base, blocks, up_weight, down_weight, bins, top, units, pieces)
        return kept, give

    def add_up(*members):
        return functools.reduce(jnp.add, [member.astype(jnp.float32) for member in members])

    def joined(pieces):
        return pieces[0] if len(pieces) == 1 else jnp.concatenate(pieces, axis=0)

    barrier = lax.optimization_barrier
    own, own_rows = make_block(moe_input[0], out_grad[0], routes[0], route_gates[0])
    left, right_rows = hop(own, -1), hop(own_rows, 1)
    own_pair = pair(own)
    table = [[group ^ place for place in range(groups)] for group in range(groups)]
    group_ids = jnp.asarray(table, jnp.int32)[lax.axis_index("ctx")]
    rows = (queries[0], key_rows[0], value_rows[0], out_grad[0])
    packed = pack_groups(group_ids, rows, groups)
    own_pair, packed = barrier((own_pair, packed))
    heads = exchange(packed)
    kept, give = work(own_pair, OWN_COST)
    heads, kept, give, left = barrier((heads, kept, give, left))
    total = add_up(kept, joined([swap(piece) for piece in give]))
    left_pair, right_grads = pair(left), out_grad[0]
    results = heads_back(heads)
    left_pair, results = barrier((left_pair, results))
    results = exchange(results)
    left_sums = []
    for d in range(1, half):
        left = hop(left, -1)
        kept, give = work(left_pair, LEFT_COST)
        left, right_rows, results, kept, give = barrier((left, right_rows, results, kept, give))
        left_sums.append(add_up(kept, joined([swap(piece) for piece in give])))
        left_pair = pair(left)
    carried = None
    for sums in reversed(left_sums):
        if carried is not None:
            sums = add_up(sums, carried)
        carried = hop(sums.astype(jnp.bfloat16), 1)
    rights = [(right_rows, hop(right_grads, 1))]
    for d in range(2, half):
        rights.append(tuple(hop(member, 1) for member in rights[-1]))
    kept, give = work(left_pair, FAR_COST)
    carried, rights, kept, give = barrier((carried, rights, kept, give))
    total = add_up(total, carried)
    carried = add_up(kept, joined([swap(piece) for piece in give]))
    for right in reversed(rights):
        carried = hop(carried.astype(jnp.bfloat16), -1)
        kept, give = work(pair(*right), RIGHT_COST, 2)
        given = [swap(piece) for piece in give]
        kept, given, carried = barrier((kept, given, carried))
        carried = add_up(kept, joined(given), carried)
    carried = hop(carried.astype(jnp.bfloat16), -1)
    outs = unpack_groups(group_ids, results)
    total = add_up(total, carried).astype(jnp.bfloat16)
    return tuple(out[None] for out in outs) + (total[None],)


def solution(mesh):
    rows = P("exp", "ctx", None)
    experts = P("exp", None, None)
    return jax.shard_map(
        per_device,
        mesh=mesh,
        in_specs=(rows,) * 7 + (experts,) * 2,
        out_specs=(rows,) * 4,
        check_vma=False,
    )
```

```python
import functools

import jax
import jax.numpy as jnp
from jax import lax
from jax.experimental import pallas as pl
from jax.experimental.pallas import tpu as pltpu
from jax.sharding import PartitionSpec as P

HD = 128
CAP = 24
NOTES = 16
PARTS = 4
VMEM_BYTES = 36 * 1024 * 1024
VMEM_EXPERTS = 45 * 1024 * 1024
def cost(units):
    return pl.CostEstimate(
        flops=units * 10**9, bytes_accessed=units * 10**6, transcendentals=0
    )


SMALL = cost(0)
OWN_COST, HEADS_COST, LEFT_COST, FAR_COST, RIGHT_COST = 30, 30, 0, 0, 30
NT = (((1,), (1,)), ((), ()))
TN = (((0,), (0,)), ((), ()))


def dot_nt(left, right):
    return lax.dot_general(left, right, NT, preferred_element_type=jnp.float32)


def dot_tn(left, right):
    return lax.dot_general(left, right, TN, preferred_element_type=jnp.float32)


def dot_nn(left, right):
    return jnp.dot(left, right, preferred_element_type=jnp.float32)


def silu_slope(preact):
    sigmoid = jax.nn.sigmoid(preact)
    return sigmoid * (1.0 + preact * (1.0 - sigmoid))


def pack_kernel(group_ref, *refs):
    members, blocks = refs[:4], refs[4:]
    width = blocks[0].shape[2]
    for place, block in enumerate(blocks):
        first = pl.multiple_of(group_ref[place] * width, 128)
        for row, member in enumerate(members):
            block[row] = member[:, pl.ds(first, width)]


def pack_groups(group_ids, members, groups):
    bins, width = members[0].shape
    block = jax.ShapeDtypeStruct((4, bins, width // groups), jnp.bfloat16)
    return pl.pallas_call(
        pack_kernel,
        out_shape=[block] * groups,
        in_specs=[pl.BlockSpec(memory_space=pltpu.SMEM)]
        + [pl.BlockSpec(memory_space=pltpu.VMEM)] * 4,
        out_specs=[pl.BlockSpec(memory_space=pltpu.VMEM)] * groups,
        compiler_params=pltpu.CompilerParams(vmem_limit_bytes=VMEM_BYTES),
        cost_estimate=SMALL,
        name="pack_groups",
    )(group_ids, *members)


def unpack_kernel(group_ref, *refs):
    blocks, outs = refs[:-3], refs[-3:]
    width = blocks[0].shape[2]
    for place, block in enumerate(blocks):
        first = pl.multiple_of(group_ref[place] * width, 128)
        for row, out in enumerate(outs):
            out[:, pl.ds(first, width)] = block[row]


def unpack_groups(group_ids, blocks):
    groups = len(blocks)
    bins, width = blocks[0].shape[1], blocks[0].shape[2] * groups
    out = jax.ShapeDtypeStruct((bins, width), jnp.bfloat16)
    return pl.pallas_call(
        unpack_kernel,
        out_shape=[out] * 3,
        in_specs=[pl.BlockSpec(memory_space=pltpu.SMEM)]
        + [pl.BlockSpec(memory_space=pltpu.VMEM)] * groups,
        out_specs=[pl.BlockSpec(memory_space=pltpu.VMEM)] * 3,
        compiler_params=pltpu.CompilerParams(vmem_limit_bytes=VMEM_BYTES),
        cost_estimate=SMALL,
        name="unpack_groups",
    )(group_ids, *blocks)


def heads_kernel(*refs):
    count = len(refs) // 2
    blocks, outs = refs[:count], refs[count:]
    bins = blocks[0].shape[1]
    scale = HD ** (-0.5)
    query, key, value, grad = (
        jnp.concatenate([block[row] for block in blocks], axis=0) for row in range(4)
    )
    scores = dot_nt(key, query) * scale
    powers = jnp.exp(scores - jnp.max(scores, axis=0, keepdims=True))
    probs = powers * (1.0 / jnp.sum(powers, axis=0, keepdims=True))
    prob_grad = dot_nt(value, grad)
    row_delta = jnp.sum(probs * prob_grad, axis=0, keepdims=True)
    score_grad = (probs * (prob_grad - row_delta)).astype(jnp.bfloat16)
    results = (
        dot_tn(score_grad, key) * scale,
        dot_nn(score_grad, query) * scale,
        dot_nn(probs.astype(jnp.bfloat16), grad),
    )
    for row, result in enumerate(results):
        result = result.astype(jnp.bfloat16)
        for place, out in enumerate(outs):
            out[row] = result[place * bins : (place + 1) * bins]


def heads_back(blocks):
    groups = len(blocks)
    bins, width = blocks[0].shape[1:]
    rows = bins * groups
    heads = width // HD
    return pl.pallas_call(
        heads_kernel,
        grid=(heads,),
        out_shape=[jax.ShapeDtypeStruct((3, bins, width), jnp.bfloat16)] * groups,
        in_specs=[pl.BlockSpec((4, bins, HD), lambda h: (0, 0, h))] * groups,
        out_specs=[pl.BlockSpec((3, bins, HD), lambda h: (0, 0, h))] * groups,
        compiler_params=pltpu.CompilerParams(vmem_limit_bytes=VMEM_BYTES),
        cost_estimate=cost(HEADS_COST),
        name="heads_back",
    )(*blocks)


def exchange(blocks):
    groups = len(blocks)
    return [blocks[0]] + [
        lax.ppermute(blocks[place], "ctx", [(i, i ^ place) for i in range(groups)])
        for place in range(1, groups)
    ]


def make_block(tokens, grads, routes, gates):
    rest = gates.T
    pieces = [(routes.T + 1).astype(jnp.float32)]
    for _ in range(3):
        piece = lax.reduce_precision(rest, 8, 7)
        rest = rest - piece
        pieces.append(piece)
    notes = jnp.concatenate(pieces, axis=0).astype(jnp.bfloat16)
    notes = jnp.pad(notes, ((0, NOTES - notes.shape[0]), (0, tokens.shape[1] - notes.shape[1])))
    return jnp.concatenate([tokens, notes, grads], axis=0)


def expert_kernel(layout, pieces, top, base_ref, *refs):
    sources, count = len(layout), sum(layout)
    block_refs, refs = refs[:count], refs[count:]
    up_hbm, down_hbm = refs[:2]
    keep_refs = refs[2 : 2 + sources // 2]
    give_refs = refs[2 + sources // 2 : -7]
    pick_ref, token_rows, gated_rows, back_rows, up_ref, down_ref, sems = refs[-7:]
    bins = keep_refs[0].shape[0]
    slots = sources * CAP
    experts = pick_ref.shape[0] // slots

    def copies(expert):
        place = expert % 2
        return [
            pltpu.make_async_copy(
                hbm.at[expert, pl.ds(part * (hbm.shape[1] // PARTS), hbm.shape[1] // PARTS)],
                vmem.at[place, pl.ds(part * (hbm.shape[1] // PARTS), hbm.shape[1] // PARTS)],
                sems.at[place, PARTS * which + part],
            )
            for which, (hbm, vmem) in enumerate(((up_hbm, up_ref), (down_hbm, down_ref)))
            for part in range(PARTS)
        ]

    for copy in copies(0):
        copy.start()

    def pick_rows():
        blocks, first = [], 0
        for length in layout:
            members = [ref[...] for ref in block_refs[first : first + length]]
            blocks.append(jnp.concatenate(members, axis=0) if length > 1 else members[0])
            first += length
        earlier = lax.broadcasted_iota(jnp.int32, (bins, bins), 0)
        later = lax.broadcasted_iota(jnp.int32, (bins, bins), 1)
        before = (earlier < later).astype(jnp.bfloat16)
        slot = lax.broadcasted_iota(jnp.int32, (slots, bins), 0).astype(jnp.float32)
        base = base_ref[0].astype(jnp.float32)
        gates = [jnp.zeros((slots, 1), jnp.float32)] * experts
        for source, block in enumerate(blocks):
            notes = block[bins : bins + NOTES, :bins].astype(jnp.float32)
            named = notes[:top] - base
            weights = notes[top : 2 * top] + notes[2 * top : 3 * top] + notes[3 * top : 4 * top]
            hits = [(named == float(local + 1)).astype(jnp.float32) for local in range(experts)]
            chosen = [jnp.sum(hit, axis=0, keepdims=True) for hit in hits]
            stacked = jnp.concatenate(chosen, axis=0)
            position = dot_nn(stacked.astype(jnp.bfloat16), before)
            for local in range(experts):
                place = jnp.where(
                    chosen[local] > 0.0, position[local : local + 1] + float(source * CAP), -1.0
                )
                pick = (slot == place).astype(jnp.float32)
                gate = jnp.sum(hits[local] * weights, axis=0, keepdims=True)
                gates[local] = gates[local] + jnp.sum(pick * gate, axis=1, keepdims=True)
                pick_ref[
                    local * slots : (local + 1) * slots, source * bins : (source + 1) * bins
                ] = pick.astype(jnp.bfloat16)
        picks = pick_ref[...]
        tokens = jnp.concatenate([block[:bins] for block in blocks], axis=0)
        token_rows[...] = dot_nn(picks, tokens).astype(jnp.bfloat16)
        grads = jnp.concatenate([block[bins + NOTES :] for block in blocks], axis=0)
        gate_column = jnp.concatenate(gates, axis=0)
        gated_rows[...] = (gate_column * dot_nn(picks, grads)).astype(jnp.bfloat16)

    pick_rows()

    @pl.loop(0, experts)
    def _(expert):
        @pl.when(expert + 1 < experts)
        def _():
            for copy in copies(expert + 1):
                copy.start()

        for copy in copies(expert):
            copy.wait()
        place = expert % 2
        rows = pl.ds(pl.multiple_of(expert * slots, 16), slots)
        preact = dot_nn(token_rows[rows, :], up_ref[place])
        back_grad = dot_nt(gated_rows[rows, :], down_ref[place])
        hidden_grad = (back_grad * silu_slope(preact)).astype(jnp.bfloat16)
        back_rows[rows, :] = dot_nt(hidden_grad, up_ref[place]).astype(jnp.bfloat16)

    sums = dot_tn(pick_ref[...], back_rows[...])
    for pair, keep in enumerate(keep_refs):
        mine, other = 2 * pair * bins, (2 * pair + 1) * bins
        keep[...] = sums[mine : mine + bins].astype(jnp.bfloat16)
        for piece in range(pieces):
            rows = bins // pieces
            give_refs[pair * pieces + piece][...] = sums[
                other + piece * rows : other + (piece + 1) * rows
            ].astype(jnp.bfloat16)


def expert_back(base, blocks, up_weight, down_weight, bins, top, units, pieces):
    sources = len(blocks)
    layout = [len(block) for block in blocks]
    experts, width, hidden = up_weight.shape
    slots = sources * CAP
    pairs = sources // 2
    return pl.pallas_call(
        functools.partial(expert_kernel, layout, pieces, top),
        out_shape=[jax.ShapeDtypeStruct((bins, width), jnp.bfloat16)] * pairs
        + [jax.ShapeDtypeStruct((bins // pieces, width), jnp.bfloat16)] * (pairs * pieces),
        in_specs=[pl.BlockSpec(memory_space=pltpu.SMEM)]
        + [pl.BlockSpec(memory_space=pltpu.VMEM)] * sum(layout)
        + [pl.BlockSpec(memory_space=pltpu.HBM)] * 2,
        out_specs=[pl.BlockSpec(memory_space=pltpu.VMEM)] * (pairs * (1 + pieces)),
        scratch_shapes=[
            pltpu.VMEM((experts * slots, sources * bins), jnp.bfloat16),
            pltpu.VMEM((experts * slots, width), jnp.bfloat16),
            pltpu.VMEM((experts * slots, width), jnp.bfloat16),
            pltpu.VMEM((experts * slots, width), jnp.bfloat16),
            pltpu.VMEM((2, width, hidden), jnp.bfloat16),
            pltpu.VMEM((2, hidden, width), jnp.bfloat16),
            pltpu.SemaphoreType.DMA((2, 2 * PARTS)),
        ],
        compiler_params=pltpu.CompilerParams(vmem_limit_bytes=VMEM_EXPERTS),
        cost_estimate=cost(units),
        name="expert_back",
    )(base, *[piece for block in blocks for piece in block], up_weight, down_weight)


def per_device(
    queries, key_rows, value_rows, out_grad, moe_input, routes, route_gates, up_weight, down_weight
):
    members = lax.axis_size("exp")
    me = lax.axis_index("exp")
    groups = lax.axis_size("ctx")
    chips = members // 2
    half = chips // 2
    _, bins, top = routes.shape
    base = (me * up_weight.shape[0]).astype(jnp.int32).reshape(1)

    def swap(block):
        return lax.ppermute(block, "exp", [(i, i ^ 1) for i in range(members)])

    def hop(block, step):
        return lax.ppermute(
            block, "exp", [(i, (i + 2 * step) % members) for i in range(members)]
        )

    def pair(*pieces):
        return [list(pieces), [swap(piece) for piece in pieces]]

    def work(blocks, units, pieces=1):
        kept, *give = expert_back(base, blocks, up_weight, down_weight, bins, top, units, pieces)
        return kept, give

    def add_up(*members):
        return functools.reduce(jnp.add, [member.astype(jnp.float32) for member in members])

    def joined(pieces):
        return pieces[0] if len(pieces) == 1 else jnp.concatenate(pieces, axis=0)

    barrier = lax.optimization_barrier
    own = make_block(moe_input[0], out_grad[0], routes[0], route_gates[0])
    left, right_rows = hop(own, -1), hop(own[: bins + NOTES], 1)
    own_pair = pair(own)
    table = [[group ^ place for place in range(groups)] for group in range(groups)]
    group_ids = jnp.asarray(table, jnp.int32)[lax.axis_index("ctx")]
    rows = (queries[0], key_rows[0], value_rows[0], out_grad[0])
    packed = pack_groups(group_ids, rows, groups)
    own_pair, packed = barrier((own_pair, packed))
    heads = exchange(packed)
    kept, give = work(own_pair, OWN_COST)
    heads, kept, give, left = barrier((heads, kept, give, left))
    total = add_up(kept, joined([swap(piece) for piece in give]))
    left_pair, right_grads = pair(left), out_grad[0]
    results = heads_back(heads)
    left_pair, results = barrier((left_pair, results))
    results = exchange(results)
    left_sums = []
    for d in range(1, half):
        left = hop(left, -1)
        kept, give = work(left_pair, LEFT_COST)
        left, right_rows, results, kept, give = barrier((left, right_rows, results, kept, give))
        left_sums.append(add_up(kept, joined([swap(piece) for piece in give])))
        left_pair = pair(left)
    carried = None
    for sums in reversed(left_sums):
        if carried is not None:
            sums = add_up(sums, carried)
        carried = hop(sums.astype(jnp.bfloat16), 1)
    rights = [(right_rows, hop(right_grads, 1))]
    for d in range(2, half):
        rights.append(tuple(hop(member, 1) for member in rights[-1]))
    kept, give = work(left_pair, FAR_COST)
    rights, kept, give = barrier((rights, kept, give))
    left_carried = carried
    carried = add_up(kept, joined([swap(piece) for piece in give]))
    for right in reversed(rights):
        carried = hop(carried.astype(jnp.bfloat16), -1)
        kept, give = work(pair(*right), RIGHT_COST, 2)
        given = [swap(piece) for piece in give]
        kept, given, carried, left_carried = barrier((kept, given, carried, left_carried))
        carried = add_up(kept, joined(given), carried)
    total = add_up(total, left_carried)
    carried = hop(carried.astype(jnp.bfloat16), -1)
    outs = unpack_groups(group_ids, results)
    total = add_up(total, carried).astype(jnp.bfloat16)
    return tuple(out[None] for out in outs) + (total[None],)


def solution(mesh):
    rows = P("exp", "ctx", None)
    experts = P("exp", None, None)
    return jax.shard_map(
        per_device,
        mesh=mesh,
        in_specs=(rows,) * 7 + (experts,) * 2,
        out_specs=(rows,) * 4,
        check_vma=False,
    )
```

```python
import functools

import jax
import jax.numpy as jnp
from jax import lax
from jax.experimental import pallas as pl
from jax.experimental.pallas import tpu as pltpu
from jax.sharding import PartitionSpec as P

HD = 128
CAP = 24
NOTES = 16
PARTS = 4
VMEM_BYTES = 36 * 1024 * 1024
VMEM_EXPERTS = 45 * 1024 * 1024
def cost(units):
    return pl.CostEstimate(
        flops=units * 10**9, bytes_accessed=units * 10**6, transcendentals=0
    )


SMALL = cost(0)
OWN_COST, HEADS_COST, LEFT_COST, FAR_COST, RIGHT_COST = 30, 30, 0, 0, 30
NT = (((1,), (1,)), ((), ()))
TN = (((0,), (0,)), ((), ()))


def dot_nt(left, right):
    return lax.dot_general(left, right, NT, preferred_element_type=jnp.float32)


def dot_tn(left, right):
    return lax.dot_general(left, right, TN, preferred_element_type=jnp.float32)


def dot_nn(left, right):
    return jnp.dot(left, right, preferred_element_type=jnp.float32)


def silu_slope(preact):
    sigmoid = jax.nn.sigmoid(preact)
    return sigmoid * (1.0 + preact * (1.0 - sigmoid))


def pack_kernel(group_ref, *refs):
    members, blocks = refs[:4], refs[4:]
    width = blocks[0].shape[2]
    for place, block in enumerate(blocks):
        first = pl.multiple_of(group_ref[place] * width, 128)
        for row, member in enumerate(members):
            block[row] = member[:, pl.ds(first, width)]


def pack_groups(group_ids, members, groups):
    bins, width = members[0].shape
    block = jax.ShapeDtypeStruct((4, bins, width // groups), jnp.bfloat16)
    return pl.pallas_call(
        pack_kernel,
        out_shape=[block] * groups,
        in_specs=[pl.BlockSpec(memory_space=pltpu.SMEM)]
        + [pl.BlockSpec(memory_space=pltpu.VMEM)] * 4,
        out_specs=[pl.BlockSpec(memory_space=pltpu.VMEM)] * groups,
        compiler_params=pltpu.CompilerParams(vmem_limit_bytes=VMEM_BYTES),
        cost_estimate=SMALL,
        name="pack_groups",
    )(group_ids, *members)


def unpack_kernel(group_ref, *refs):
    blocks, outs = refs[:-3], refs[-3:]
    width = blocks[0].shape[2]
    for place, block in enumerate(blocks):
        first = pl.multiple_of(group_ref[place] * width, 128)
        for row, out in enumerate(outs):
            out[:, pl.ds(first, width)] = block[row]


def unpack_groups(group_ids, blocks):
    groups = len(blocks)
    bins, width = blocks[0].shape[1], blocks[0].shape[2] * groups
    out = jax.ShapeDtypeStruct((bins, width), jnp.bfloat16)
    return pl.pallas_call(
        unpack_kernel,
        out_shape=[out] * 3,
        in_specs=[pl.BlockSpec(memory_space=pltpu.SMEM)]
        + [pl.BlockSpec(memory_space=pltpu.VMEM)] * groups,
        out_specs=[pl.BlockSpec(memory_space=pltpu.VMEM)] * 3,
        compiler_params=pltpu.CompilerParams(vmem_limit_bytes=VMEM_BYTES),
        cost_estimate=SMALL,
        name="unpack_groups",
    )(group_ids, *blocks)


def heads_kernel(*refs):
    count = len(refs) // 2
    blocks, outs = refs[:count], refs[count:]
    bins = blocks[0].shape[1]
    scale = HD ** (-0.5)
    query, key, value, grad = (
        jnp.concatenate([block[row] for block in blocks], axis=0) for row in range(4)
    )
    scores = dot_nt(key, query) * scale
    powers = jnp.exp(scores - jnp.max(scores, axis=0, keepdims=True))
    probs = powers * (1.0 / jnp.sum(powers, axis=0, keepdims=True))
    prob_grad = dot_nt(value, grad)
    row_delta = jnp.sum(probs * prob_grad, axis=0, keepdims=True)
    score_grad = (probs * (prob_grad - row_delta)).astype(jnp.bfloat16)
    results = (
        dot_tn(score_grad, key) * scale,
        dot_nn(score_grad, query) * scale,
        dot_nn(probs.astype(jnp.bfloat16), grad),
    )
    for row, result in enumerate(results):
        result = result.astype(jnp.bfloat16)
        for place, out in enumerate(outs):
            out[row] = result[place * bins : (place + 1) * bins]


def heads_back(blocks):
    groups = len(blocks)
    bins, width = blocks[0].shape[1:]
    rows = bins * groups
    heads = width // HD
    return pl.pallas_call(
        heads_kernel,
        grid=(heads,),
        out_shape=[jax.ShapeDtypeStruct((3, bins, width), jnp.bfloat16)] * groups,
        in_specs=[pl.BlockSpec((4, bins, HD), lambda h: (0, 0, h))] * groups,
        out_specs=[pl.BlockSpec((3, bins, HD), lambda h: (0, 0, h))] * groups,
        compiler_params=pltpu.CompilerParams(vmem_limit_bytes=VMEM_BYTES),
        cost_estimate=cost(HEADS_COST),
        name="heads_back",
    )(*blocks)


def exchange(blocks):
    groups = len(blocks)
    return [blocks[0]] + [
        lax.ppermute(blocks[place], "ctx", [(i, i ^ place) for i in range(groups)])
        for place in range(1, groups)
    ]


def make_block(tokens, grads, routes, gates):
    rest = gates.T
    pieces = [(routes.T + 1).astype(jnp.float32)]
    for _ in range(3):
        piece = lax.reduce_precision(rest, 8, 7)
        rest = rest - piece
        pieces.append(piece)
    notes = jnp.concatenate(pieces, axis=0).astype(jnp.bfloat16)
    notes = jnp.pad(notes, ((0, NOTES - notes.shape[0]), (0, tokens.shape[1] - notes.shape[1])))
    return jnp.concatenate([tokens, notes, grads], axis=0)


def pick_slots(notes, base, top, experts, pick_ref):
    bins = notes[0].shape[1]
    slots = len(notes) * CAP
    earlier = lax.broadcasted_iota(jnp.int32, (bins, bins), 0)
    later = lax.broadcasted_iota(jnp.int32, (bins, bins), 1)
    before = (earlier < later).astype(jnp.bfloat16)
    slot = lax.broadcasted_iota(jnp.int32, (slots, bins), 0).astype(jnp.float32)
    gates = [jnp.zeros((slots, 1), jnp.float32)] * experts
    for source, note in enumerate(notes):
        note = note.astype(jnp.float32)
        named = note[:top] - base
        weights = note[top : 2 * top] + note[2 * top : 3 * top] + note[3 * top : 4 * top]
        hits = [(named == float(local + 1)).astype(jnp.float32) for local in range(experts)]
        chosen = [jnp.sum(hit, axis=0, keepdims=True) for hit in hits]
        stacked = jnp.concatenate(chosen, axis=0)
        position = dot_nn(stacked.astype(jnp.bfloat16), before)
        for local in range(experts):
            place = jnp.where(
                chosen[local] > 0.0, position[local : local + 1] + float(source * CAP), -1.0
            )
            pick = (slot == place).astype(jnp.float32)
            gate = jnp.sum(hits[local] * weights, axis=0, keepdims=True)
            gates[local] = gates[local] + jnp.sum(pick * gate, axis=1, keepdims=True)
            pick_ref[
                local * slots : (local + 1) * slots, source * bins : (source + 1) * bins
            ] = pick.astype(jnp.bfloat16)
    return jnp.concatenate(gates, axis=0)


def expert_kernel(layout, ahead, later, pieces, top, base_ref, *refs):
    refs = list(refs)

    def take(count):
        taken = refs[:count]
        del refs[:count]
        return taken

    sources = len(layout)
    blocks = [take(length) for length in layout]
    ahead_refs = take(ahead)
    slope_refs = take(1 if later else 0)
    up_hbm, down_hbm = take(2)
    (keep_ref,) = take(1)
    give_refs = take(pieces)
    ahead_slopes = take(1 if ahead else 0)
    pick_ref, token_rows, gated_rows, back_rows, up_ref, down_ref, sems = take(7)
    ahead_picks = take(1 if ahead else 0)
    bins = keep_ref.shape[0]
    slots = sources * CAP
    experts = pick_ref.shape[0] // slots
    wide = slots + ahead * CAP

    def copies(expert):
        place = expert % 2
        return [
            pltpu.make_async_copy(
                hbm.at[expert, pl.ds(part * (hbm.shape[1] // PARTS), hbm.shape[1] // PARTS)],
                vmem.at[place, pl.ds(part * (hbm.shape[1] // PARTS), hbm.shape[1] // PARTS)],
                sems.at[place, PARTS * which + part],
            )
            for which, (hbm, vmem) in enumerate(((up_hbm, up_ref), (down_hbm, down_ref)))
            for part in range(PARTS)
        ]

    for copy in copies(0):
        copy.start()

    values = [
        jnp.concatenate([piece[...] for piece in block], axis=0) if len(block) > 1 else block[0]
        for block in blocks
    ]
    base = base_ref[0].astype(jnp.float32)
    notes = [value[bins : bins + NOTES, :bins] for value in values]
    gate_column = pick_slots(notes, base, top, experts, pick_ref)
    grads = jnp.concatenate([value[bins + NOTES :] for value in values], axis=0)
    gated_rows[...] = (gate_column * dot_nn(pick_ref[...], grads)).astype(jnp.bfloat16)
    if not later:
        tokens = jnp.concatenate([value[:bins] for value in values], axis=0)
        picked = dot_nn(pick_ref[...], tokens).astype(jnp.bfloat16)
        for local in range(experts):
            token_rows[local * wide : local * wide + slots] = picked[
                local * slots : (local + 1) * slots
            ]
    if ahead:
        notes = [ref[bins : bins + NOTES, :bins] for ref in ahead_refs]
        pick_slots(notes, base, top, experts, ahead_picks[0])
        tokens = jnp.concatenate([ref[:bins] for ref in ahead_refs], axis=0)
        picked = dot_nn(ahead_picks[0][...], tokens).astype(jnp.bfloat16)
        more = ahead * CAP
        for local in range(experts):
            token_rows[local * wide + slots : (local + 1) * wide] = picked[
                local * more : (local + 1) * more
            ]

    @pl.loop(0, experts)
    def _(expert):
        @pl.when(expert + 1 < experts)
        def _():
            for copy in copies(expert + 1):
                copy.start()

        for copy in copies(expert):
            copy.wait()
        place = expert % 2
        rows = pl.ds(pl.multiple_of(expert * slots, 16), slots)
        if later:
            slopes = slope_refs[0][rows, :]
        else:
            wide_rows = pl.ds(pl.multiple_of(expert * wide, 16), wide)
            slopes = silu_slope(dot_nn(token_rows[wide_rows, :], up_ref[place]))
        if ahead:
            more = ahead * CAP
            ahead_slopes[0][pl.ds(pl.multiple_of(expert * more, 16), more), :] = slopes[slots:]
            slopes = slopes[:slots]
        back_grad = dot_nt(gated_rows[rows, :], down_ref[place])
        hidden_grad = (back_grad * slopes).astype(jnp.bfloat16)
        back_rows[rows, :] = dot_nt(hidden_grad, up_ref[place]).astype(jnp.bfloat16)

    sums = dot_tn(pick_ref[...], back_rows[...])
    keep_ref[...] = sums[:bins].astype(jnp.bfloat16)
    rows = bins // pieces
    for piece, give_ref in enumerate(give_refs):
        give_ref[...] = sums[bins + piece * rows : bins + (piece + 1) * rows].astype(jnp.bfloat16)


def expert_back(base, blocks, up_weight, down_weight, bins, top, units, pieces, ahead, slopes):
    layout = [len(block) for block in blocks]
    later = slopes is not None
    experts, width, hidden = up_weight.shape
    slots = len(blocks) * CAP
    wide = slots + len(ahead) * CAP
    operands = [piece for block in blocks for piece in block] + list(ahead)
    operands += [slopes] if later else []
    more = [jax.ShapeDtypeStruct((experts * len(ahead) * CAP, hidden), jnp.float32)]
    out_shape = (
        [jax.ShapeDtypeStruct((bins, width), jnp.bfloat16)]
        + [jax.ShapeDtypeStruct((bins // pieces, width), jnp.bfloat16)] * pieces
        + (more if ahead else [])
    )
    return pl.pallas_call(
        functools.partial(expert_kernel, layout, len(ahead), later, pieces, top),
        out_shape=out_shape,
        in_specs=[pl.BlockSpec(memory_space=pltpu.SMEM)]
        + [pl.BlockSpec(memory_space=pltpu.VMEM)] * len(operands)
        + [pl.BlockSpec(memory_space=pltpu.HBM)] * 2,
        out_specs=[pl.BlockSpec(memory_space=pltpu.VMEM)] * len(out_shape),
        scratch_shapes=[
            pltpu.VMEM((experts * slots, len(blocks) * bins), jnp.bfloat16),
            pltpu.VMEM((16 if later else experts * wide, width), jnp.bfloat16),
            pltpu.VMEM((experts * slots, width), jnp.bfloat16),
            pltpu.VMEM((experts * slots, width), jnp.bfloat16),
            pltpu.VMEM((2, width, hidden), jnp.bfloat16),
            pltpu.VMEM((2, hidden, width), jnp.bfloat16),
            pltpu.SemaphoreType.DMA((2, 2 * PARTS)),
        ]
        + [pltpu.VMEM((experts * len(ahead) * CAP, len(ahead) * bins), jnp.bfloat16)]
        * (1 if ahead else 0),
        compiler_params=pltpu.CompilerParams(vmem_limit_bytes=VMEM_EXPERTS),
        cost_estimate=cost(units),
        name="expert_back",
    )(base, *operands, up_weight, down_weight)


def per_device(
    queries, key_rows, value_rows, out_grad, moe_input, routes, route_gates, up_weight, down_weight
):
    members = lax.axis_size("exp")
    me = lax.axis_index("exp")
    groups = lax.axis_size("ctx")
    chips = members // 2
    half = chips // 2
    _, bins, top = routes.shape
    base = (me * up_weight.shape[0]).astype(jnp.int32).reshape(1)

    def swap(block):
        return lax.ppermute(block, "exp", [(i, i ^ 1) for i in range(members)])

    def hop(block, step):
        return lax.ppermute(
            block, "exp", [(i, (i + 2 * step) % members) for i in range(members)]
        )

    def pair(*pieces):
        return [list(pieces), [swap(piece) for piece in pieces]]

    def work(blocks, units, pieces=1, ahead=(), slopes=None):
        kept, *rest = expert_back(
            base, blocks, up_weight, down_weight, bins, top, units, pieces, ahead, slopes
        )
        return kept, rest[:pieces], rest[pieces:]

    def add_up(*members):
        return functools.reduce(jnp.add, [member.astype(jnp.float32) for member in members])

    def joined(pieces):
        return pieces[0] if len(pieces) == 1 else jnp.concatenate(pieces, axis=0)

    barrier = lax.optimization_barrier
    own = make_block(moe_input[0], out_grad[0], routes[0], route_gates[0])
    left, right_rows = hop(own, -1), hop(own[: bins + NOTES], 1)
    own_pair = pair(own)
    table = [[group ^ place for place in range(groups)] for group in range(groups)]
    group_ids = jnp.asarray(table, jnp.int32)[lax.axis_index("ctx")]
    rows = (queries[0], key_rows[0], value_rows[0], out_grad[0])
    packed = pack_groups(group_ids, rows, groups)
    own_pair, packed = barrier((own_pair, packed))
    heads = exchange(packed)
    kept, give, _ = work(own_pair, OWN_COST)
    heads, kept, give, left = barrier((heads, kept, give, left))
    total = add_up(kept, joined([swap(piece) for piece in give]))
    left_pair, right_grads = pair(left), out_grad[0]
    results = heads_back(heads)
    left_pair, results, right_rows = barrier((left_pair, results, right_rows))
    results = exchange(results)
    right_partner = swap(right_rows)
    left_sums, slopes = [], None
    for d in range(1, half):
        left = hop(left, -1)
        ahead = () if d > 1 else (right_rows, right_partner)
        kept, give, more = work(left_pair, LEFT_COST, ahead=ahead)
        slopes = more[0] if d == 1 else slopes
        left, results, kept, give = barrier((left, results, kept, give))
        left_sums.append(add_up(kept, joined([swap(piece) for piece in give])))
        left_pair = pair(left)
    carried = left_sums[-1].astype(jnp.bfloat16)
    for sums in reversed(left_sums[:-1]):
        carried = add_up(sums, hop(carried, 1)).astype(jnp.bfloat16)
    left_halves = [hop(carried[: bins // 2], 1), hop(carried[bins // 2 :], 1)]
    rights = [(right_rows, hop(right_grads, 1))]
    for d in range(2, half):
        rights.append(tuple(hop(member, 1) for member in rights[-1]))
    kept, give, _ = work(left_pair, FAR_COST)
    left_halves[0], rights, kept, give = barrier((left_halves[0], rights, kept, give))
    carried = add_up(kept, joined([swap(piece) for piece in give]))
    for d in range(half - 1, 0, -1):
        carried = hop(carried.astype(jnp.bfloat16), -1)
        right_pair = pair(*rights[d - 1])
        if d == 1:
            right_pair[1][0] = right_partner
        kept, give, _ = work(right_pair, RIGHT_COST, 2, slopes=slopes if d == 1 else None)
        given = [swap(piece) for piece in give]
        kept, given, carried, left_halves = barrier((kept, given, carried, left_halves))
        carried = add_up(kept, joined(given), carried)
    total = add_up(total, joined(left_halves))
    carried = hop(carried.astype(jnp.bfloat16), -1)
    outs = unpack_groups(group_ids, results)
    total = add_up(total, carried).astype(jnp.bfloat16)
    return tuple(out[None] for out in outs) + (total[None],)


def solution(mesh):
    rows = P("exp", "ctx", None)
    experts = P("exp", None, None)
    return jax.shard_map(
        per_device,
        mesh=mesh,
        in_specs=(rows,) * 7 + (experts,) * 2,
        out_specs=(rows,) * 4,
        check_vma=False,
    )
```

```python
import functools

import jax
import jax.numpy as jnp
from jax import lax
from jax.experimental import pallas as pl
from jax.experimental.pallas import tpu as pltpu
from jax.sharding import PartitionSpec as P

HD = 128
CAP = 24
NOTES = 16
PARTS = 4
VMEM_BYTES = 36 * 1024 * 1024
VMEM_PACK = 58 * 1024 * 1024
VMEM_EXPERTS = 45 * 1024 * 1024
def cost(units):
    return pl.CostEstimate(
        flops=units * 10**9, bytes_accessed=units * 10**6, transcendentals=0
    )


SMALL = cost(0)
OWN_COST, HEADS_COST, LEFT_COST, FAR_COST, RIGHT_COST = 30, 30, 0, 0, 30
NT = (((1,), (1,)), ((), ()))
TN = (((0,), (0,)), ((), ()))


def dot_nt(left, right):
    return lax.dot_general(left, right, NT, preferred_element_type=jnp.float32)


def dot_tn(left, right):
    return lax.dot_general(left, right, TN, preferred_element_type=jnp.float32)


def dot_nn(left, right):
    return jnp.dot(left, right, preferred_element_type=jnp.float32)


def silu_slope(preact):
    sigmoid = jax.nn.sigmoid(preact)
    return sigmoid * (1.0 + preact * (1.0 - sigmoid))


def pack_kernel(mine_ref, *refs):
    members, blocks = refs[:4], refs[4:]
    width = blocks[0].shape[2]
    for place, block in enumerate(blocks):
        first = pl.multiple_of((mine_ref[0] ^ place) * width, 128)
        for row, member in enumerate(members):
            block[row] = member[:, pl.ds(first, width)]


def pack_groups(mine, members, groups):
    bins, width = members[0].shape
    block = jax.ShapeDtypeStruct((4, bins, width // groups), jnp.bfloat16)
    return pl.pallas_call(
        pack_kernel,
        out_shape=[block] * groups,
        in_specs=[pl.BlockSpec(memory_space=pltpu.SMEM)]
        + [pl.BlockSpec(memory_space=pltpu.VMEM)] * 4,
        out_specs=[pl.BlockSpec(memory_space=pltpu.VMEM)] * groups,
        compiler_params=pltpu.CompilerParams(vmem_limit_bytes=VMEM_PACK),
        cost_estimate=SMALL,
        name="pack_groups",
    )(mine, *members)


def unpack_kernel(mine_ref, *refs):
    blocks, outs = refs[:-3], refs[-3:]
    width = blocks[0].shape[2]
    for place, block in enumerate(blocks):
        first = pl.multiple_of((mine_ref[0] ^ place) * width, 128)
        for row, out in enumerate(outs):
            out[:, pl.ds(first, width)] = block[row]


def unpack_groups(mine, blocks):
    groups = len(blocks)
    bins, width = blocks[0].shape[1], blocks[0].shape[2] * groups
    out = jax.ShapeDtypeStruct((bins, width), jnp.bfloat16)
    return pl.pallas_call(
        unpack_kernel,
        out_shape=[out] * 3,
        in_specs=[pl.BlockSpec(memory_space=pltpu.SMEM)]
        + [pl.BlockSpec(memory_space=pltpu.VMEM)] * groups,
        out_specs=[pl.BlockSpec(memory_space=pltpu.VMEM)] * 3,
        compiler_params=pltpu.CompilerParams(vmem_limit_bytes=VMEM_BYTES),
        cost_estimate=SMALL,
        name="unpack_groups",
    )(mine, *blocks)


def heads_kernel(*refs):
    count = len(refs) // 2
    blocks, outs = refs[:count], refs[count:]
    bins = blocks[0].shape[1]
    scale = HD ** (-0.5)
    query, key, value, grad = (
        jnp.concatenate([block[row] for block in blocks], axis=0) for row in range(4)
    )
    scores = dot_nt(key, query) * scale
    powers = jnp.exp(scores - jnp.max(scores, axis=0, keepdims=True))
    probs = powers * (1.0 / jnp.sum(powers, axis=0, keepdims=True))
    prob_grad = dot_nt(value, grad)
    row_delta = jnp.sum(probs * prob_grad, axis=0, keepdims=True)
    score_grad = (probs * (prob_grad - row_delta)).astype(jnp.bfloat16)
    results = (
        dot_tn(score_grad, key) * scale,
        dot_nn(score_grad, query) * scale,
        dot_nn(probs.astype(jnp.bfloat16), grad),
    )
    for row, result in enumerate(results):
        result = result.astype(jnp.bfloat16)
        for place, out in enumerate(outs):
            out[row] = result[place * bins : (place + 1) * bins]


def heads_back(blocks):
    groups = len(blocks)
    bins, width = blocks[0].shape[1:]
    rows = bins * groups
    heads = width // HD
    return pl.pallas_call(
        heads_kernel,
        grid=(heads,),
        out_shape=[jax.ShapeDtypeStruct((3, bins, width), jnp.bfloat16)] * groups,
        in_specs=[pl.BlockSpec((4, bins, HD), lambda h: (0, 0, h))] * groups,
        out_specs=[pl.BlockSpec((3, bins, HD), lambda h: (0, 0, h))] * groups,
        compiler_params=pltpu.CompilerParams(vmem_limit_bytes=VMEM_BYTES),
        cost_estimate=cost(HEADS_COST),
        name="heads_back",
    )(*blocks)


def exchange(blocks):
    groups = len(blocks)
    return [blocks[0]] + [
        lax.ppermute(blocks[place], "ctx", [(i, i ^ place) for i in range(groups)])
        for place in range(1, groups)
    ]


def make_block(tokens, grads, routes, gates):
    rest = gates.T
    pieces = [(routes.T + 1).astype(jnp.float32)]
    for _ in range(3):
        piece = lax.reduce_precision(rest, 8, 7)
        rest = rest - piece
        pieces.append(piece)
    notes = jnp.concatenate(pieces, axis=0).astype(jnp.bfloat16)
    notes = jnp.pad(notes, ((0, NOTES - notes.shape[0]), (0, tokens.shape[1] - notes.shape[1])))
    return jnp.concatenate([tokens, notes, grads], axis=0)


def pick_slots(notes, base, top, experts, pick_ref):
    bins = notes[0].shape[1]
    slots = len(notes) * CAP
    earlier = lax.broadcasted_iota(jnp.int32, (bins, bins), 0)
    later = lax.broadcasted_iota(jnp.int32, (bins, bins), 1)
    before = (earlier < later).astype(jnp.bfloat16)
    slot = lax.broadcasted_iota(jnp.int32, (slots, bins), 0).astype(jnp.float32)
    gates = [jnp.zeros((slots, 1), jnp.float32)] * experts
    for source, note in enumerate(notes):
        note = note.astype(jnp.float32)
        named = note[:top] - base
        weights = note[top : 2 * top] + note[2 * top : 3 * top] + note[3 * top : 4 * top]
        hits = [(named == float(local + 1)).astype(jnp.float32) for local in range(experts)]
        chosen = [jnp.sum(hit, axis=0, keepdims=True) for hit in hits]
        stacked = jnp.concatenate(chosen, axis=0)
        position = dot_nn(stacked.astype(jnp.bfloat16), before)
        for local in range(experts):
            place = jnp.where(
                chosen[local] > 0.0, position[local : local + 1] + float(source * CAP), -1.0
            )
            pick = (slot == place).astype(jnp.float32)
            gate = jnp.sum(hits[local] * weights, axis=0, keepdims=True)
            gates[local] = gates[local] + jnp.sum(pick * gate, axis=1, keepdims=True)
            pick_ref[
                local * slots : (local + 1) * slots, source * bins : (source + 1) * bins
            ] = pick.astype(jnp.bfloat16)
    return jnp.concatenate(gates, axis=0)


def expert_kernel(layout, ahead, later, pieces, top, base_ref, *refs):
    refs = list(refs)

    def take(count):
        taken = refs[:count]
        del refs[:count]
        return taken

    sources = len(layout)
    blocks = [take(length) for length in layout]
    ahead_refs = take(ahead)
    slope_refs = take(1 if later else 0)
    up_hbm, down_hbm = take(2)
    (keep_ref,) = take(1)
    give_refs = take(pieces)
    ahead_slopes = take(1 if ahead else 0)
    pick_ref, token_rows, gated_rows, back_rows, up_ref, down_ref, sems = take(7)
    ahead_picks = take(1 if ahead else 0)
    bins = keep_ref.shape[0]
    slots = sources * CAP
    experts = pick_ref.shape[0] // slots
    wide = slots + ahead * CAP

    def copies(expert):
        place = expert % 2
        return [
            pltpu.make_async_copy(
                hbm.at[expert, pl.ds(part * (hbm.shape[1] // PARTS), hbm.shape[1] // PARTS)],
                vmem.at[place, pl.ds(part * (hbm.shape[1] // PARTS), hbm.shape[1] // PARTS)],
                sems.at[place, PARTS * which + part],
            )
            for which, (hbm, vmem) in enumerate(((up_hbm, up_ref), (down_hbm, down_ref)))
            for part in range(PARTS)
        ]

    for copy in copies(0):
        copy.start()

    values = [
        jnp.concatenate([piece[...] for piece in block], axis=0) if len(block) > 1 else block[0]
        for block in blocks
    ]
    base = base_ref[0].astype(jnp.float32)
    notes = [value[bins : bins + NOTES, :bins] for value in values]
    gate_column = pick_slots(notes, base, top, experts, pick_ref)
    grads = jnp.concatenate([value[bins + NOTES :] for value in values], axis=0)
    gated_rows[...] = (gate_column * dot_nn(pick_ref[...], grads)).astype(jnp.bfloat16)
    if not later:
        tokens = jnp.concatenate([value[:bins] for value in values], axis=0)
        picked = dot_nn(pick_ref[...], tokens).astype(jnp.bfloat16)
        for local in range(experts):
            token_rows[local * wide : local * wide + slots] = picked[
                local * slots : (local + 1) * slots
            ]
    if ahead:
        notes = [ref[bins : bins + NOTES, :bins] for ref in ahead_refs]
        pick_slots(notes, base, top, experts, ahead_picks[0])
        tokens = jnp.concatenate([ref[:bins] for ref in ahead_refs], axis=0)
        picked = dot_nn(ahead_picks[0][...], tokens).astype(jnp.bfloat16)
        more = ahead * CAP
        for local in range(experts):
            token_rows[local * wide + slots : (local + 1) * wide] = picked[
                local * more : (local + 1) * more
            ]

    @pl.loop(0, experts)
    def _(expert):
        @pl.when(expert + 1 < experts)
        def _():
            for copy in copies(expert + 1):
                copy.start()

        for copy in copies(expert):
            copy.wait()
        place = expert % 2
        rows = pl.ds(pl.multiple_of(expert * slots, 16), slots)
        if later:
            slopes = slope_refs[0][rows, :]
        else:
            wide_rows = pl.ds(pl.multiple_of(expert * wide, 16), wide)
            slopes = silu_slope(dot_nn(token_rows[wide_rows, :], up_ref[place]))
        if ahead:
            more = ahead * CAP
            ahead_slopes[0][pl.ds(pl.multiple_of(expert * more, 16), more), :] = slopes[slots:]
            slopes = slopes[:slots]
        back_grad = dot_nt(gated_rows[rows, :], down_ref[place])
        hidden_grad = (back_grad * slopes).astype(jnp.bfloat16)
        back_rows[rows, :] = dot_nt(hidden_grad, up_ref[place]).astype(jnp.bfloat16)

    sums = dot_tn(pick_ref[...], back_rows[...])
    keep_ref[...] = sums[:bins].astype(jnp.bfloat16)
    rows = bins // pieces
    for piece, give_ref in enumerate(give_refs):
        give_ref[...] = sums[bins + piece * rows : bins + (piece + 1) * rows].astype(jnp.bfloat16)


def expert_back(base, blocks, up_weight, down_weight, bins, top, units, pieces, ahead, slopes):
    layout = [len(block) for block in blocks]
    later = slopes is not None
    experts, width, hidden = up_weight.shape
    slots = len(blocks) * CAP
    wide = slots + len(ahead) * CAP
    operands = [piece for block in blocks for piece in block] + list(ahead)
    operands += [slopes] if later else []
    more = [jax.ShapeDtypeStruct((experts * len(ahead) * CAP, hidden), jnp.float32)]
    out_shape = (
        [jax.ShapeDtypeStruct((bins, width), jnp.bfloat16)]
        + [jax.ShapeDtypeStruct((bins // pieces, width), jnp.bfloat16)] * pieces
        + (more if ahead else [])
    )
    return pl.pallas_call(
        functools.partial(expert_kernel, layout, len(ahead), later, pieces, top),
        out_shape=out_shape,
        in_specs=[pl.BlockSpec(memory_space=pltpu.SMEM)]
        + [pl.BlockSpec(memory_space=pltpu.VMEM)] * len(operands)
        + [pl.BlockSpec(memory_space=pltpu.HBM)] * 2,
        out_specs=[pl.BlockSpec(memory_space=pltpu.VMEM)] * len(out_shape),
        scratch_shapes=[
            pltpu.VMEM((experts * slots, len(blocks) * bins), jnp.bfloat16),
            pltpu.VMEM((16 if later else experts * wide, width), jnp.bfloat16),
            pltpu.VMEM((experts * slots, width), jnp.bfloat16),
            pltpu.VMEM((experts * slots, width), jnp.bfloat16),
            pltpu.VMEM((2, width, hidden), jnp.bfloat16),
            pltpu.VMEM((2, hidden, width), jnp.bfloat16),
            pltpu.SemaphoreType.DMA((2, 2 * PARTS)),
        ]
        + [pltpu.VMEM((experts * len(ahead) * CAP, len(ahead) * bins), jnp.bfloat16)]
        * (1 if ahead else 0),
        compiler_params=pltpu.CompilerParams(vmem_limit_bytes=VMEM_EXPERTS),
        cost_estimate=cost(units),
        name="expert_back",
    )(base, *operands, up_weight, down_weight)


def per_device(
    queries, key_rows, value_rows, out_grad, moe_input, routes, route_gates, up_weight, down_weight
):
    members = lax.axis_size("exp")
    me = lax.axis_index("exp")
    groups = lax.axis_size("ctx")
    chips = members // 2
    half = chips // 2
    _, bins, top = routes.shape
    base = (me * up_weight.shape[0]).astype(jnp.int32).reshape(1)

    def swap(block):
        return lax.ppermute(block, "exp", [(i, i ^ 1) for i in range(members)])

    def hop(block, step):
        return lax.ppermute(
            block, "exp", [(i, (i + 2 * step) % members) for i in range(members)]
        )

    def pair(*pieces):
        return [list(pieces), [swap(piece) for piece in pieces]]

    def work(blocks, units, pieces=1, ahead=(), slopes=None):
        kept, *rest = expert_back(
            base, blocks, up_weight, down_weight, bins, top, units, pieces, ahead, slopes
        )
        return kept, rest[:pieces], rest[pieces:]

    def add_up(*members):
        return functools.reduce(jnp.add, [member.astype(jnp.float32) for member in members])

    def joined(pieces):
        return pieces[0] if len(pieces) == 1 else jnp.concatenate(pieces, axis=0)

    barrier = lax.optimization_barrier
    own = make_block(moe_input[0], out_grad[0], routes[0], route_gates[0])
    left, right_rows = hop(own, -1), hop(own[: bins + NOTES], 1)
    own_pair = pair(own)
    mine = lax.axis_index("ctx").astype(jnp.int32).reshape(1)
    rows = (queries[0], key_rows[0], value_rows[0], out_grad[0])
    packed = pack_groups(mine, rows, groups)
    own_pair, packed = barrier((own_pair, packed))
    heads = exchange(packed)
    kept, give, _ = work(own_pair, OWN_COST)
    heads, kept, give, left = barrier((heads, kept, give, left))
    total = add_up(kept, joined([swap(piece) for piece in give]))
    left_pair, right_grads = pair(left), out_grad[0]
    results = heads_back(heads)
    left_pair, results, right_rows = barrier((left_pair, results, right_rows))
    results = exchange(results)
    right_partner = swap(right_rows)
    left_sums, slopes = [], None
    for d in range(1, half):
        left = hop(left, -1)
        ahead = () if d > 1 else (right_rows, right_partner)
        kept, give, more = work(left_pair, LEFT_COST, ahead=ahead)
        slopes = more[0] if d == 1 else slopes
        left, results, kept, give = barrier((left, results, kept, give))
        left_sums.append(add_up(kept, joined([swap(piece) for piece in give])))
        left_pair = pair(left)
    carried = left_sums[-1].astype(jnp.bfloat16)
    for sums in reversed(left_sums[:-1]):
        carried = add_up(sums, hop(carried, 1)).astype(jnp.bfloat16)
    left_halves = [hop(carried[: bins // 2], 1), hop(carried[bins // 2 :], 1)]
    rights = [(right_rows, hop(right_grads, 1))]
    for d in range(2, half):
        rights.append(tuple(hop(member, 1) for member in rights[-1]))
    kept, give, _ = work(left_pair, FAR_COST)
    left_halves[0], rights, kept, give = barrier((left_halves[0], rights, kept, give))
    carried = add_up(kept, joined([swap(piece) for piece in give]))
    for d in range(half - 1, 0, -1):
        carried = hop(carried.astype(jnp.bfloat16), -1)
        right_pair = pair(*rights[d - 1])
        if d == 1:
            right_pair[1][0] = right_partner
        kept, give, _ = work(right_pair, RIGHT_COST, 2, slopes=slopes if d == 1 else None)
        given = [swap(piece) for piece in give]
        kept, given, carried, left_halves = barrier((kept, given, carried, left_halves))
        carried = add_up(kept, joined(given), carried)
    total = add_up(total, joined(left_halves))
    carried = hop(carried.astype(jnp.bfloat16), -1)
    outs = unpack_groups(mine, results)
    total = add_up(total, carried).astype(jnp.bfloat16)
    return tuple(out[None] for out in outs) + (total[None],)


def solution(mesh):
    rows = P("exp", "ctx", None)
    experts = P("exp", None, None)
    return jax.shard_map(
        per_device,
        mesh=mesh,
        in_specs=(rows,) * 7 + (experts,) * 2,
        out_specs=(rows,) * 4,
        check_vma=False,
    )
```

```python
import functools

import jax
import jax.numpy as jnp
from jax import lax
from jax.experimental import pallas as pl
from jax.experimental.pallas import tpu as pltpu
from jax.sharding import PartitionSpec as P

HD = 128
CAP = 24
NOTES = 16
PARTS = 4
VMEM_BYTES = 36 * 1024 * 1024
VMEM_PACK = 58 * 1024 * 1024
VMEM_EXPERTS = 45 * 1024 * 1024
def cost(units):
    return pl.CostEstimate(
        flops=units * 10**9, bytes_accessed=units * 10**6, transcendentals=0
    )


SMALL = cost(0)
OWN_COST, HEADS_COST, LEFT_COST, FAR_COST, RIGHT_COST = 30, 30, 0, 0, 30
NT = (((1,), (1,)), ((), ()))
TN = (((0,), (0,)), ((), ()))


def dot_nt(left, right):
    return lax.dot_general(left, right, NT, preferred_element_type=jnp.float32)


def dot_tn(left, right):
    return lax.dot_general(left, right, TN, preferred_element_type=jnp.float32)


def dot_nn(left, right):
    return jnp.dot(left, right, preferred_element_type=jnp.float32)


def silu_slope(preact):
    sigmoid = jax.nn.sigmoid(preact)
    return sigmoid * (1.0 + preact * (1.0 - sigmoid))


def pack_kernel(mine_ref, *refs):
    members, blocks = refs[:4], refs[4:]
    width = blocks[0].shape[2]
    for place, block in enumerate(blocks):
        first = pl.multiple_of((mine_ref[0] ^ place) * width, 128)
        for row, member in enumerate(members):
            block[row] = member[:, pl.ds(first, width)]


def pack_groups(mine, members, groups):
    bins, width = members[0].shape
    block = jax.ShapeDtypeStruct((4, bins, width // groups), jnp.bfloat16)
    return pl.pallas_call(
        pack_kernel,
        out_shape=[block] * groups,
        in_specs=[pl.BlockSpec(memory_space=pltpu.SMEM)]
        + [pl.BlockSpec(memory_space=pltpu.VMEM)] * 4,
        out_specs=[pl.BlockSpec(memory_space=pltpu.VMEM)] * groups,
        compiler_params=pltpu.CompilerParams(vmem_limit_bytes=VMEM_PACK),
        cost_estimate=SMALL,
        name="pack_groups",
    )(mine, *members)


def unpack_kernel(mine_ref, *refs):
    blocks, outs = refs[:-3], refs[-3:]
    width = blocks[0].shape[2]
    for place, block in enumerate(blocks):
        first = pl.multiple_of((mine_ref[0] ^ place) * width, 128)
        for row, out in enumerate(outs):
            out[:, pl.ds(first, width)] = block[row]


def unpack_groups(mine, blocks):
    groups = len(blocks)
    bins, width = blocks[0].shape[1], blocks[0].shape[2] * groups
    out = jax.ShapeDtypeStruct((bins, width), jnp.bfloat16)
    return pl.pallas_call(
        unpack_kernel,
        out_shape=[out] * 3,
        in_specs=[pl.BlockSpec(memory_space=pltpu.SMEM)]
        + [pl.BlockSpec(memory_space=pltpu.VMEM)] * groups,
        out_specs=[pl.BlockSpec(memory_space=pltpu.VMEM)] * 3,
        compiler_params=pltpu.CompilerParams(vmem_limit_bytes=VMEM_BYTES),
        cost_estimate=SMALL,
        name="unpack_groups",
    )(mine, *blocks)


def heads_kernel(*refs):
    count = len(refs) // 2
    blocks, outs = refs[:count], refs[count:]
    bins = blocks[0].shape[1]
    scale = HD ** (-0.5)
    query, key, value, grad = (
        jnp.concatenate([block[row] for block in blocks], axis=0) for row in range(4)
    )
    scores = dot_nt(key, query) * scale
    powers = jnp.exp(scores - jnp.max(scores, axis=0, keepdims=True))
    probs = powers * (1.0 / jnp.sum(powers, axis=0, keepdims=True))
    prob_grad = dot_nt(value, grad)
    row_delta = jnp.sum(probs * prob_grad, axis=0, keepdims=True)
    score_grad = (probs * (prob_grad - row_delta)).astype(jnp.bfloat16)
    results = (
        dot_tn(score_grad, key) * scale,
        dot_nn(score_grad, query) * scale,
        dot_nn(probs.astype(jnp.bfloat16), grad),
    )
    for row, result in enumerate(results):
        result = result.astype(jnp.bfloat16)
        for place, out in enumerate(outs):
            out[row] = result[place * bins : (place + 1) * bins]


def heads_back(blocks):
    groups = len(blocks)
    bins, width = blocks[0].shape[1:]
    rows = bins * groups
    heads = width // HD
    return pl.pallas_call(
        heads_kernel,
        grid=(heads,),
        out_shape=[jax.ShapeDtypeStruct((3, bins, width), jnp.bfloat16)] * groups,
        in_specs=[pl.BlockSpec((4, bins, HD), lambda h: (0, 0, h))] * groups,
        out_specs=[pl.BlockSpec((3, bins, HD), lambda h: (0, 0, h))] * groups,
        compiler_params=pltpu.CompilerParams(vmem_limit_bytes=VMEM_BYTES),
        cost_estimate=cost(HEADS_COST),
        name="heads_back",
    )(*blocks)


def exchange(blocks):
    groups = len(blocks)
    return [blocks[0]] + [
        lax.ppermute(blocks[place], "ctx", [(i, i ^ place) for i in range(groups)])
        for place in range(1, groups)
    ]


def make_block(tokens, grads, routes, gates):
    rest = gates.T
    pieces = [(routes.T + 1).astype(jnp.float32)]
    for _ in range(3):
        piece = lax.reduce_precision(rest, 8, 7)
        rest = rest - piece
        pieces.append(piece)
    notes = jnp.concatenate(pieces, axis=0).astype(jnp.bfloat16)
    notes = jnp.pad(notes, ((0, NOTES - notes.shape[0]), (0, tokens.shape[1] - notes.shape[1])))
    return jnp.concatenate([tokens, notes, grads], axis=0)


def pick_slots(notes, base, top, experts, pick_ref):
    bins = notes[0].shape[1]
    slots = len(notes) * CAP
    earlier = lax.broadcasted_iota(jnp.int32, (bins, bins), 0)
    later = lax.broadcasted_iota(jnp.int32, (bins, bins), 1)
    before = (earlier < later).astype(jnp.bfloat16)
    slot = lax.broadcasted_iota(jnp.int32, (slots, bins), 0).astype(jnp.float32)
    gates = [jnp.zeros((slots, 1), jnp.float32)] * experts
    for source, note in enumerate(notes):
        note = note.astype(jnp.float32)
        named = note[:top] - base
        weights = note[top : 2 * top] + note[2 * top : 3 * top] + note[3 * top : 4 * top]
        hits = [(named == float(local + 1)).astype(jnp.float32) for local in range(experts)]
        chosen = [jnp.sum(hit, axis=0, keepdims=True) for hit in hits]
        stacked = jnp.concatenate(chosen, axis=0)
        position = dot_nn(stacked.astype(jnp.bfloat16), before)
        for local in range(experts):
            place = jnp.where(
                chosen[local] > 0.0, position[local : local + 1] + float(source * CAP), -1.0
            )
            pick = (slot == place).astype(jnp.float32)
            gate = jnp.sum(hits[local] * weights, axis=0, keepdims=True)
            gates[local] = gates[local] + jnp.sum(pick * gate, axis=1, keepdims=True)
            pick_ref[
                local * slots : (local + 1) * slots, source * bins : (source + 1) * bins
            ] = pick.astype(jnp.bfloat16)
    return jnp.concatenate(gates, axis=0)


def expert_kernel(layout, ahead, later, pieces, top, base_ref, *refs):
    refs = list(refs)

    def take(count):
        taken = refs[:count]
        del refs[:count]
        return taken

    sources = len(layout)
    blocks = [take(length) for length in layout]
    ahead_refs = take(ahead)
    slope_refs = take(1 if later else 0)
    up_hbm, down_hbm = take(2)
    (keep_ref,) = take(1)
    give_refs = take(pieces)
    ahead_slopes = take(1 if ahead else 0)
    pick_ref, token_rows, gated_rows, back_columns, up_ref, down_ref, sems = take(7)
    ahead_picks = take(1 if ahead else 0)
    bins = keep_ref.shape[0]
    slots = sources * CAP
    experts = pick_ref.shape[0] // slots
    wide = slots + ahead * CAP

    def copies(expert):
        place = expert % 2
        return [
            pltpu.make_async_copy(
                hbm.at[expert, pl.ds(part * (hbm.shape[1] // PARTS), hbm.shape[1] // PARTS)],
                vmem.at[place, pl.ds(part * (hbm.shape[1] // PARTS), hbm.shape[1] // PARTS)],
                sems.at[place, PARTS * which + part],
            )
            for which, (hbm, vmem) in enumerate(((up_hbm, up_ref), (down_hbm, down_ref)))
            for part in range(PARTS)
        ]

    for copy in copies(0):
        copy.start()

    values = [
        jnp.concatenate([piece[...] for piece in block], axis=0) if len(block) > 1 else block[0]
        for block in blocks
    ]
    base = base_ref[0].astype(jnp.float32)
    notes = [value[bins : bins + NOTES, :bins] for value in values]
    gate_column = pick_slots(notes, base, top, experts, pick_ref)
    grads = jnp.concatenate([value[bins + NOTES :] for value in values], axis=0)
    gated_rows[...] = (gate_column * dot_nn(pick_ref[...], grads)).astype(jnp.bfloat16)
    if not later:
        tokens = jnp.concatenate([value[:bins] for value in values], axis=0)
        picked = dot_nn(pick_ref[...], tokens).astype(jnp.bfloat16)
        for local in range(experts):
            token_rows[local * wide : local * wide + slots] = picked[
                local * slots : (local + 1) * slots
            ]
    if ahead:
        notes = [ref[bins : bins + NOTES, :bins] for ref in ahead_refs]
        pick_slots(notes, base, top, experts, ahead_picks[0])
        tokens = jnp.concatenate([ref[:bins] for ref in ahead_refs], axis=0)
        picked = dot_nn(ahead_picks[0][...], tokens).astype(jnp.bfloat16)
        more = ahead * CAP
        for local in range(experts):
            token_rows[local * wide + slots : (local + 1) * wide] = picked[
                local * more : (local + 1) * more
            ]

    @pl.loop(0, experts)
    def _(expert):
        @pl.when(expert + 1 < experts)
        def _():
            for copy in copies(expert + 1):
                copy.start()

        for copy in copies(expert):
            copy.wait()
        place = expert % 2
        rows = pl.ds(pl.multiple_of(expert * slots, 16), slots)
        if later:
            slopes = slope_refs[0][rows, :]
        else:
            wide_rows = pl.ds(pl.multiple_of(expert * wide, 16), wide)
            slopes = silu_slope(dot_nn(token_rows[wide_rows, :], up_ref[place]))
        if ahead:
            more = ahead * CAP
            ahead_slopes[0][pl.ds(pl.multiple_of(expert * more, 16), more), :] = slopes[slots:]
            slopes = slopes[:slots]
        back_grad = dot_nt(down_ref[place], gated_rows[rows, :])
        hidden_grad = (back_grad * slopes.T).astype(jnp.bfloat16)
        back_columns[expert] = dot_nn(up_ref[place], hidden_grad).astype(jnp.bfloat16)

    columns = jnp.concatenate([back_columns[local] for local in range(experts)], axis=1)
    sums = lax.dot_general(
        pick_ref[...], columns, (((0,), (1,)), ((), ())), preferred_element_type=jnp.float32
    )
    keep_ref[...] = sums[:bins].astype(jnp.bfloat16)
    rows = bins // pieces
    for piece, give_ref in enumerate(give_refs):
        give_ref[...] = sums[bins + piece * rows : bins + (piece + 1) * rows].astype(jnp.bfloat16)


def expert_back(base, blocks, up_weight, down_weight, bins, top, units, pieces, ahead, slopes):
    layout = [len(block) for block in blocks]
    later = slopes is not None
    experts, width, hidden = up_weight.shape
    slots = len(blocks) * CAP
    wide = slots + len(ahead) * CAP
    operands = [piece for block in blocks for piece in block] + list(ahead)
    operands += [slopes] if later else []
    more = [jax.ShapeDtypeStruct((experts * len(ahead) * CAP, hidden), jnp.float32)]
    out_shape = (
        [jax.ShapeDtypeStruct((bins, width), jnp.bfloat16)]
        + [jax.ShapeDtypeStruct((bins // pieces, width), jnp.bfloat16)] * pieces
        + (more if ahead else [])
    )
    return pl.pallas_call(
        functools.partial(expert_kernel, layout, len(ahead), later, pieces, top),
        out_shape=out_shape,
        in_specs=[pl.BlockSpec(memory_space=pltpu.SMEM)]
        + [pl.BlockSpec(memory_space=pltpu.VMEM)] * len(operands)
        + [pl.BlockSpec(memory_space=pltpu.HBM)] * 2,
        out_specs=[pl.BlockSpec(memory_space=pltpu.VMEM)] * len(out_shape),
        scratch_shapes=[
            pltpu.VMEM((experts * slots, len(blocks) * bins), jnp.bfloat16),
            pltpu.VMEM((16 if later else experts * wide, width), jnp.bfloat16),
            pltpu.VMEM((experts * slots, width), jnp.bfloat16),
            pltpu.VMEM((experts, width, slots), jnp.bfloat16),
            pltpu.VMEM((2, width, hidden), jnp.bfloat16),
            pltpu.VMEM((2, hidden, width), jnp.bfloat16),
            pltpu.SemaphoreType.DMA((2, 2 * PARTS)),
        ]
        + [pltpu.VMEM((experts * len(ahead) * CAP, len(ahead) * bins), jnp.bfloat16)]
        * (1 if ahead else 0),
        compiler_params=pltpu.CompilerParams(vmem_limit_bytes=VMEM_EXPERTS),
        cost_estimate=cost(units),
        name="expert_back",
    )(base, *operands, up_weight, down_weight)


def per_device(
    queries, key_rows, value_rows, out_grad, moe_input, routes, route_gates, up_weight, down_weight
):
    members = lax.axis_size("exp")
    me = lax.axis_index("exp")
    groups = lax.axis_size("ctx")
    chips = members // 2
    half = chips // 2
    _, bins, top = routes.shape
    base = (me * up_weight.shape[0]).astype(jnp.int32).reshape(1)

    def swap(block):
        return lax.ppermute(block, "exp", [(i, i ^ 1) for i in range(members)])

    def hop(block, step):
        return lax.ppermute(
            block, "exp", [(i, (i + 2 * step) % members) for i in range(members)]
        )

    def pair(*pieces):
        return [list(pieces), [swap(piece) for piece in pieces]]

    def work(blocks, units, pieces=1, ahead=(), slopes=None):
        kept, *rest = expert_back(
            base, blocks, up_weight, down_weight, bins, top, units, pieces, ahead, slopes
        )
        return kept, rest[:pieces], rest[pieces:]

    def add_up(*members):
        return functools.reduce(jnp.add, [member.astype(jnp.float32) for member in members])

    def joined(pieces):
        return pieces[0] if len(pieces) == 1 else jnp.concatenate(pieces, axis=0)

    barrier = lax.optimization_barrier
    own = make_block(moe_input[0], out_grad[0], routes[0], route_gates[0])
    left, right_rows = hop(own, -1), hop(own[: bins + NOTES], 1)
    own_pair = pair(own)
    mine = lax.axis_index("ctx").astype(jnp.int32).reshape(1)
    rows = (queries[0], key_rows[0], value_rows[0], out_grad[0])
    packed = pack_groups(mine, rows, groups)
    own_pair, packed = barrier((own_pair, packed))
    heads = exchange(packed)
    kept, give, _ = work(own_pair, OWN_COST)
    heads, kept, give, left = barrier((heads, kept, give, left))
    total = add_up(kept, joined([swap(piece) for piece in give]))
    left_pair, right_grads = pair(left), out_grad[0]
    results = heads_back(heads)
    left_pair, results, right_rows = barrier((left_pair, results, right_rows))
    results = exchange(results)
    right_partner = swap(right_rows)
    left_sums, slopes = [], None
    for d in range(1, half):
        left = hop(left, -1)
        ahead = () if d > 1 else (right_rows, right_partner)
        kept, give, more = work(left_pair, LEFT_COST, ahead=ahead)
        slopes = more[0] if d == 1 else slopes
        left, results, kept, give = barrier((left, results, kept, give))
        left_sums.append(add_up(kept, joined([swap(piece) for piece in give])))
        left_pair = pair(left)
    carried = left_sums[-1].astype(jnp.bfloat16)
    for sums in reversed(left_sums[:-1]):
        carried = add_up(sums, hop(carried, 1)).astype(jnp.bfloat16)
    left_halves = [hop(carried[: bins // 2], 1), hop(carried[bins // 2 :], 1)]
    rights = [(right_rows, hop(right_grads, 1))]
    for d in range(2, half):
        rights.append(tuple(hop(member, 1) for member in rights[-1]))
    kept, give, _ = work(left_pair, FAR_COST)
    left_halves[0], rights, kept, give = barrier((left_halves[0], rights, kept, give))
    carried = add_up(kept, joined([swap(piece) for piece in give]))
    for d in range(half - 1, 0, -1):
        carried = hop(carried.astype(jnp.bfloat16), -1)
        right_pair = pair(*rights[d - 1])
        if d == 1:
            right_pair[1][0] = right_partner
        kept, give, _ = work(right_pair, RIGHT_COST, 2, slopes=slopes if d == 1 else None)
        given = [swap(piece) for piece in give]
        kept, given, carried, left_halves = barrier((kept, given, carried, left_halves))
        carried = add_up(kept, joined(given), carried)
    total = add_up(total, joined(left_halves))
    carried = hop(carried.astype(jnp.bfloat16), -1)
    outs = unpack_groups(mine, results)
    total = add_up(total, carried).astype(jnp.bfloat16)
    return tuple(out[None] for out in outs) + (total[None],)


def solution(mesh):
    rows = P("exp", "ctx", None)
    experts = P("exp", None, None)
    return jax.shard_map(
        per_device,
        mesh=mesh,
        in_specs=(rows,) * 7 + (experts,) * 2,
        out_specs=(rows,) * 4,
        check_vma=False,
    )
```

```python
import functools

import jax
import jax.numpy as jnp
from jax import lax
from jax.experimental import pallas as pl
from jax.experimental.pallas import tpu as pltpu
from jax.sharding import PartitionSpec as P

HD = 128
CAP = 24
NOTES = 16
PARTS = 4
VMEM_BYTES = 36 * 1024 * 1024
VMEM_PACK = 58 * 1024 * 1024
VMEM_EXPERTS = 18 * 1024 * 1024
def cost(units):
    return pl.CostEstimate(
        flops=units * 10**9, bytes_accessed=units * 10**6, transcendentals=0
    )


SMALL = cost(0)
OWN_COST, HEADS_COST, LEFT_COST, FAR_COST, RIGHT_COST = 30, 30, 0, 0, 30
NT = (((1,), (1,)), ((), ()))
TN = (((0,), (0,)), ((), ()))


def dot_nt(left, right):
    return lax.dot_general(left, right, NT, preferred_element_type=jnp.float32)


def dot_tn(left, right):
    return lax.dot_general(left, right, TN, preferred_element_type=jnp.float32)


def dot_nn(left, right):
    return jnp.dot(left, right, preferred_element_type=jnp.float32)


def silu_slope(preact):
    sigmoid = jax.nn.sigmoid(preact)
    return sigmoid * (1.0 + preact * (1.0 - sigmoid))


def pack_kernel(mine_ref, *refs):
    members, blocks = refs[:4], refs[4:]
    width = blocks[0].shape[2]
    for place, block in enumerate(blocks):
        first = pl.multiple_of((mine_ref[0] ^ place) * width, 128)
        for row, member in enumerate(members):
            block[row] = member[:, pl.ds(first, width)]


def pack_groups(mine, members, groups):
    bins, width = members[0].shape
    block = jax.ShapeDtypeStruct((4, bins, width // groups), jnp.bfloat16)
    return pl.pallas_call(
        pack_kernel,
        out_shape=[block] * groups,
        in_specs=[pl.BlockSpec(memory_space=pltpu.SMEM)]
        + [pl.BlockSpec(memory_space=pltpu.VMEM)] * 4,
        out_specs=[pl.BlockSpec(memory_space=pltpu.VMEM)] * groups,
        compiler_params=pltpu.CompilerParams(vmem_limit_bytes=VMEM_PACK),
        cost_estimate=SMALL,
        name="pack_groups",
    )(mine, *members)


def unpack_kernel(mine_ref, *refs):
    blocks, outs = refs[:-3], refs[-3:]
    width = blocks[0].shape[2]
    for place, block in enumerate(blocks):
        first = pl.multiple_of((mine_ref[0] ^ place) * width, 128)
        for row, out in enumerate(outs):
            out[:, pl.ds(first, width)] = block[row]


def unpack_groups(mine, blocks):
    groups = len(blocks)
    bins, width = blocks[0].shape[1], blocks[0].shape[2] * groups
    out = jax.ShapeDtypeStruct((bins, width), jnp.bfloat16)
    return pl.pallas_call(
        unpack_kernel,
        out_shape=[out] * 3,
        in_specs=[pl.BlockSpec(memory_space=pltpu.SMEM)]
        + [pl.BlockSpec(memory_space=pltpu.VMEM)] * groups,
        out_specs=[pl.BlockSpec(memory_space=pltpu.VMEM)] * 3,
        compiler_params=pltpu.CompilerParams(vmem_limit_bytes=VMEM_BYTES),
        cost_estimate=SMALL,
        name="unpack_groups",
    )(mine, *blocks)


def heads_kernel(*refs):
    count = len(refs) // 2
    blocks, outs = refs[:count], refs[count:]
    bins = blocks[0].shape[1]
    scale = HD ** (-0.5)
    query, key, value, grad = (
        jnp.concatenate([block[row] for block in blocks], axis=0) for row in range(4)
    )
    scores = dot_nt(key, query) * scale
    powers = jnp.exp(scores - jnp.max(scores, axis=0, keepdims=True))
    probs = powers * (1.0 / jnp.sum(powers, axis=0, keepdims=True))
    prob_grad = dot_nt(value, grad)
    row_delta = jnp.sum(probs * prob_grad, axis=0, keepdims=True)
    score_grad = (probs * (prob_grad - row_delta)).astype(jnp.bfloat16)
    results = (
        dot_tn(score_grad, key) * scale,
        dot_nn(score_grad, query) * scale,
        dot_nn(probs.astype(jnp.bfloat16), grad),
    )
    for row, result in enumerate(results):
        result = result.astype(jnp.bfloat16)
        for place, out in enumerate(outs):
            out[row] = result[place * bins : (place + 1) * bins]


def heads_back(blocks):
    groups = len(blocks)
    bins, width = blocks[0].shape[1:]
    rows = bins * groups
    heads = width // HD
    return pl.pallas_call(
        heads_kernel,
        grid=(heads,),
        out_shape=[jax.ShapeDtypeStruct((3, bins, width), jnp.bfloat16)] * groups,
        in_specs=[pl.BlockSpec((4, bins, HD), lambda h: (0, 0, h))] * groups,
        out_specs=[pl.BlockSpec((3, bins, HD), lambda h: (0, 0, h))] * groups,
        compiler_params=pltpu.CompilerParams(vmem_limit_bytes=6 * 1024 * 1024 + 40 * rows * rows),
        cost_estimate=cost(HEADS_COST),
        name="heads_back",
    )(*blocks)


def exchange(blocks):
    groups = len(blocks)
    return [blocks[0]] + [
        lax.ppermute(blocks[place], "ctx", [(i, i ^ place) for i in range(groups)])
        for place in range(1, groups)
    ]


def make_block(tokens, grads, routes, gates):
    rest = gates.T
    pieces = [(routes.T + 1).astype(jnp.float32)]
    for _ in range(3):
        piece = lax.reduce_precision(rest, 8, 7)
        rest = rest - piece
        pieces.append(piece)
    notes = jnp.concatenate(pieces, axis=0).astype(jnp.bfloat16)
    notes = jnp.pad(notes, ((0, NOTES - notes.shape[0]), (0, tokens.shape[1] - notes.shape[1])))
    return jnp.concatenate([tokens, notes, grads], axis=0)


def pick_slots(notes, base, top, experts, pick_ref):
    bins = notes[0].shape[1]
    slots = len(notes) * CAP
    earlier = lax.broadcasted_iota(jnp.int32, (bins, bins), 0)
    later = lax.broadcasted_iota(jnp.int32, (bins, bins), 1)
    before = (earlier < later).astype(jnp.bfloat16)
    slot = lax.broadcasted_iota(jnp.int32, (slots, bins), 0).astype(jnp.float32)
    gates = [jnp.zeros((slots, 1), jnp.float32)] * experts
    for source, note in enumerate(notes):
        note = note.astype(jnp.float32)
        named = note[:top] - base
        weights = note[top : 2 * top] + note[2 * top : 3 * top] + note[3 * top : 4 * top]
        hits = [(named == float(local + 1)).astype(jnp.float32) for local in range(experts)]
        chosen = [jnp.sum(hit, axis=0, keepdims=True) for hit in hits]
        stacked = jnp.concatenate(chosen, axis=0)
        position = dot_nn(stacked.astype(jnp.bfloat16), before)
        for local in range(experts):
            place = jnp.where(
                chosen[local] > 0.0, position[local : local + 1] + float(source * CAP), -1.0
            )
            pick = (slot == place).astype(jnp.float32)
            gate = jnp.sum(hits[local] * weights, axis=0, keepdims=True)
            gates[local] = gates[local] + jnp.sum(pick * gate, axis=1, keepdims=True)
            pick_ref[
                local * slots : (local + 1) * slots, source * bins : (source + 1) * bins
            ] = pick.astype(jnp.bfloat16)
    return jnp.concatenate(gates, axis=0)


def expert_kernel(layout, ahead, later, loads, pieces, top, base_ref, *refs):
    refs = list(refs)

    def take(count):
        taken = refs[:count]
        del refs[:count]
        return taken

    sources = len(layout)
    blocks = [take(length) for length in layout]
    ahead_refs = take(ahead)
    slope_refs = take(1 if later else 0)
    weights = take(2)
    (keep_ref,) = take(1)
    give_refs = take(pieces)
    ahead_slopes = take(1 if ahead else 0)
    up_ref, down_ref = take(2) if loads else weights
    pick_ref, token_rows, gated_rows, back_rows = take(4)
    ahead_picks = take(1 if ahead else 0)
    sems = take(1)[0] if loads else None
    bins = keep_ref.shape[0]
    slots = sources * CAP
    experts = pick_ref.shape[0] // slots
    wide = slots + ahead * CAP

    def copies(expert):
        parts = []
        for which, (hbm, vmem) in enumerate(zip(weights, (up_ref, down_ref))):
            length = hbm.shape[1] // PARTS
            for part in range(PARTS):
                rows = (expert, pl.ds(part * length, length))
                sem = sems.at[expert, PARTS * which + part]
                parts.append(pltpu.make_async_copy(hbm.at[rows], vmem.at[rows], sem))
        return parts

    if loads:
        for local in range(experts):
            for copy in copies(local):
                copy.start()

    values = [
        jnp.concatenate([piece[...] for piece in block], axis=0) if len(block) > 1 else block[0]
        for block in blocks
    ]
    base = base_ref[0].astype(jnp.float32)
    notes = [value[bins : bins + NOTES, :bins] for value in values]
    gate_column = pick_slots(notes, base, top, experts, pick_ref)
    grads = jnp.concatenate([value[bins + NOTES :] for value in values], axis=0)
    gated_rows[...] = (gate_column * dot_nn(pick_ref[...], grads)).astype(jnp.bfloat16)
    if not later:
        tokens = jnp.concatenate([value[:bins] for value in values], axis=0)
        picked = dot_nn(pick_ref[...], tokens).astype(jnp.bfloat16)
        for local in range(experts):
            token_rows[local * wide : local * wide + slots] = picked[
                local * slots : (local + 1) * slots
            ]
    if ahead:
        notes = [ref[bins : bins + NOTES, :bins] for ref in ahead_refs]
        pick_slots(notes, base, top, experts, ahead_picks[0])
        tokens = jnp.concatenate([ref[:bins] for ref in ahead_refs], axis=0)
        picked = dot_nn(ahead_picks[0][...], tokens).astype(jnp.bfloat16)
        more = ahead * CAP
        for local in range(experts):
            token_rows[local * wide + slots : (local + 1) * wide] = picked[
                local * more : (local + 1) * more
            ]

    @pl.loop(0, experts)
    def _(expert):
        if loads:
            for copy in copies(expert):
                copy.wait()
        rows = pl.ds(pl.multiple_of(expert * slots, 16), slots)
        if later:
            slopes = slope_refs[0][rows, :]
        else:
            wide_rows = pl.ds(pl.multiple_of(expert * wide, 16), wide)
            slopes = silu_slope(dot_nn(token_rows[wide_rows, :], up_ref[expert]))
        if ahead:
            more = ahead * CAP
            ahead_slopes[0][pl.ds(pl.multiple_of(expert * more, 16), more), :] = slopes[slots:]
            slopes = slopes[:slots]
        back_grad = dot_nt(gated_rows[rows, :], down_ref[expert])
        hidden_grad = (back_grad * slopes).astype(jnp.bfloat16)
        back_rows[rows, :] = dot_nt(hidden_grad, up_ref[expert]).astype(jnp.bfloat16)

    sums = dot_tn(pick_ref[...], back_rows[...])
    keep_ref[...] = sums[:bins].astype(jnp.bfloat16)
    rows = bins // pieces
    for piece, give_ref in enumerate(give_refs):
        give_ref[...] = sums[bins + piece * rows : bins + (piece + 1) * rows].astype(jnp.bfloat16)


def expert_back(base, blocks, weights, loads, bins, top, units, pieces, ahead, slopes):
    layout = [len(block) for block in blocks]
    later = slopes is not None
    experts, width, hidden = weights[0].shape
    slots = len(blocks) * CAP
    wide = slots + len(ahead) * CAP
    operands = [piece for block in blocks for piece in block] + list(ahead)
    operands += [slopes] if later else []
    more = [jax.ShapeDtypeStruct((experts * len(ahead) * CAP, hidden), jnp.float32)]
    out_shape = (
        [jax.ShapeDtypeStruct((bins, width), jnp.bfloat16)]
        + [jax.ShapeDtypeStruct((bins // pieces, width), jnp.bfloat16)] * pieces
        + (more if ahead else [])
        + ([jax.ShapeDtypeStruct(weight.shape, weight.dtype) for weight in weights] if loads else [])
    )
    return pl.pallas_call(
        functools.partial(expert_kernel, layout, len(ahead), later, loads, pieces, top),
        out_shape=out_shape,
        in_specs=[pl.BlockSpec(memory_space=pltpu.SMEM)]
        + [pl.BlockSpec(memory_space=pltpu.VMEM)] * len(operands)
        + [pl.BlockSpec(memory_space=pltpu.HBM if loads else pltpu.VMEM)] * 2,
        out_specs=[pl.BlockSpec(memory_space=pltpu.VMEM)] * len(out_shape),
        scratch_shapes=[
            pltpu.VMEM((experts * slots, len(blocks) * bins), jnp.bfloat16),
            pltpu.VMEM((16 if later else experts * wide, width), jnp.bfloat16),
            pltpu.VMEM((experts * slots, width), jnp.bfloat16),
            pltpu.VMEM((experts * slots, width), jnp.bfloat16),
        ]
        + [pltpu.VMEM((experts * len(ahead) * CAP, len(ahead) * bins), jnp.bfloat16)]
        * (1 if ahead else 0)
        + [pltpu.SemaphoreType.DMA((experts, 2 * PARTS))] * (1 if loads else 0),
        compiler_params=pltpu.CompilerParams(vmem_limit_bytes=VMEM_EXPERTS),
        cost_estimate=cost(units),
        name="expert_back",
    )(base, *operands, *weights)


def per_device(
    queries, key_rows, value_rows, out_grad, moe_input, routes, route_gates, up_weight, down_weight
):
    members = lax.axis_size("exp")
    me = lax.axis_index("exp")
    groups = lax.axis_size("ctx")
    chips = members // 2
    half = chips // 2
    _, bins, top = routes.shape
    base = (me * up_weight.shape[0]).astype(jnp.int32).reshape(1)

    def swap(block):
        return lax.ppermute(block, "exp", [(i, i ^ 1) for i in range(members)])

    def hop(block, step):
        return lax.ppermute(
            block, "exp", [(i, (i + 2 * step) % members) for i in range(members)]
        )

    def pair(*pieces):
        return [list(pieces), [swap(piece) for piece in pieces]]

    def work(blocks, weights, units, pieces=1, ahead=(), slopes=None, loads=False):
        kept, *rest = expert_back(
            base, blocks, weights, loads, bins, top, units, pieces, ahead, slopes
        )
        return kept, rest[:pieces], rest[pieces:]

    def add_up(*members):
        return functools.reduce(jnp.add, [member.astype(jnp.float32) for member in members])

    def joined(pieces):
        return pieces[0] if len(pieces) == 1 else jnp.concatenate(pieces, axis=0)

    barrier = lax.optimization_barrier
    own = make_block(moe_input[0], out_grad[0], routes[0], route_gates[0])
    left, right_rows = hop(own, -1), hop(own[: bins + NOTES], 1)
    own_pair = pair(own)
    mine = lax.axis_index("ctx").astype(jnp.int32).reshape(1)
    rows = (queries[0], key_rows[0], value_rows[0], out_grad[0])
    packed = pack_groups(mine, rows, groups)
    own_pair, packed = barrier((own_pair, packed))
    heads = exchange(packed)
    kept, give, weights = work(own_pair, (up_weight, down_weight), OWN_COST, loads=True)
    heads, kept, give, left = barrier((heads, kept, give, left))
    total = add_up(kept, joined([swap(piece) for piece in give]))
    left_pair, right_grads = pair(left), out_grad[0]
    results = heads_back(heads)
    left_pair, results, right_rows = barrier((left_pair, results, right_rows))
    results = exchange(results)
    right_partner = swap(right_rows)
    left_sums, slopes = [], None
    for d in range(1, half):
        left = hop(left, -1)
        ahead = () if d > 1 else (right_rows, right_partner)
        kept, give, more = work(left_pair, weights, LEFT_COST, ahead=ahead)
        slopes = more[0] if d == 1 else slopes
        left, results, kept, give = barrier((left, results, kept, give))
        left_sums.append(add_up(kept, joined([swap(piece) for piece in give])))
        left_pair = pair(left)
    carried = left_sums[-1].astype(jnp.bfloat16)
    for sums in reversed(left_sums[:-1]):
        carried = add_up(sums, hop(carried, 1)).astype(jnp.bfloat16)
    left_halves = [hop(carried[: bins // 2], 1), hop(carried[bins // 2 :], 1)]
    rights = [(right_rows, hop(right_grads, 1))]
    for d in range(2, half):
        rights.append(tuple(hop(member, 1) for member in rights[-1]))
    kept, give, _ = work(left_pair, weights, FAR_COST)
    left_halves[0], rights, kept, give = barrier((left_halves[0], rights, kept, give))
    carried = add_up(kept, joined([swap(piece) for piece in give]))
    for d in range(half - 1, 0, -1):
        carried = hop(carried.astype(jnp.bfloat16), -1)
        right_pair = pair(*rights[d - 1])
        if d == 1:
            right_pair[1][0] = right_partner
        kept, give, _ = work(
            right_pair, weights, RIGHT_COST, 2, slopes=slopes if d == 1 else None
        )
        given = [swap(piece) for piece in give]
        kept, given, carried, left_halves = barrier((kept, given, carried, left_halves))
        carried = add_up(kept, joined(given), carried)
    total = add_up(total, joined(left_halves))
    carried = hop(carried.astype(jnp.bfloat16), -1)
    outs = unpack_groups(mine, results)
    total = add_up(total, carried).astype(jnp.bfloat16)
    return tuple(out[None] for out in outs) + (total[None],)


def solution(mesh):
    rows = P("exp", "ctx", None)
    experts = P("exp", None, None)
    return jax.shard_map(
        per_device,
        mesh=mesh,
        in_specs=(rows,) * 7 + (experts,) * 2,
        out_specs=(rows,) * 4,
        check_vma=False,
    )
```

```python
import functools

import jax
import jax.numpy as jnp
from jax import lax
from jax.experimental import pallas as pl
from jax.experimental.pallas import tpu as pltpu
from jax.sharding import PartitionSpec as P

HD = 128
CAP = 24
NOTES = 16
PARTS = 4
VMEM_BYTES = 36 * 1024 * 1024
VMEM_PACK = 58 * 1024 * 1024
VMEM_EXPERTS = 18 * 1024 * 1024
def cost(units):
    return pl.CostEstimate(
        flops=units * 10**9, bytes_accessed=units * 10**6, transcendentals=0
    )


SMALL = cost(0)
OWN_COST, HEADS_COST, LEFT_COST, FAR_COST, RIGHT_COST = 30, 30, 0, 0, 0
NT = (((1,), (1,)), ((), ()))
TN = (((0,), (0,)), ((), ()))


def dot_nt(left, right):
    return lax.dot_general(left, right, NT, preferred_element_type=jnp.float32)


def dot_tn(left, right):
    return lax.dot_general(left, right, TN, preferred_element_type=jnp.float32)


def dot_nn(left, right):
    return jnp.dot(left, right, preferred_element_type=jnp.float32)


def silu_slope(preact):
    sigmoid = jax.nn.sigmoid(preact)
    return sigmoid * (1.0 + preact * (1.0 - sigmoid))


def pack_kernel(mine_ref, *refs):
    members, blocks = refs[:4], refs[4:]
    width = blocks[0].shape[2]
    for place, block in enumerate(blocks):
        first = pl.multiple_of((mine_ref[0] ^ place) * width, 128)
        for row, member in enumerate(members):
            block[row] = member[:, pl.ds(first, width)]


def pack_groups(mine, members, groups):
    bins, width = members[0].shape
    block = jax.ShapeDtypeStruct((4, bins, width // groups), jnp.bfloat16)
    return pl.pallas_call(
        pack_kernel,
        out_shape=[block] * groups,
        in_specs=[pl.BlockSpec(memory_space=pltpu.SMEM)]
        + [pl.BlockSpec(memory_space=pltpu.VMEM)] * 4,
        out_specs=[pl.BlockSpec(memory_space=pltpu.VMEM)] * groups,
        compiler_params=pltpu.CompilerParams(vmem_limit_bytes=VMEM_PACK),
        cost_estimate=SMALL,
        name="pack_groups",
    )(mine, *members)


def unpack_kernel(mine_ref, *refs):
    blocks, outs = refs[:-3], refs[-3:]
    width = blocks[0].shape[2]
    for place, block in enumerate(blocks):
        first = pl.multiple_of((mine_ref[0] ^ place) * width, 128)
        for row, out in enumerate(outs):
            out[:, pl.ds(first, width)] = block[row]


def unpack_groups(mine, blocks):
    groups = len(blocks)
    bins, width = blocks[0].shape[1], blocks[0].shape[2] * groups
    out = jax.ShapeDtypeStruct((bins, width), jnp.bfloat16)
    return pl.pallas_call(
        unpack_kernel,
        out_shape=[out] * 3,
        in_specs=[pl.BlockSpec(memory_space=pltpu.SMEM)]
        + [pl.BlockSpec(memory_space=pltpu.VMEM)] * groups,
        out_specs=[pl.BlockSpec(memory_space=pltpu.VMEM)] * 3,
        compiler_params=pltpu.CompilerParams(vmem_limit_bytes=VMEM_BYTES),
        cost_estimate=SMALL,
        name="unpack_groups",
    )(mine, *blocks)


def heads_kernel(*refs):
    count = len(refs) // 2
    blocks, outs = refs[:count], refs[count:]
    bins = blocks[0].shape[1]
    scale = HD ** (-0.5)
    query, key, value, grad = (
        jnp.concatenate([block[row] for block in blocks], axis=0) for row in range(4)
    )
    scores = dot_nt(key, query) * scale
    powers = jnp.exp(scores - jnp.max(scores, axis=0, keepdims=True))
    probs = powers * (1.0 / jnp.sum(powers, axis=0, keepdims=True))
    prob_grad = dot_nt(value, grad)
    row_delta = jnp.sum(probs * prob_grad, axis=0, keepdims=True)
    score_grad = (probs * (prob_grad - row_delta)).astype(jnp.bfloat16)
    results = (
        dot_tn(score_grad, key) * scale,
        dot_nn(score_grad, query) * scale,
        dot_nn(probs.astype(jnp.bfloat16), grad),
    )
    for row, result in enumerate(results):
        result = result.astype(jnp.bfloat16)
        for place, out in enumerate(outs):
            out[row] = result[place * bins : (place + 1) * bins]


def heads_back(blocks):
    groups = len(blocks)
    bins, width = blocks[0].shape[1:]
    rows = bins * groups
    heads = width // HD
    return pl.pallas_call(
        heads_kernel,
        grid=(heads,),
        out_shape=[jax.ShapeDtypeStruct((3, bins, width), jnp.bfloat16)] * groups,
        in_specs=[pl.BlockSpec((4, bins, HD), lambda h: (0, 0, h))] * groups,
        out_specs=[pl.BlockSpec((3, bins, HD), lambda h: (0, 0, h))] * groups,
        compiler_params=pltpu.CompilerParams(vmem_limit_bytes=6 * 1024 * 1024 + 40 * rows * rows),
        cost_estimate=cost(HEADS_COST),
        name="heads_back",
    )(*blocks)


def exchange(blocks):
    groups = len(blocks)
    return [blocks[0]] + [
        lax.ppermute(blocks[place], "ctx", [(i, i ^ place) for i in range(groups)])
        for place in range(1, groups)
    ]


def make_block(tokens, grads, routes, gates):
    rest = gates.T
    pieces = [(routes.T + 1).astype(jnp.float32)]
    for _ in range(3):
        piece = lax.reduce_precision(rest, 8, 7)
        rest = rest - piece
        pieces.append(piece)
    notes = jnp.concatenate(pieces, axis=0).astype(jnp.bfloat16)
    notes = jnp.pad(notes, ((0, NOTES - notes.shape[0]), (0, tokens.shape[1] - notes.shape[1])))
    return jnp.concatenate([tokens, notes, grads], axis=0)


def pick_slots(notes, base, top, experts, pick_ref):
    bins = notes[0].shape[1]
    slots = len(notes) * CAP
    earlier = lax.broadcasted_iota(jnp.int32, (bins, bins), 0)
    later = lax.broadcasted_iota(jnp.int32, (bins, bins), 1)
    before = (earlier < later).astype(jnp.bfloat16)
    slot = lax.broadcasted_iota(jnp.int32, (slots, bins), 0).astype(jnp.float32)
    gates = [jnp.zeros((slots, 1), jnp.float32)] * experts
    for source, note in enumerate(notes):
        note = note.astype(jnp.float32)
        named = note[:top] - base
        weights = note[top : 2 * top] + note[2 * top : 3 * top] + note[3 * top : 4 * top]
        hits = [(named == float(local + 1)).astype(jnp.float32) for local in range(experts)]
        chosen = [jnp.sum(hit, axis=0, keepdims=True) for hit in hits]
        stacked = jnp.concatenate(chosen, axis=0)
        position = dot_nn(stacked.astype(jnp.bfloat16), before)
        for local in range(experts):
            place = jnp.where(
                chosen[local] > 0.0, position[local : local + 1] + float(source * CAP), -1.0
            )
            pick = (slot == place).astype(jnp.float32)
            gate = jnp.sum(hits[local] * weights, axis=0, keepdims=True)
            gates[local] = gates[local] + jnp.sum(pick * gate, axis=1, keepdims=True)
            pick_ref[
                local * slots : (local + 1) * slots, source * bins : (source + 1) * bins
            ] = pick.astype(jnp.bfloat16)
    return jnp.concatenate(gates, axis=0)


def expert_kernel(layout, ahead, later, loads, pieces, top, base_ref, *refs):
    refs = list(refs)

    def take(count):
        taken = refs[:count]
        del refs[:count]
        return taken

    sources = len(layout)
    blocks = [take(length) for length in layout]
    ahead_refs = take(ahead)
    slope_refs = take(1 if later else 0)
    weights = take(2)
    (keep_ref,) = take(1)
    give_refs = take(pieces)
    ahead_slopes = take(1 if ahead else 0)
    up_ref, down_ref = take(2) if loads else weights
    pick_ref, token_rows, gated_rows, back_rows = take(4)
    ahead_picks = take(1 if ahead else 0)
    sems = take(1)[0] if loads else None
    bins = keep_ref.shape[0]
    slots = sources * CAP
    experts = pick_ref.shape[0] // slots
    wide = slots + ahead * CAP

    def copies(expert):
        parts = []
        for which, (hbm, vmem) in enumerate(zip(weights, (up_ref, down_ref))):
            length = hbm.shape[1] // PARTS
            for part in range(PARTS):
                rows = (expert, pl.ds(part * length, length))
                sem = sems.at[expert, PARTS * which + part]
                parts.append(pltpu.make_async_copy(hbm.at[rows], vmem.at[rows], sem))
        return parts

    if loads:
        for local in range(experts):
            for copy in copies(local):
                copy.start()

    values = [
        jnp.concatenate([piece[...] for piece in block], axis=0) if len(block) > 1 else block[0]
        for block in blocks
    ]
    base = base_ref[0].astype(jnp.float32)
    notes = [value[bins : bins + NOTES, :bins] for value in values]
    gate_column = pick_slots(notes, base, top, experts, pick_ref)
    grads = jnp.concatenate([value[bins + NOTES :] for value in values], axis=0)
    gated_rows[...] = (gate_column * dot_nn(pick_ref[...], grads)).astype(jnp.bfloat16)
    if not later:
        tokens = jnp.concatenate([value[:bins] for value in values], axis=0)
        picked = dot_nn(pick_ref[...], tokens).astype(jnp.bfloat16)
        for local in range(experts):
            token_rows[local * wide : local * wide + slots] = picked[
                local * slots : (local + 1) * slots
            ]
    if ahead:
        notes = [ref[bins : bins + NOTES, :bins] for ref in ahead_refs]
        pick_slots(notes, base, top, experts, ahead_picks[0])
        tokens = jnp.concatenate([ref[:bins] for ref in ahead_refs], axis=0)
        picked = dot_nn(ahead_picks[0][...], tokens).astype(jnp.bfloat16)
        more = ahead * CAP
        for local in range(experts):
            token_rows[local * wide + slots : (local + 1) * wide] = picked[
                local * more : (local + 1) * more
            ]

    @pl.loop(0, experts)
    def _(expert):
        if loads:
            for copy in copies(expert):
                copy.wait()
        rows = pl.ds(pl.multiple_of(expert * slots, 16), slots)
        if later:
            slopes = slope_refs[0][rows, :]
        else:
            wide_rows = pl.ds(pl.multiple_of(expert * wide, 16), wide)
            slopes = silu_slope(dot_nn(token_rows[wide_rows, :], up_ref[expert]))
        if ahead:
            more = ahead * CAP
            ahead_slopes[0][pl.ds(pl.multiple_of(expert * more, 16), more), :] = slopes[slots:]
            slopes = slopes[:slots]
        back_grad = dot_nt(gated_rows[rows, :], down_ref[expert])
        hidden_grad = (back_grad * slopes).astype(jnp.bfloat16)
        back_rows[rows, :] = dot_nt(hidden_grad, up_ref[expert]).astype(jnp.bfloat16)

    sums = dot_tn(pick_ref[...], back_rows[...])
    keep_ref[...] = sums[:bins].astype(jnp.bfloat16)
    rows = bins // pieces
    for piece, give_ref in enumerate(give_refs):
        give_ref[...] = sums[bins + piece * rows : bins + (piece + 1) * rows].astype(jnp.bfloat16)


def expert_back(base, blocks, weights, loads, bins, top, units, pieces, ahead, slopes):
    layout = [len(block) for block in blocks]
    later = slopes is not None
    experts, width, hidden = weights[0].shape
    slots = len(blocks) * CAP
    wide = slots + len(ahead) * CAP
    operands = [piece for block in blocks for piece in block] + list(ahead)
    operands += [slopes] if later else []
    more = [jax.ShapeDtypeStruct((experts * len(ahead) * CAP, hidden), jnp.float32)]
    out_shape = (
        [jax.ShapeDtypeStruct((bins, width), jnp.bfloat16)]
        + [jax.ShapeDtypeStruct((bins // pieces, width), jnp.bfloat16)] * pieces
        + (more if ahead else [])
        + ([jax.ShapeDtypeStruct(weight.shape, weight.dtype) for weight in weights] if loads else [])
    )
    return pl.pallas_call(
        functools.partial(expert_kernel, layout, len(ahead), later, loads, pieces, top),
        out_shape=out_shape,
        in_specs=[pl.BlockSpec(memory_space=pltpu.SMEM)]
        + [pl.BlockSpec(memory_space=pltpu.VMEM)] * len(operands)
        + [pl.BlockSpec(memory_space=pltpu.HBM if loads else pltpu.VMEM)] * 2,
        out_specs=[pl.BlockSpec(memory_space=pltpu.VMEM)] * len(out_shape),
        scratch_shapes=[
            pltpu.VMEM((experts * slots, len(blocks) * bins), jnp.bfloat16),
            pltpu.VMEM((16 if later else experts * wide, width), jnp.bfloat16),
            pltpu.VMEM((experts * slots, width), jnp.bfloat16),
            pltpu.VMEM((experts * slots, width), jnp.bfloat16),
        ]
        + [pltpu.VMEM((experts * len(ahead) * CAP, len(ahead) * bins), jnp.bfloat16)]
        * (1 if ahead else 0)
        + [pltpu.SemaphoreType.DMA((experts, 2 * PARTS))] * (1 if loads else 0),
        compiler_params=pltpu.CompilerParams(vmem_limit_bytes=VMEM_EXPERTS),
        cost_estimate=cost(units),
        name="expert_back",
    )(base, *operands, *weights)


def per_device(
    queries, key_rows, value_rows, out_grad, moe_input, routes, route_gates, up_weight, down_weight
):
    members = lax.axis_size("exp")
    me = lax.axis_index("exp")
    groups = lax.axis_size("ctx")
    chips = members // 2
    half = chips // 2
    _, bins, top = routes.shape
    base = (me * up_weight.shape[0]).astype(jnp.int32).reshape(1)

    def swap(block):
        return lax.ppermute(block, "exp", [(i, i ^ 1) for i in range(members)])

    def hop(block, step):
        return lax.ppermute(
            block, "exp", [(i, (i + 2 * step) % members) for i in range(members)]
        )

    def pair(*pieces):
        return [list(pieces), [swap(piece) for piece in pieces]]

    def work(blocks, weights, units, pieces=1, ahead=(), slopes=None, loads=False):
        kept, *rest = expert_back(
            base, blocks, weights, loads, bins, top, units, pieces, ahead, slopes
        )
        return kept, rest[:pieces], rest[pieces:]

    def add_up(*members):
        return functools.reduce(jnp.add, [member.astype(jnp.float32) for member in members])

    def joined(pieces):
        return pieces[0] if len(pieces) == 1 else jnp.concatenate(pieces, axis=0)

    barrier = lax.optimization_barrier
    own = make_block(moe_input[0], out_grad[0], routes[0], route_gates[0])
    left, right_rows = hop(own, -1), hop(own[: bins + NOTES], 1)
    own_pair = pair(own)
    mine = lax.axis_index("ctx").astype(jnp.int32).reshape(1)
    rows = (queries[0], key_rows[0], value_rows[0], out_grad[0])
    packed = pack_groups(mine, rows, groups)
    own_pair, packed = barrier((own_pair, packed))
    heads = exchange(packed)
    kept, give, weights = work(own_pair, (up_weight, down_weight), OWN_COST, loads=True)
    heads, kept, give, left = barrier((heads, kept, give, left))
    total = add_up(kept, joined([swap(piece) for piece in give]))
    left_pair, right_grads = pair(left), out_grad[0]
    results = heads_back(heads)
    left_pair, results, right_rows = barrier((left_pair, results, right_rows))
    results = exchange(results)
    right_partner = swap(right_rows)
    left_sums, slopes = [], None
    for d in range(1, half):
        left = hop(left, -1)
        ahead = () if d > 1 else (right_rows, right_partner)
        kept, give, more = work(left_pair, weights, LEFT_COST, ahead=ahead)
        slopes = more[0] if d == 1 else slopes
        left, results, kept, give = barrier((left, results, kept, give))
        left_sums.append(add_up(kept, joined([swap(piece) for piece in give])))
        left_pair = pair(left)
    carried = left_sums[-1].astype(jnp.bfloat16)
    for sums in reversed(left_sums[:-1]):
        carried = add_up(sums, hop(carried, 1)).astype(jnp.bfloat16)
    left_carried = hop(carried, 1)
    rights = [(right_rows, hop(right_grads, 1))]
    for d in range(2, half):
        rights.append(tuple(hop(member, 1) for member in rights[-1]))
    kept, give, _ = work(left_pair, weights, FAR_COST, 2)
    rights, kept, give = barrier((rights, kept, give))
    carried = add_up(kept, joined([swap(piece) for piece in give]))
    for d in range(half - 1, 0, -1):
        carried = hop(carried.astype(jnp.bfloat16), -1)
        rows, grads = rights[d - 1]
        halves = [swap(grads[: bins // 2]), swap(grads[bins // 2 :])]
        right_pair = [[rows, grads], [right_partner if d == 1 else swap(rows), *halves]]
        if d == 1:
            right_pair, left_carried = barrier((right_pair, left_carried))
        kept, give, _ = work(
            right_pair, weights, RIGHT_COST, 2, slopes=slopes if d == 1 else None
        )
        given = [swap(piece) for piece in give]
        kept, given, carried = barrier((kept, given, carried))
        carried = add_up(kept, joined(given), carried)
    total = add_up(total, left_carried)
    carried = hop(carried.astype(jnp.bfloat16), -1)
    outs = unpack_groups(mine, results)
    total = add_up(total, carried).astype(jnp.bfloat16)
    return tuple(out[None] for out in outs) + (total[None],)


def solution(mesh):
    rows = P("exp", "ctx", None)
    experts = P("exp", None, None)
    return jax.shard_map(
        per_device,
        mesh=mesh,
        in_specs=(rows,) * 7 + (experts,) * 2,
        out_specs=(rows,) * 4,
        check_vma=False,
    )
```

```python
import functools

import jax
import jax.numpy as jnp
from jax import lax
from jax.experimental import pallas as pl
from jax.experimental.pallas import tpu as pltpu
from jax.sharding import PartitionSpec as P

HD = 128
CAP = 24
NOTES = 16
PARTS = 4
VMEM_BYTES = 36 * 1024 * 1024
VMEM_PACK = 58 * 1024 * 1024
VMEM_EXPERTS = 18 * 1024 * 1024
def cost(units):
    return pl.CostEstimate(
        flops=units * 10**9, bytes_accessed=units * 10**6, transcendentals=0
    )


SMALL = cost(0)
OWN_COST, HEADS_COST, LEFT_COST, FAR_COST, RIGHT_COST = 30, 30, 0, 0, 30
NT = (((1,), (1,)), ((), ()))
TN = (((0,), (0,)), ((), ()))


def dot_nt(left, right):
    return lax.dot_general(left, right, NT, preferred_element_type=jnp.float32)


def dot_tn(left, right):
    return lax.dot_general(left, right, TN, preferred_element_type=jnp.float32)


def dot_nn(left, right):
    return jnp.dot(left, right, preferred_element_type=jnp.float32)


def silu_slope(preact):
    sigmoid = jax.nn.sigmoid(preact)
    return sigmoid * (1.0 + preact * (1.0 - sigmoid))


def pack_kernel(mine_ref, *refs):
    members, blocks = refs[:4], refs[4:]
    width = blocks[0].shape[2]
    for place, block in enumerate(blocks):
        first = pl.multiple_of((mine_ref[0] ^ place) * width, 128)
        for row, member in enumerate(members):
            block[row] = member[:, pl.ds(first, width)]


def pack_groups(mine, members, groups):
    bins, width = members[0].shape
    block = jax.ShapeDtypeStruct((4, bins, width // groups), jnp.bfloat16)
    return pl.pallas_call(
        pack_kernel,
        out_shape=[block] * groups,
        in_specs=[pl.BlockSpec(memory_space=pltpu.SMEM)]
        + [pl.BlockSpec(memory_space=pltpu.VMEM)] * 4,
        out_specs=[pl.BlockSpec(memory_space=pltpu.VMEM)] * groups,
        compiler_params=pltpu.CompilerParams(vmem_limit_bytes=VMEM_PACK),
        cost_estimate=SMALL,
        name="pack_groups",
    )(mine, *members)


def unpack_kernel(mine_ref, *refs):
    blocks, outs = refs[:-3], refs[-3:]
    width = blocks[0].shape[2]
    for place, block in enumerate(blocks):
        first = pl.multiple_of((mine_ref[0] ^ place) * width, 128)
        for row, out in enumerate(outs):
            out[:, pl.ds(first, width)] = block[row]


def unpack_groups(mine, blocks):
    groups = len(blocks)
    bins, width = blocks[0].shape[1], blocks[0].shape[2] * groups
    out = jax.ShapeDtypeStruct((bins, width), jnp.bfloat16)
    return pl.pallas_call(
        unpack_kernel,
        out_shape=[out] * 3,
        in_specs=[pl.BlockSpec(memory_space=pltpu.SMEM)]
        + [pl.BlockSpec(memory_space=pltpu.VMEM)] * groups,
        out_specs=[pl.BlockSpec(memory_space=pltpu.VMEM)] * 3,
        compiler_params=pltpu.CompilerParams(vmem_limit_bytes=VMEM_BYTES),
        cost_estimate=SMALL,
        name="unpack_groups",
    )(mine, *blocks)


def heads_kernel(*refs):
    count = len(refs) // 2
    blocks, outs = refs[:count], refs[count:]
    bins = blocks[0].shape[1]
    scale = HD ** (-0.5)
    query, key, value, grad = (
        jnp.concatenate([block[row] for block in blocks], axis=0) for row in range(4)
    )
    scores = dot_nt(key, query) * scale
    powers = jnp.exp(scores - jnp.max(scores, axis=0, keepdims=True))
    probs = powers * (1.0 / jnp.sum(powers, axis=0, keepdims=True))
    prob_grad = dot_nt(value, grad)
    row_delta = jnp.sum(probs * prob_grad, axis=0, keepdims=True)
    score_grad = (probs * (prob_grad - row_delta)).astype(jnp.bfloat16)
    results = (
        dot_tn(score_grad, key) * scale,
        dot_nn(score_grad, query) * scale,
        dot_nn(probs.astype(jnp.bfloat16), grad),
    )
    for row, result in enumerate(results):
        result = result.astype(jnp.bfloat16)
        for place, out in enumerate(outs):
            out[row] = result[place * bins : (place + 1) * bins]


def heads_back(blocks):
    groups = len(blocks)
    bins, width = blocks[0].shape[1:]
    rows = bins * groups
    heads = width // HD
    return pl.pallas_call(
        heads_kernel,
        grid=(heads,),
        out_shape=[jax.ShapeDtypeStruct((3, bins, width), jnp.bfloat16)] * groups,
        in_specs=[pl.BlockSpec((4, bins, HD), lambda h: (0, 0, h))] * groups,
        out_specs=[pl.BlockSpec((3, bins, HD), lambda h: (0, 0, h))] * groups,
        compiler_params=pltpu.CompilerParams(vmem_limit_bytes=6 * 1024 * 1024 + 40 * rows * rows),
        cost_estimate=cost(HEADS_COST),
        name="heads_back",
    )(*blocks)


def exchange(blocks):
    groups = len(blocks)
    return [blocks[0]] + [
        lax.ppermute(blocks[place], "ctx", [(i, i ^ place) for i in range(groups)])
        for place in range(1, groups)
    ]


def make_block(tokens, grads, routes, gates):
    rest = gates.T
    pieces = [(routes.T + 1).astype(jnp.float32)]
    for _ in range(3):
        piece = lax.reduce_precision(rest, 8, 7)
        rest = rest - piece
        pieces.append(piece)
    notes = jnp.concatenate(pieces, axis=0).astype(jnp.bfloat16)
    notes = jnp.pad(notes, ((0, NOTES - notes.shape[0]), (0, tokens.shape[1] - notes.shape[1])))
    return jnp.concatenate([tokens, notes, grads], axis=0)


def pick_slots(notes, base, top, experts, pick_ref):
    bins = notes[0].shape[1]
    slots = len(notes) * CAP
    earlier = lax.broadcasted_iota(jnp.int32, (bins, bins), 0)
    later = lax.broadcasted_iota(jnp.int32, (bins, bins), 1)
    before = (earlier < later).astype(jnp.bfloat16)
    slot = lax.broadcasted_iota(jnp.int32, (slots, bins), 0).astype(jnp.float32)
    gates = [jnp.zeros((slots, 1), jnp.float32)] * experts
    for source, note in enumerate(notes):
        note = note.astype(jnp.float32)
        named = note[:top] - base
        weights = note[top : 2 * top] + note[2 * top : 3 * top] + note[3 * top : 4 * top]
        hits = [(named == float(local + 1)).astype(jnp.float32) for local in range(experts)]
        chosen = [jnp.sum(hit, axis=0, keepdims=True) for hit in hits]
        stacked = jnp.concatenate(chosen, axis=0)
        position = dot_nn(stacked.astype(jnp.bfloat16), before)
        for local in range(experts):
            place = jnp.where(
                chosen[local] > 0.0, position[local : local + 1] + float(source * CAP), -1.0
            )
            pick = (slot == place).astype(jnp.float32)
            gate = jnp.sum(hits[local] * weights, axis=0, keepdims=True)
            gates[local] = gates[local] + jnp.sum(pick * gate, axis=1, keepdims=True)
            pick_ref[
                local * slots : (local + 1) * slots, source * bins : (source + 1) * bins
            ] = pick.astype(jnp.bfloat16)
    return jnp.concatenate(gates, axis=0)


def expert_kernel(layout, ahead, later, loads, pieces, top, base_ref, *refs):
    refs = list(refs)

    def take(count):
        taken = refs[:count]
        del refs[:count]
        return taken

    sources = len(layout)
    blocks = [take(length) for length in layout]
    ahead_refs = take(ahead)
    slope_refs = take(1 if later else 0)
    weights = take(2)
    (keep_ref,) = take(1)
    give_refs = take(pieces)
    ahead_slopes = take(1 if ahead else 0)
    up_ref, down_ref = take(2) if loads else weights
    pick_ref, token_rows, gated_rows, back_rows = take(4)
    ahead_picks = take(1 if ahead else 0)
    sems = take(1)[0] if loads else None
    bins = keep_ref.shape[0]
    slots = sources * CAP
    experts = pick_ref.shape[0] // slots
    wide = slots + ahead * CAP

    def copies(expert):
        parts = []
        for which, (hbm, vmem) in enumerate(zip(weights, (up_ref, down_ref))):
            length = hbm.shape[1] // PARTS
            for part in range(PARTS):
                rows = (expert, pl.ds(part * length, length))
                sem = sems.at[expert, PARTS * which + part]
                parts.append(pltpu.make_async_copy(hbm.at[rows], vmem.at[rows], sem))
        return parts

    if loads:
        for local in range(experts):
            for copy in copies(local):
                copy.start()

    values = [
        jnp.concatenate([piece[...] for piece in block], axis=0) if len(block) > 1 else block[0]
        for block in blocks
    ]
    base = base_ref[0].astype(jnp.float32)
    notes = [value[bins : bins + NOTES, :bins] for value in values]
    gate_column = pick_slots(notes, base, top, experts, pick_ref)
    grads = jnp.concatenate([value[bins + NOTES :] for value in values], axis=0)
    gated_rows[...] = (gate_column * dot_nn(pick_ref[...], grads)).astype(jnp.bfloat16)
    if not later:
        tokens = jnp.concatenate([value[:bins] for value in values], axis=0)
        picked = dot_nn(pick_ref[...], tokens).astype(jnp.bfloat16)
        for local in range(experts):
            token_rows[local * wide : local * wide + slots] = picked[
                local * slots : (local + 1) * slots
            ]
    if ahead:
        notes = [ref[bins : bins + NOTES, :bins] for ref in ahead_refs]
        pick_slots(notes, base, top, experts, ahead_picks[0])
        tokens = jnp.concatenate([ref[:bins] for ref in ahead_refs], axis=0)
        picked = dot_nn(ahead_picks[0][...], tokens).astype(jnp.bfloat16)
        more = ahead * CAP
        for local in range(experts):
            token_rows[local * wide + slots : (local + 1) * wide] = picked[
                local * more : (local + 1) * more
            ]

    @pl.loop(0, experts)
    def _(expert):
        if loads:
            for copy in copies(expert):
                copy.wait()
        rows = pl.ds(pl.multiple_of(expert * slots, 16), slots)
        if later:
            slopes = slope_refs[0][rows, :]
        else:
            wide_rows = pl.ds(pl.multiple_of(expert * wide, 16), wide)
            slopes = silu_slope(dot_nn(token_rows[wide_rows, :], up_ref[expert]))
        if ahead:
            more = ahead * CAP
            ahead_slopes[0][pl.ds(pl.multiple_of(expert * more, 16), more), :] = slopes[slots:]
            slopes = slopes[:slots]
        back_grad = dot_nt(gated_rows[rows, :], down_ref[expert])
        hidden_grad = (back_grad * slopes).astype(jnp.bfloat16)
        back_rows[rows, :] = dot_nt(hidden_grad, up_ref[expert]).astype(jnp.bfloat16)

    sums = dot_tn(pick_ref[...], back_rows[...])
    keep_ref[...] = sums[:bins].astype(jnp.bfloat16)
    rows = bins // pieces
    for piece, give_ref in enumerate(give_refs):
        give_ref[...] = sums[bins + piece * rows : bins + (piece + 1) * rows].astype(jnp.bfloat16)


def expert_back(base, blocks, weights, loads, bins, top, units, pieces, ahead, slopes):
    layout = [len(block) for block in blocks]
    later = slopes is not None
    experts, width, hidden = weights[0].shape
    slots = len(blocks) * CAP
    wide = slots + len(ahead) * CAP
    operands = [piece for block in blocks for piece in block] + list(ahead)
    operands += [slopes] if later else []
    more = [jax.ShapeDtypeStruct((experts * len(ahead) * CAP, hidden), jnp.float32)]
    out_shape = (
        [jax.ShapeDtypeStruct((bins, width), jnp.bfloat16)]
        + [jax.ShapeDtypeStruct((bins // pieces, width), jnp.bfloat16)] * pieces
        + (more if ahead else [])
        + ([jax.ShapeDtypeStruct(weight.shape, weight.dtype) for weight in weights] if loads else [])
    )
    return pl.pallas_call(
        functools.partial(expert_kernel, layout, len(ahead), later, loads, pieces, top),
        out_shape=out_shape,
        in_specs=[pl.BlockSpec(memory_space=pltpu.SMEM)]
        + [pl.BlockSpec(memory_space=pltpu.VMEM)] * len(operands)
        + [pl.BlockSpec(memory_space=pltpu.HBM if loads else pltpu.VMEM)] * 2,
        out_specs=[pl.BlockSpec(memory_space=pltpu.VMEM)] * len(out_shape),
        scratch_shapes=[
            pltpu.VMEM((experts * slots, len(blocks) * bins), jnp.bfloat16),
            pltpu.VMEM((16 if later else experts * wide, width), jnp.bfloat16),
            pltpu.VMEM((experts * slots, width), jnp.bfloat16),
            pltpu.VMEM((experts * slots, width), jnp.bfloat16),
        ]
        + [pltpu.VMEM((experts * len(ahead) * CAP, len(ahead) * bins), jnp.bfloat16)]
        * (1 if ahead else 0)
        + [pltpu.SemaphoreType.DMA((experts, 2 * PARTS))] * (1 if loads else 0),
        compiler_params=pltpu.CompilerParams(vmem_limit_bytes=VMEM_EXPERTS),
        cost_estimate=cost(units),
        name="expert_back",
    )(base, *operands, *weights)


def per_device(
    queries, key_rows, value_rows, out_grad, moe_input, routes, route_gates, up_weight, down_weight
):
    members = lax.axis_size("exp")
    me = lax.axis_index("exp")
    groups = lax.axis_size("ctx")
    chips = members // 2
    half = chips // 2
    _, bins, top = routes.shape
    base = (me * up_weight.shape[0]).astype(jnp.int32).reshape(1)

    def swap(block):
        return lax.ppermute(block, "exp", [(i, i ^ 1) for i in range(members)])

    def hop(block, step):
        return lax.ppermute(
            block, "exp", [(i, (i + 2 * step) % members) for i in range(members)]
        )

    def pair(*pieces):
        return [list(pieces), [swap(piece) for piece in pieces]]

    def work(blocks, weights, units, pieces=1, ahead=(), slopes=None, loads=False):
        kept, *rest = expert_back(
            base, blocks, weights, loads, bins, top, units, pieces, ahead, slopes
        )
        return kept, rest[:pieces], rest[pieces:]

    def add_up(*members):
        return functools.reduce(jnp.add, [member.astype(jnp.float32) for member in members])

    def joined(pieces):
        return pieces[0] if len(pieces) == 1 else jnp.concatenate(pieces, axis=0)

    barrier = lax.optimization_barrier
    own = make_block(moe_input[0], out_grad[0], routes[0], route_gates[0])
    left, right_rows = hop(own, -1), hop(own[: bins + NOTES], 1)
    own_pair = pair(own)
    mine = lax.axis_index("ctx").astype(jnp.int32).reshape(1)
    rows = (queries[0], key_rows[0], value_rows[0], out_grad[0])
    packed = pack_groups(mine, rows, groups)
    own_pair, packed = barrier((own_pair, packed))
    heads = exchange(packed)
    kept, give, weights = work(own_pair, (up_weight, down_weight), OWN_COST, loads=True)
    heads, kept, give, left = barrier((heads, kept, give, left))
    total = add_up(kept, joined([swap(piece) for piece in give]))
    left_pair, right_grads = pair(left), out_grad[0]
    results = heads_back(heads)
    left_pair, results, right_rows = barrier((left_pair, results, right_rows))
    results = exchange(results)
    right_partner = swap(right_rows)
    left_sums, slopes = [], None
    for d in range(1, half):
        left = hop(left, -1)
        ahead = () if d > 1 else (right_rows, right_partner)
        kept, give, more = work(left_pair, weights, LEFT_COST, ahead=ahead)
        slopes = more[0] if d == 1 else slopes
        left, results, kept, give = barrier((left, results, kept, give))
        left_sums.append(add_up(kept, joined([swap(piece) for piece in give])))
        left_pair = pair(left)
    carried = left_sums[-1].astype(jnp.bfloat16)
    for sums in reversed(left_sums[:-1]):
        carried = add_up(sums, hop(carried, 1)).astype(jnp.bfloat16)
    left_halves = [hop(carried[: bins // 2], 1), hop(carried[bins // 2 :], 1)]
    rights = [(right_rows, hop(right_grads, 1))]
    for d in range(2, half):
        rights.append(tuple(hop(member, 1) for member in rights[-1]))
    kept, give, _ = work(left_pair, weights, FAR_COST)
    left_halves[0], rights, kept, give = barrier((left_halves[0], rights, kept, give))
    carried = add_up(kept, joined([swap(piece) for piece in give]))
    for d in range(half - 1, 0, -1):
        carried = hop(carried.astype(jnp.bfloat16), -1)
        right_pair = pair(*rights[d - 1])
        if d == 1:
            right_pair[1][0] = right_partner
        kept, give, _ = work(
            right_pair, weights, RIGHT_COST, 2, slopes=slopes if d == 1 else None
        )
        given = [swap(piece) for piece in give]
        kept, given, carried = barrier((kept, given, carried))
        carried = add_up(kept, joined(given), carried)
    carried = hop(carried.astype(jnp.bfloat16), -1)
    outs = unpack_groups(mine, results)
    total = add_up(total, joined(left_halves), carried).astype(jnp.bfloat16)
    return tuple(out[None] for out in outs) + (total[None],)


def solution(mesh):
    rows = P("exp", "ctx", None)
    experts = P("exp", None, None)
    return jax.shard_map(
        per_device,
        mesh=mesh,
        in_specs=(rows,) * 7 + (experts,) * 2,
        out_specs=(rows,) * 4,
        check_vma=False,
    )
```

```python
import functools

import jax
import jax.numpy as jnp
from jax import lax
from jax.experimental import pallas as pl
from jax.experimental.pallas import tpu as pltpu
from jax.sharding import PartitionSpec as P

HD = 128
CAP = 24
NOTES = 16
PARTS = 4
VMEM_BYTES = 36 * 1024 * 1024
VMEM_PACK = 58 * 1024 * 1024
VMEM_EXPERTS = 18 * 1024 * 1024
def cost(units):
    return pl.CostEstimate(
        flops=units * 10**9, bytes_accessed=units * 10**6, transcendentals=0
    )


SMALL = cost(0)
OWN_COST, HEADS_COST, LEFT_COST, FAR_COST, RIGHT_COST = 30, 30, 0, 0, 30
NT = (((1,), (1,)), ((), ()))
TN = (((0,), (0,)), ((), ()))


def dot_nt(left, right):
    return lax.dot_general(left, right, NT, preferred_element_type=jnp.float32)


def dot_tn(left, right):
    return lax.dot_general(left, right, TN, preferred_element_type=jnp.float32)


def dot_nn(left, right):
    return jnp.dot(left, right, preferred_element_type=jnp.float32)


def silu_slope(preact):
    sigmoid = jax.nn.sigmoid(preact)
    return sigmoid * (1.0 + preact * (1.0 - sigmoid))


def pack_kernel(mine_ref, *refs):
    members, blocks = refs[:4], refs[4:]
    width = blocks[0].shape[2]
    for place, block in enumerate(blocks):
        first = pl.multiple_of((mine_ref[0] ^ place) * width, 128)
        for row, member in enumerate(members):
            block[row] = member[:, pl.ds(first, width)]


def pack_groups(mine, members, groups):
    bins, width = members[0].shape
    block = jax.ShapeDtypeStruct((4, bins, width // groups), jnp.bfloat16)
    return pl.pallas_call(
        pack_kernel,
        out_shape=[block] * groups,
        in_specs=[pl.BlockSpec(memory_space=pltpu.SMEM)]
        + [pl.BlockSpec(memory_space=pltpu.VMEM)] * 4,
        out_specs=[pl.BlockSpec(memory_space=pltpu.VMEM)] * groups,
        compiler_params=pltpu.CompilerParams(vmem_limit_bytes=VMEM_PACK),
        cost_estimate=SMALL,
        name="pack_groups",
    )(mine, *members)


def unpack_kernel(mine_ref, *refs):
    blocks, outs = refs[:-3], refs[-3:]
    width = blocks[0].shape[2]
    for place, block in enumerate(blocks):
        first = pl.multiple_of((mine_ref[0] ^ place) * width, 128)
        for row, out in enumerate(outs):
            out[:, pl.ds(first, width)] = block[row]


def unpack_groups(mine, blocks):
    groups = len(blocks)
    bins, width = blocks[0].shape[1], blocks[0].shape[2] * groups
    out = jax.ShapeDtypeStruct((bins, width), jnp.bfloat16)
    return pl.pallas_call(
        unpack_kernel,
        out_shape=[out] * 3,
        in_specs=[pl.BlockSpec(memory_space=pltpu.SMEM)]
        + [pl.BlockSpec(memory_space=pltpu.VMEM)] * groups,
        out_specs=[pl.BlockSpec(memory_space=pltpu.VMEM)] * 3,
        compiler_params=pltpu.CompilerParams(vmem_limit_bytes=VMEM_BYTES),
        cost_estimate=SMALL,
        name="unpack_groups",
    )(mine, *blocks)


def heads_kernel(*refs):
    count = len(refs) // 2
    blocks, outs = refs[:count], refs[count:]
    bins = blocks[0].shape[1]
    scale = HD ** (-0.5)
    query, key, value, grad = (
        jnp.concatenate([block[row] for block in blocks], axis=0) for row in range(4)
    )
    scores = dot_nt(key, query) * scale
    powers = jnp.exp(scores - jnp.max(scores, axis=0, keepdims=True))
    probs = powers * (1.0 / jnp.sum(powers, axis=0, keepdims=True))
    prob_grad = dot_nt(value, grad)
    row_delta = jnp.sum(probs * prob_grad, axis=0, keepdims=True)
    score_grad = (probs * (prob_grad - row_delta)).astype(jnp.bfloat16)
    results = (
        dot_tn(score_grad, key) * scale,
        dot_nn(score_grad, query) * scale,
        dot_nn(probs.astype(jnp.bfloat16), grad),
    )
    for row, result in enumerate(results):
        result = result.astype(jnp.bfloat16)
        for place, out in enumerate(outs):
            out[row] = result[place * bins : (place + 1) * bins]


def heads_back(blocks):
    groups = len(blocks)
    bins, width = blocks[0].shape[1:]
    rows = bins * groups
    heads = width // HD
    return pl.pallas_call(
        heads_kernel,
        grid=(heads,),
        out_shape=[jax.ShapeDtypeStruct((3, bins, width), jnp.bfloat16)] * groups,
        in_specs=[pl.BlockSpec((4, bins, HD), lambda h: (0, 0, h))] * groups,
        out_specs=[pl.BlockSpec((3, bins, HD), lambda h: (0, 0, h))] * groups,
        compiler_params=pltpu.CompilerParams(vmem_limit_bytes=6 * 1024 * 1024 + 40 * rows * rows),
        cost_estimate=cost(HEADS_COST),
        name="heads_back",
    )(*blocks)


def exchange(blocks):
    groups = len(blocks)
    return [blocks[0]] + [
        lax.ppermute(blocks[place], "ctx", [(i, i ^ place) for i in range(groups)])
        for place in range(1, groups)
    ]


def make_block(tokens, grads, routes, gates):
    rest = gates.T
    pieces = [(routes.T + 1).astype(jnp.float32)]
    for _ in range(3):
        piece = lax.reduce_precision(rest, 8, 7)
        rest = rest - piece
        pieces.append(piece)
    notes = jnp.concatenate(pieces, axis=0).astype(jnp.bfloat16)
    notes = jnp.pad(notes, ((0, NOTES - notes.shape[0]), (0, tokens.shape[1] - notes.shape[1])))
    return jnp.concatenate([tokens, notes, grads], axis=0)


def pick_slots(notes, base, top, experts, pick_ref):
    bins = notes[0].shape[1]
    slots = len(notes) * CAP
    earlier = lax.broadcasted_iota(jnp.int32, (bins, bins), 0)
    later = lax.broadcasted_iota(jnp.int32, (bins, bins), 1)
    before = (earlier < later).astype(jnp.bfloat16)
    slot = lax.broadcasted_iota(jnp.int32, (slots, bins), 0).astype(jnp.float32)
    gates = [jnp.zeros((slots, 1), jnp.float32)] * experts
    for source, note in enumerate(notes):
        note = note.astype(jnp.float32)
        named = note[:top] - base
        weights = note[top : 2 * top] + note[2 * top : 3 * top] + note[3 * top : 4 * top]
        hits = [(named == float(local + 1)).astype(jnp.float32) for local in range(experts)]
        chosen = [jnp.sum(hit, axis=0, keepdims=True) for hit in hits]
        stacked = jnp.concatenate(chosen, axis=0)
        position = dot_nn(stacked.astype(jnp.bfloat16), before)
        for local in range(experts):
            place = jnp.where(
                chosen[local] > 0.0, position[local : local + 1] + float(source * CAP), -1.0
            )
            pick = (slot == place).astype(jnp.float32)
            gate = jnp.sum(hits[local] * weights, axis=0, keepdims=True)
            gates[local] = gates[local] + jnp.sum(pick * gate, axis=1, keepdims=True)
            pick_ref[
                local * slots : (local + 1) * slots, source * bins : (source + 1) * bins
            ] = pick.astype(jnp.bfloat16)
    return jnp.concatenate(gates, axis=0)


def expert_kernel(layout, ahead, later, loads, pieces, top, base_ref, *refs):
    refs = list(refs)

    def take(count):
        taken = refs[:count]
        del refs[:count]
        return taken

    sources = len(layout)
    blocks = [take(length) for length in layout]
    ahead_refs = take(ahead)
    slope_refs = take(1 if later else 0)
    weights = take(2)
    (keep_ref,) = take(1)
    give_refs = take(pieces)
    ahead_slopes = take(1 if ahead else 0)
    up_ref, down_ref = take(2) if loads else weights
    pick_ref, token_rows, gated_rows, back_rows = take(4)
    ahead_picks = take(1 if ahead else 0)
    sems = take(1)[0] if loads else None
    bins = keep_ref.shape[0]
    slots = sources * CAP
    experts = pick_ref.shape[0] // slots
    wide = slots + ahead * CAP

    def copies(expert):
        parts = []
        for which, (hbm, vmem) in enumerate(zip(weights, (up_ref, down_ref))):
            length = hbm.shape[1] // PARTS
            for part in range(PARTS):
                rows = (expert, pl.ds(part * length, length))
                sem = sems.at[expert, PARTS * which + part]
                parts.append(pltpu.make_async_copy(hbm.at[rows], vmem.at[rows], sem))
        return parts

    if loads:
        for local in range(experts):
            for copy in copies(local):
                copy.start()

    values = [
        jnp.concatenate([piece[...] for piece in block], axis=0) if len(block) > 1 else block[0]
        for block in blocks
    ]
    base = base_ref[0].astype(jnp.float32)
    notes = [value[bins : bins + NOTES, :bins] for value in values]
    gate_column = pick_slots(notes, base, top, experts, pick_ref)
    grads = jnp.concatenate([value[bins + NOTES :] for value in values], axis=0)
    gated_rows[...] = (gate_column * dot_nn(pick_ref[...], grads)).astype(jnp.bfloat16)
    if not later:
        tokens = jnp.concatenate([value[:bins] for value in values], axis=0)
        picked = dot_nn(pick_ref[...], tokens).astype(jnp.bfloat16)
        for local in range(experts):
            token_rows[local * wide : local * wide + slots] = picked[
                local * slots : (local + 1) * slots
            ]
    if ahead:
        notes = [ref[bins : bins + NOTES, :bins] for ref in ahead_refs]
        pick_slots(notes, base, top, experts, ahead_picks[0])
        tokens = jnp.concatenate([ref[:bins] for ref in ahead_refs], axis=0)
        picked = dot_nn(ahead_picks[0][...], tokens).astype(jnp.bfloat16)
        more = ahead * CAP
        for local in range(experts):
            token_rows[local * wide + slots : (local + 1) * wide] = picked[
                local * more : (local + 1) * more
            ]

    @pl.loop(0, experts)
    def _(expert):
        if loads:
            for copy in copies(expert):
                copy.wait()
        rows = pl.ds(pl.multiple_of(expert * slots, 16), slots)
        if later:
            slopes = slope_refs[0][rows, :]
        else:
            wide_rows = pl.ds(pl.multiple_of(expert * wide, 16), wide)
            slopes = silu_slope(dot_nn(token_rows[wide_rows, :], up_ref[expert]))
        if ahead:
            more = ahead * CAP
            ahead_slopes[0][pl.ds(pl.multiple_of(expert * more, 16), more), :] = slopes[slots:]
            slopes = slopes[:slots]
        back_grad = dot_nt(gated_rows[rows, :], down_ref[expert])
        hidden_grad = (back_grad * slopes).astype(jnp.bfloat16)
        back_rows[rows, :] = dot_nt(hidden_grad, up_ref[expert]).astype(jnp.bfloat16)

    sums = dot_tn(pick_ref[...], back_rows[...])
    keep_ref[...] = sums[:bins].astype(jnp.bfloat16)
    rows = bins // pieces
    for piece, give_ref in enumerate(give_refs):
        give_ref[...] = sums[bins + piece * rows : bins + (piece + 1) * rows].astype(jnp.bfloat16)


def expert_back(base, blocks, weights, loads, bins, top, units, pieces, ahead, slopes):
    layout = [len(block) for block in blocks]
    later = slopes is not None
    experts, width, hidden = weights[0].shape
    slots = len(blocks) * CAP
    wide = slots + len(ahead) * CAP
    operands = [piece for block in blocks for piece in block] + list(ahead)
    operands += [slopes] if later else []
    more = [jax.ShapeDtypeStruct((experts * len(ahead) * CAP, hidden), jnp.float32)]
    out_shape = (
        [jax.ShapeDtypeStruct((bins, width), jnp.bfloat16)]
        + [jax.ShapeDtypeStruct((bins // pieces, width), jnp.bfloat16)] * pieces
        + (more if ahead else [])
        + ([jax.ShapeDtypeStruct(weight.shape, weight.dtype) for weight in weights] if loads else [])
    )
    return pl.pallas_call(
        functools.partial(expert_kernel, layout, len(ahead), later, loads, pieces, top),
        out_shape=out_shape,
        in_specs=[pl.BlockSpec(memory_space=pltpu.SMEM)]
        + [pl.BlockSpec(memory_space=pltpu.VMEM)] * len(operands)
        + [pl.BlockSpec(memory_space=pltpu.HBM if loads else pltpu.VMEM)] * 2,
        out_specs=[pl.BlockSpec(memory_space=pltpu.VMEM)] * len(out_shape),
        scratch_shapes=[
            pltpu.VMEM((experts * slots, len(blocks) * bins), jnp.bfloat16),
            pltpu.VMEM((16 if later else experts * wide, width), jnp.bfloat16),
            pltpu.VMEM((experts * slots, width), jnp.bfloat16),
            pltpu.VMEM((experts * slots, width), jnp.bfloat16),
        ]
        + [pltpu.VMEM((experts * len(ahead) * CAP, len(ahead) * bins), jnp.bfloat16)]
        * (1 if ahead else 0)
        + [pltpu.SemaphoreType.DMA((experts, 2 * PARTS))] * (1 if loads else 0),
        compiler_params=pltpu.CompilerParams(vmem_limit_bytes=VMEM_EXPERTS),
        cost_estimate=cost(units),
        name="expert_back",
    )(base, *operands, *weights)


def per_device(
    queries, key_rows, value_rows, out_grad, moe_input, routes, route_gates, up_weight, down_weight
):
    members = lax.axis_size("exp")
    me = lax.axis_index("exp")
    groups = lax.axis_size("ctx")
    chips = members // 2
    half = chips // 2
    _, bins, top = routes.shape
    base = (me * up_weight.shape[0]).astype(jnp.int32).reshape(1)

    def swap(block):
        return lax.ppermute(block, "exp", [(i, i ^ 1) for i in range(members)])

    def hop(block, step):
        return lax.ppermute(
            block, "exp", [(i, (i + 2 * step) % members) for i in range(members)]
        )

    def pair(*pieces):
        return [list(pieces), [swap(piece) for piece in pieces]]

    def work(blocks, weights, units, pieces=1, ahead=(), slopes=None, loads=False):
        kept, *rest = expert_back(
            base, blocks, weights, loads, bins, top, units, pieces, ahead, slopes
        )
        return kept, rest[:pieces], rest[pieces:]

    def add_up(*members):
        return functools.reduce(jnp.add, [member.astype(jnp.float32) for member in members])

    def joined(pieces):
        return pieces[0] if len(pieces) == 1 else jnp.concatenate(pieces, axis=0)

    barrier = lax.optimization_barrier
    own = make_block(moe_input[0], out_grad[0], routes[0], route_gates[0])
    left, right_rows = hop(own, -1), hop(own[: bins + NOTES], 1)
    own_pair = pair(own)
    mine = lax.axis_index("ctx").astype(jnp.int32).reshape(1)
    rows = (queries[0], key_rows[0], value_rows[0], out_grad[0])
    packed = pack_groups(mine, rows, groups)
    own_pair, packed = barrier((own_pair, packed))
    heads = exchange(packed)
    kept, give, weights = work(own_pair, (up_weight, down_weight), OWN_COST, loads=True)
    heads, kept, give, left = barrier((heads, kept, give, left))
    total = add_up(kept, joined([swap(piece) for piece in give]))
    left_pair, right_grads = pair(left), out_grad[0]
    results = heads_back(heads)
    left_pair, results, right_rows = barrier((left_pair, results, right_rows))
    results = exchange(results)
    right_partner = swap(right_rows)
    left_sums, slopes = [], None
    for d in range(1, half):
        left = hop(left, -1)
        ahead = () if d > 1 else (right_rows, right_partner)
        kept, give, more = work(left_pair, weights, LEFT_COST, ahead=ahead)
        slopes = more[0] if d == 1 else slopes
        left, results, kept, give = barrier((left, results, kept, give))
        left_sums.append(add_up(kept, joined([swap(piece) for piece in give])))
        left_pair = pair(left)
    carried = left_sums[-1].astype(jnp.bfloat16)
    for sums in reversed(left_sums[:-1]):
        carried = add_up(sums, hop(carried, 1)).astype(jnp.bfloat16)
    left_halves = [hop(carried[: bins // 2], 1), hop(carried[bins // 2 :], 1)]
    rights = [(right_rows, hop(right_grads, 1))]
    for d in range(2, half):
        rights.append(tuple(hop(member, 1) for member in rights[-1]))
    kept, give, _ = work(left_pair, weights, FAR_COST)
    left_halves[0], rights, kept, give = barrier((left_halves[0], rights, kept, give))
    carried = add_up(kept, joined([swap(piece) for piece in give]))
    for d in range(half - 1, 0, -1):
        cut = bins - bins // 4
        carried = carried.astype(jnp.bfloat16)
        most, last = hop(carried[:cut], -1), hop(carried[cut:], -1)
        right_pair = pair(*rights[d - 1])
        if d == 1:
            right_pair[1][0] = right_partner
        kept, give, _ = work(
            right_pair, weights, RIGHT_COST, 4, slopes=slopes if d == 1 else None
        )
        kept, give, left_halves = barrier((kept, give, left_halves))
        given = [swap(piece) for piece in give]
        sums = [add_up(kept[:cut], joined(given[:3]), most), add_up(kept[cut:], given[3], last)]
        carried = jnp.concatenate(sums, axis=0)
    total = add_up(total, joined(left_halves))
    returned = [hop(part.astype(jnp.bfloat16), -1) for part in sums]
    outs = unpack_groups(mine, results)
    total = add_up(total, joined(returned)).astype(jnp.bfloat16)
    return tuple(out[None] for out in outs) + (total[None],)


def solution(mesh):
    rows = P("exp", "ctx", None)
    experts = P("exp", None, None)
    return jax.shard_map(
        per_device,
        mesh=mesh,
        in_specs=(rows,) * 7 + (experts,) * 2,
        out_specs=(rows,) * 4,
        check_vma=False,
    )
```

```python
import functools

import jax
import jax.numpy as jnp
from jax import lax
from jax.experimental import pallas as pl
from jax.experimental.pallas import tpu as pltpu
from jax.sharding import PartitionSpec as P

HD = 128
CAP = 24
NOTES = 16
PARTS = 4
VMEM_BYTES = 36 * 1024 * 1024
VMEM_PACK = 58 * 1024 * 1024
VMEM_EXPERTS = 18 * 1024 * 1024
def cost(units):
    return pl.CostEstimate(
        flops=units * 10**9, bytes_accessed=units * 10**6, transcendentals=0
    )


SMALL = cost(0)
OWN_COST, HEADS_COST, LEFT_COST, FAR_COST, RIGHT_COST = 30, 30, 0, 0, 30
NT = (((1,), (1,)), ((), ()))
TN = (((0,), (0,)), ((), ()))


def dot_nt(left, right):
    return lax.dot_general(left, right, NT, preferred_element_type=jnp.float32)


def dot_tn(left, right):
    return lax.dot_general(left, right, TN, preferred_element_type=jnp.float32)


def dot_nn(left, right):
    return jnp.dot(left, right, preferred_element_type=jnp.float32)


def silu_slope(preact):
    sigmoid = jax.nn.sigmoid(preact)
    return sigmoid * (1.0 + preact * (1.0 - sigmoid))


def pack_kernel(mine_ref, *refs):
    members, blocks = refs[:4], refs[4:]
    width = blocks[0].shape[2]
    for place, block in enumerate(blocks):
        first = pl.multiple_of((mine_ref[0] ^ place) * width, 128)
        for row, member in enumerate(members):
            block[row] = member[:, pl.ds(first, width)]


def pack_groups(mine, members, groups):
    bins, width = members[0].shape
    block = jax.ShapeDtypeStruct((4, bins, width // groups), jnp.bfloat16)
    return pl.pallas_call(
        pack_kernel,
        out_shape=[block] * groups,
        in_specs=[pl.BlockSpec(memory_space=pltpu.SMEM)]
        + [pl.BlockSpec(memory_space=pltpu.VMEM)] * 4,
        out_specs=[pl.BlockSpec(memory_space=pltpu.VMEM)] * groups,
        compiler_params=pltpu.CompilerParams(vmem_limit_bytes=VMEM_PACK),
        cost_estimate=SMALL,
        name="pack_groups",
    )(mine, *members)


def unpack_kernel(mine_ref, *refs):
    blocks, outs = refs[:-3], refs[-3:]
    width = blocks[0].shape[2]
    for place, block in enumerate(blocks):
        first = pl.multiple_of((mine_ref[0] ^ place) * width, 128)
        for row, out in enumerate(outs):
            out[:, pl.ds(first, width)] = block[row]


def unpack_groups(mine, blocks):
    groups = len(blocks)
    bins, width = blocks[0].shape[1], blocks[0].shape[2] * groups
    out = jax.ShapeDtypeStruct((bins, width), jnp.bfloat16)
    return pl.pallas_call(
        unpack_kernel,
        out_shape=[out] * 3,
        in_specs=[pl.BlockSpec(memory_space=pltpu.SMEM)]
        + [pl.BlockSpec(memory_space=pltpu.VMEM)] * groups,
        out_specs=[pl.BlockSpec(memory_space=pltpu.VMEM)] * 3,
        compiler_params=pltpu.CompilerParams(vmem_limit_bytes=VMEM_BYTES),
        cost_estimate=SMALL,
        name="unpack_groups",
    )(mine, *blocks)


def heads_kernel(*refs):
    count = len(refs) // 2
    blocks, outs = refs[:count], refs[count:]
    bins = blocks[0].shape[1]
    scale = HD ** (-0.5)
    query, key, value, grad = (
        jnp.concatenate([block[row] for block in blocks], axis=0) for row in range(4)
    )
    scores = dot_nt(key, query) * scale
    powers = jnp.exp(scores - jnp.max(scores, axis=0, keepdims=True))
    probs = powers * (1.0 / jnp.sum(powers, axis=0, keepdims=True))
    prob_grad = dot_nt(value, grad)
    row_delta = jnp.sum(probs * prob_grad, axis=0, keepdims=True)
    score_grad = (probs * (prob_grad - row_delta)).astype(jnp.bfloat16)
    results = (
        dot_tn(score_grad, key) * scale,
        dot_nn(score_grad, query) * scale,
        dot_nn(probs.astype(jnp.bfloat16), grad),
    )
    for row, result in enumerate(results):
        result = result.astype(jnp.bfloat16)
        for place, out in enumerate(outs):
            out[row] = result[place * bins : (place + 1) * bins]


def heads_back(blocks):
    groups = len(blocks)
    bins, width = blocks[0].shape[1:]
    rows = bins * groups
    heads = width // HD
    return pl.pallas_call(
        heads_kernel,
        grid=(heads,),
        out_shape=[jax.ShapeDtypeStruct((3, bins, width), jnp.bfloat16)] * groups,
        in_specs=[pl.BlockSpec((4, bins, HD), lambda h: (0, 0, h))] * groups,
        out_specs=[pl.BlockSpec((3, bins, HD), lambda h: (0, 0, h))] * groups,
        compiler_params=pltpu.CompilerParams(vmem_limit_bytes=6 * 1024 * 1024 + 40 * rows * rows),
        cost_estimate=cost(HEADS_COST),
        name="heads_back",
    )(*blocks)


def exchange(blocks):
    groups = len(blocks)
    return [blocks[0]] + [
        lax.ppermute(blocks[place], "ctx", [(i, i ^ place) for i in range(groups)])
        for place in range(1, groups)
    ]


def make_block(tokens, grads, routes, gates):
    rest = gates.T
    pieces = [(routes.T + 1).astype(jnp.float32)]
    for _ in range(3):
        piece = lax.reduce_precision(rest, 8, 7)
        rest = rest - piece
        pieces.append(piece)
    notes = jnp.concatenate(pieces, axis=0).astype(jnp.bfloat16)
    notes = jnp.pad(notes, ((0, NOTES - notes.shape[0]), (0, tokens.shape[1] - notes.shape[1])))
    return jnp.concatenate([tokens, notes, grads], axis=0)


def pick_slots(notes, base, top, experts, pick_ref):
    bins = notes[0].shape[1]
    slots = len(notes) * CAP
    earlier = lax.broadcasted_iota(jnp.int32, (bins, bins), 0)
    later = lax.broadcasted_iota(jnp.int32, (bins, bins), 1)
    before = (earlier < later).astype(jnp.bfloat16)
    slot = lax.broadcasted_iota(jnp.int32, (slots, bins), 0).astype(jnp.float32)
    gates = [jnp.zeros((slots, 1), jnp.float32)] * experts
    for source, note in enumerate(notes):
        note = note.astype(jnp.float32)
        named = note[:top] - base
        weights = note[top : 2 * top] + note[2 * top : 3 * top] + note[3 * top : 4 * top]
        hits = [(named == float(local + 1)).astype(jnp.float32) for local in range(experts)]
        chosen = [jnp.sum(hit, axis=0, keepdims=True) for hit in hits]
        stacked = jnp.concatenate(chosen, axis=0)
        position = dot_nn(stacked.astype(jnp.bfloat16), before)
        for local in range(experts):
            place = jnp.where(
                chosen[local] > 0.0, position[local : local + 1] + float(source * CAP), -1.0
            )
            pick = (slot == place).astype(jnp.float32)
            gate = jnp.sum(hits[local] * weights, axis=0, keepdims=True)
            gates[local] = gates[local] + jnp.sum(pick * gate, axis=1, keepdims=True)
            pick_ref[
                local * slots : (local + 1) * slots, source * bins : (source + 1) * bins
            ] = pick.astype(jnp.bfloat16)
    return jnp.concatenate(gates, axis=0)


def expert_kernel(layout, ahead, later, loads, pieces, top, base_ref, *refs):
    refs = list(refs)

    def take(count):
        taken = refs[:count]
        del refs[:count]
        return taken

    sources = len(layout)
    blocks = [take(length) for length in layout]
    ahead_refs = take(ahead)
    slope_refs = take(1 if later else 0)
    weights = take(2)
    (keep_ref,) = take(1)
    give_refs = take(pieces)
    ahead_slopes = take(1 if ahead else 0)
    up_ref, down_ref = take(2) if loads else weights
    pick_ref, token_rows, gated_rows, back_rows = take(4)
    ahead_picks = take(1 if ahead else 0)
    sems = take(1)[0] if loads else None
    bins = keep_ref.shape[0]
    slots = sources * CAP
    experts = pick_ref.shape[0] // slots
    wide = slots + ahead * CAP

    def copies(expert):
        parts = []
        for which, (hbm, vmem) in enumerate(zip(weights, (up_ref, down_ref))):
            length = hbm.shape[1] // PARTS
            for part in range(PARTS):
                rows = (expert, pl.ds(part * length, length))
                sem = sems.at[expert, PARTS * which + part]
                parts.append(pltpu.make_async_copy(hbm.at[rows], vmem.at[rows], sem))
        return parts

    if loads:
        for local in range(experts):
            for copy in copies(local):
                copy.start()

    values = [
        jnp.concatenate([piece[...] for piece in block], axis=0) if len(block) > 1 else block[0]
        for block in blocks
    ]
    base = base_ref[0].astype(jnp.float32)
    notes = [value[bins : bins + NOTES, :bins] for value in values]
    gate_column = pick_slots(notes, base, top, experts, pick_ref)
    grads = jnp.concatenate([value[bins + NOTES :] for value in values], axis=0)
    gated_rows[...] = (gate_column * dot_nn(pick_ref[...], grads)).astype(jnp.bfloat16)
    if not later:
        tokens = jnp.concatenate([value[:bins] for value in values], axis=0)
        picked = dot_nn(pick_ref[...], tokens).astype(jnp.bfloat16)
        for local in range(experts):
            token_rows[local * wide : local * wide + slots] = picked[
                local * slots : (local + 1) * slots
            ]
    if ahead:
        notes = [ref[bins : bins + NOTES, :bins] for ref in ahead_refs]
        pick_slots(notes, base, top, experts, ahead_picks[0])
        tokens = jnp.concatenate([ref[:bins] for ref in ahead_refs], axis=0)
        picked = dot_nn(ahead_picks[0][...], tokens).astype(jnp.bfloat16)
        more = ahead * CAP
        for local in range(experts):
            token_rows[local * wide + slots : (local + 1) * wide] = picked[
                local * more : (local + 1) * more
            ]

    @pl.loop(0, experts)
    def _(expert):
        if loads:
            for copy in copies(expert):
                copy.wait()
        rows = pl.ds(pl.multiple_of(expert * slots, 16), slots)
        if later:
            slopes = slope_refs[0][rows, :]
        else:
            wide_rows = pl.ds(pl.multiple_of(expert * wide, 16), wide)
            slopes = silu_slope(dot_nn(token_rows[wide_rows, :], up_ref[expert]))
        if ahead:
            more = ahead * CAP
            ahead_slopes[0][pl.ds(pl.multiple_of(expert * more, 16), more), :] = slopes[slots:]
            slopes = slopes[:slots]
        back_grad = dot_nt(gated_rows[rows, :], down_ref[expert])
        hidden_grad = (back_grad * slopes).astype(jnp.bfloat16)
        back_rows[rows, :] = dot_nt(hidden_grad, up_ref[expert]).astype(jnp.bfloat16)

    sums = dot_tn(pick_ref[...], back_rows[...])
    keep_ref[...] = sums[:bins].astype(jnp.bfloat16)
    rows = bins // pieces
    for piece, give_ref in enumerate(give_refs):
        give_ref[...] = sums[bins + piece * rows : bins + (piece + 1) * rows].astype(jnp.bfloat16)


def expert_back(base, blocks, weights, loads, bins, top, units, pieces, ahead, slopes):
    layout = [len(block) for block in blocks]
    later = slopes is not None
    experts, width, hidden = weights[0].shape
    slots = len(blocks) * CAP
    wide = slots + len(ahead) * CAP
    operands = [piece for block in blocks for piece in block] + list(ahead)
    operands += [slopes] if later else []
    more = [jax.ShapeDtypeStruct((experts * len(ahead) * CAP, hidden), jnp.float32)]
    out_shape = (
        [jax.ShapeDtypeStruct((bins, width), jnp.bfloat16)]
        + [jax.ShapeDtypeStruct((bins // pieces, width), jnp.bfloat16)] * pieces
        + (more if ahead else [])
        + ([jax.ShapeDtypeStruct(weight.shape, weight.dtype) for weight in weights] if loads else [])
    )
    return pl.pallas_call(
        functools.partial(expert_kernel, layout, len(ahead), later, loads, pieces, top),
        out_shape=out_shape,
        in_specs=[pl.BlockSpec(memory_space=pltpu.SMEM)]
        + [pl.BlockSpec(memory_space=pltpu.VMEM)] * len(operands)
        + [pl.BlockSpec(memory_space=pltpu.HBM if loads else pltpu.VMEM)] * 2,
        out_specs=[pl.BlockSpec(memory_space=pltpu.VMEM)] * len(out_shape),
        scratch_shapes=[
            pltpu.VMEM((experts * slots, len(blocks) * bins), jnp.bfloat16),
            pltpu.VMEM((16 if later else experts * wide, width), jnp.bfloat16),
            pltpu.VMEM((experts * slots, width), jnp.bfloat16),
            pltpu.VMEM((experts * slots, width), jnp.bfloat16),
        ]
        + [pltpu.VMEM((experts * len(ahead) * CAP, len(ahead) * bins), jnp.bfloat16)]
        * (1 if ahead else 0)
        + [pltpu.SemaphoreType.DMA((experts, 2 * PARTS))] * (1 if loads else 0),
        compiler_params=pltpu.CompilerParams(vmem_limit_bytes=VMEM_EXPERTS),
        cost_estimate=cost(units),
        name="expert_back",
    )(base, *operands, *weights)


def per_device(
    queries, key_rows, value_rows, out_grad, moe_input, routes, route_gates, up_weight, down_weight
):
    members = lax.axis_size("exp")
    me = lax.axis_index("exp")
    groups = lax.axis_size("ctx")
    chips = members // 2
    half = chips // 2
    _, bins, top = routes.shape
    base = (me * up_weight.shape[0]).astype(jnp.int32).reshape(1)

    def swap(block):
        return lax.ppermute(block, "exp", [(i, i ^ 1) for i in range(members)])

    def hop(block, step):
        return lax.ppermute(
            block, "exp", [(i, (i + 2 * step) % members) for i in range(members)]
        )

    def pair(*pieces):
        return [list(pieces), [swap(piece) for piece in pieces]]

    def work(blocks, weights, units, pieces=1, ahead=(), slopes=None, loads=False):
        kept, *rest = expert_back(
            base, blocks, weights, loads, bins, top, units, pieces, ahead, slopes
        )
        return kept, rest[:pieces], rest[pieces:]

    def add_up(*members):
        return functools.reduce(jnp.add, [member.astype(jnp.float32) for member in members])

    def joined(pieces):
        return pieces[0] if len(pieces) == 1 else jnp.concatenate(pieces, axis=0)

    barrier = lax.optimization_barrier
    own = make_block(moe_input[0], out_grad[0], routes[0], route_gates[0])
    left, right_rows = hop(own, -1), hop(own[: bins + NOTES], 1)
    own_pair = pair(own)
    mine = lax.axis_index("ctx").astype(jnp.int32).reshape(1)
    rows = (queries[0], key_rows[0], value_rows[0], out_grad[0])
    packed = pack_groups(mine, rows, groups)
    own_pair, packed = barrier((own_pair, packed))
    heads = exchange(packed)
    kept, give, weights = work(own_pair, (up_weight, down_weight), OWN_COST, loads=True)
    heads, kept, give, left = barrier((heads, kept, give, left))
    total = add_up(kept, joined([swap(piece) for piece in give]))
    left_pair, right_grads = pair(left), out_grad[0]
    results = heads_back(heads)
    left_pair, results, right_rows = barrier((left_pair, results, right_rows))
    results = exchange(results)
    right_partner = swap(right_rows)
    left_sums, slopes = [], None
    for d in range(1, half):
        left = hop(left, -1)
        ahead = () if d > 1 else (right_rows, right_partner)
        kept, give, more = work(left_pair, weights, LEFT_COST, ahead=ahead)
        slopes = more[0] if d == 1 else slopes
        left, results, kept, give = barrier((left, results, kept, give))
        left_sums.append(add_up(kept, joined([swap(piece) for piece in give])))
        left_pair = pair(left)
    carried = left_sums[-1].astype(jnp.bfloat16)
    for sums in reversed(left_sums[:-1]):
        carried = add_up(sums, hop(carried, 1)).astype(jnp.bfloat16)
    left_halves = [hop(carried[: bins // 4], 1), hop(carried[bins // 4 :], 1)]
    rights = [(right_rows, hop(right_grads, 1))]
    for d in range(2, half):
        rights.append(tuple(hop(member, 1) for member in rights[-1]))
    kept, give, _ = work(left_pair, weights, FAR_COST)
    left_halves[0], rights, kept, give = barrier((left_halves[0], rights, kept, give))
    carried = add_up(kept, joined([swap(piece) for piece in give]))
    for d in range(half - 1, 0, -1):
        cut = bins - bins // 4
        carried = carried.astype(jnp.bfloat16)
        most, last = hop(carried[:cut], -1), hop(carried[cut:], -1)
        right_pair = pair(*rights[d - 1])
        if d == 1:
            right_pair[1][0] = right_partner
        kept, give, _ = work(
            right_pair, weights, RIGHT_COST, 4, slopes=slopes if d == 1 else None
        )
        kept, give, left_halves = barrier((kept, give, left_halves))
        given = [swap(piece) for piece in give]
        sums = [add_up(kept[:cut], joined(given[:3]), most), add_up(kept[cut:], given[3], last)]
        carried = jnp.concatenate(sums, axis=0)
    total = add_up(total, joined(left_halves))
    returned = [hop(part.astype(jnp.bfloat16), -1) for part in sums]
    outs = unpack_groups(mine, results)
    total = add_up(total, joined(returned)).astype(jnp.bfloat16)
    return tuple(out[None] for out in outs) + (total[None],)


def solution(mesh):
    rows = P("exp", "ctx", None)
    experts = P("exp", None, None)
    return jax.shard_map(
        per_device,
        mesh=mesh,
        in_specs=(rows,) * 7 + (experts,) * 2,
        out_specs=(rows,) * 4,
        check_vma=False,
    )
```

```python
import functools

import jax
import jax.numpy as jnp
from jax import lax
from jax.experimental import pallas as pl
from jax.experimental.pallas import tpu as pltpu
from jax.sharding import PartitionSpec as P

HD = 128
CAP = 24
NOTES = 16
PARTS = 4
VMEM_BYTES = 36 * 1024 * 1024
VMEM_PACK = 58 * 1024 * 1024
VMEM_EXPERTS = 18 * 1024 * 1024
def cost(units):
    return pl.CostEstimate(
        flops=units * 10**9, bytes_accessed=units * 10**6, transcendentals=0
    )


SMALL = cost(0)
OWN_COST, HEADS_COST, LEFT_COST, FAR_COST, RIGHT_COST = 30, 30, 0, 0, 30
NT = (((1,), (1,)), ((), ()))
TN = (((0,), (0,)), ((), ()))


def dot_nt(left, right):
    return lax.dot_general(left, right, NT, preferred_element_type=jnp.float32)


def dot_tn(left, right):
    return lax.dot_general(left, right, TN, preferred_element_type=jnp.float32)


def dot_nn(left, right):
    return jnp.dot(left, right, preferred_element_type=jnp.float32)


def silu_slope(preact):
    sigmoid = jax.nn.sigmoid(preact)
    return sigmoid * (1.0 + preact * (1.0 - sigmoid))


def pack_kernel(mine_ref, *refs):
    members, blocks = refs[:4], refs[4:]
    width = blocks[0].shape[2]
    for place, block in enumerate(blocks):
        first = pl.multiple_of((mine_ref[0] ^ place) * width, 128)
        for row, member in enumerate(members):
            block[row] = member[:, pl.ds(first, width)]


def pack_groups(mine, members, groups):
    bins, width = members[0].shape
    block = jax.ShapeDtypeStruct((4, bins, width // groups), jnp.bfloat16)
    return pl.pallas_call(
        pack_kernel,
        out_shape=[block] * groups,
        in_specs=[pl.BlockSpec(memory_space=pltpu.SMEM)]
        + [pl.BlockSpec(memory_space=pltpu.VMEM)] * 4,
        out_specs=[pl.BlockSpec(memory_space=pltpu.VMEM)] * groups,
        compiler_params=pltpu.CompilerParams(vmem_limit_bytes=VMEM_PACK),
        cost_estimate=SMALL,
        name="pack_groups",
    )(mine, *members)


def unpack_kernel(mine_ref, *refs):
    blocks, outs = refs[:-3], refs[-3:]
    width = blocks[0].shape[2]
    for place, block in enumerate(blocks):
        first = pl.multiple_of((mine_ref[0] ^ place) * width, 128)
        for row, out in enumerate(outs):
            out[:, pl.ds(first, width)] = block[row]


def unpack_groups(mine, blocks):
    groups = len(blocks)
    bins, width = blocks[0].shape[1], blocks[0].shape[2] * groups
    out = jax.ShapeDtypeStruct((bins, width), jnp.bfloat16)
    return pl.pallas_call(
        unpack_kernel,
        out_shape=[out] * 3,
        in_specs=[pl.BlockSpec(memory_space=pltpu.SMEM)]
        + [pl.BlockSpec(memory_space=pltpu.VMEM)] * groups,
        out_specs=[pl.BlockSpec(memory_space=pltpu.VMEM)] * 3,
        compiler_params=pltpu.CompilerParams(vmem_limit_bytes=VMEM_BYTES),
        cost_estimate=SMALL,
        name="unpack_groups",
    )(mine, *blocks)


def heads_kernel(*refs):
    count = len(refs) // 2
    blocks, outs = refs[:count], refs[count:]
    bins = blocks[0].shape[1]
    scale = HD ** (-0.5)
    query, key, value, grad = (
        jnp.concatenate([block[row] for block in blocks], axis=0) for row in range(4)
    )
    scores = dot_nt(key, query) * scale
    powers = jnp.exp(scores - jnp.max(scores, axis=0, keepdims=True))
    probs = powers * (1.0 / jnp.sum(powers, axis=0, keepdims=True))
    prob_grad = dot_nt(value, grad)
    row_delta = jnp.sum(probs * prob_grad, axis=0, keepdims=True)
    score_grad = (probs * (prob_grad - row_delta)).astype(jnp.bfloat16)
    results = (
        dot_tn(score_grad, key) * scale,
        dot_nn(score_grad, query) * scale,
        dot_nn(probs.astype(jnp.bfloat16), grad),
    )
    for row, result in enumerate(results):
        result = result.astype(jnp.bfloat16)
        for place, out in enumerate(outs):
            out[row] = result[place * bins : (place + 1) * bins]


def heads_back(blocks):
    groups = len(blocks)
    bins, width = blocks[0].shape[1:]
    rows = bins * groups
    heads = width // HD
    return pl.pallas_call(
        heads_kernel,
        grid=(heads,),
        out_shape=[jax.ShapeDtypeStruct((3, bins, width), jnp.bfloat16)] * groups,
        in_specs=[pl.BlockSpec((4, bins, HD), lambda h: (0, 0, h))] * groups,
        out_specs=[pl.BlockSpec((3, bins, HD), lambda h: (0, 0, h))] * groups,
        compiler_params=pltpu.CompilerParams(vmem_limit_bytes=6 * 1024 * 1024 + 40 * rows * rows),
        cost_estimate=cost(HEADS_COST),
        name="heads_back",
    )(*blocks)


def exchange(blocks):
    groups = len(blocks)
    return [blocks[0]] + [
        lax.ppermute(blocks[place], "ctx", [(i, i ^ place) for i in range(groups)])
        for place in range(1, groups)
    ]


def make_block(tokens, grads, routes, gates):
    rest = gates.T
    pieces = [(routes.T + 1).astype(jnp.float32)]
    for _ in range(3):
        piece = lax.reduce_precision(rest, 8, 7)
        rest = rest - piece
        pieces.append(piece)
    notes = jnp.concatenate(pieces, axis=0).astype(jnp.bfloat16)
    notes = jnp.pad(notes, ((0, NOTES - notes.shape[0]), (0, tokens.shape[1] - notes.shape[1])))
    return jnp.concatenate([tokens, notes, grads], axis=0)


def pick_slots(notes, base, top, experts, pick_ref):
    bins = notes[0].shape[1]
    slots = len(notes) * CAP
    earlier = lax.broadcasted_iota(jnp.int32, (bins, bins), 0)
    later = lax.broadcasted_iota(jnp.int32, (bins, bins), 1)
    before = (earlier < later).astype(jnp.bfloat16)
    slot = lax.broadcasted_iota(jnp.int32, (slots, bins), 0).astype(jnp.float32)
    gates = [jnp.zeros((slots, 1), jnp.float32)] * experts
    for source, note in enumerate(notes):
        note = note.astype(jnp.float32)
        named = note[:top] - base
        weights = note[top : 2 * top] + note[2 * top : 3 * top] + note[3 * top : 4 * top]
        hits = [(named == float(local + 1)).astype(jnp.float32) for local in range(experts)]
        chosen = [jnp.sum(hit, axis=0, keepdims=True) for hit in hits]
        stacked = jnp.concatenate(chosen, axis=0)
        position = dot_nn(stacked.astype(jnp.bfloat16), before)
        for local in range(experts):
            place = jnp.where(
                chosen[local] > 0.0, position[local : local + 1] + float(source * CAP), -1.0
            )
            pick = (slot == place).astype(jnp.float32)
            gate = jnp.sum(hits[local] * weights, axis=0, keepdims=True)
            gates[local] = gates[local] + jnp.sum(pick * gate, axis=1, keepdims=True)
            pick_ref[
                local * slots : (local + 1) * slots, source * bins : (source + 1) * bins
            ] = pick.astype(jnp.bfloat16)
    return jnp.concatenate(gates, axis=0)


def expert_kernel(layout, ahead, later, loads, pieces, top, base_ref, *refs):
    refs = list(refs)

    def take(count):
        taken = refs[:count]
        del refs[:count]
        return taken

    sources = len(layout)
    blocks = [take(length) for length in layout]
    ahead_refs = take(ahead)
    slope_refs = take(1 if later else 0)
    weights = take(2)
    (keep_ref,) = take(1)
    give_refs = take(pieces)
    ahead_slopes = take(1 if ahead else 0)
    up_ref, down_ref = take(2) if loads else weights
    pick_ref, token_rows, gated_rows, back_rows = take(4)
    ahead_picks = take(1 if ahead else 0)
    sems = take(1)[0] if loads else None
    bins = keep_ref.shape[0]
    slots = sources * CAP
    experts = pick_ref.shape[0] // slots
    wide = slots + ahead * CAP

    def copies(expert):
        parts = []
        for which, (hbm, vmem) in enumerate(zip(weights, (up_ref, down_ref))):
            length = hbm.shape[1] // PARTS
            for part in range(PARTS):
                rows = (expert, pl.ds(part * length, length))
                sem = sems.at[expert, PARTS * which + part]
                parts.append(pltpu.make_async_copy(hbm.at[rows], vmem.at[rows], sem))
        return parts

    if loads:
        for local in range(experts):
            for copy in copies(local):
                copy.start()

    values = [
        jnp.concatenate([piece[...] for piece in block], axis=0) if len(block) > 1 else block[0]
        for block in blocks
    ]
    base = base_ref[0].astype(jnp.float32)
    notes = [value[bins : bins + NOTES, :bins] for value in values]
    gate_column = pick_slots(notes, base, top, experts, pick_ref)
    grads = jnp.concatenate([value[bins + NOTES :] for value in values], axis=0)
    gated_rows[...] = (gate_column * dot_nn(pick_ref[...], grads)).astype(jnp.bfloat16)
    if not later:
        tokens = jnp.concatenate([value[:bins] for value in values], axis=0)
        picked = dot_nn(pick_ref[...], tokens).astype(jnp.bfloat16)
        for local in range(experts):
            token_rows[local * wide : local * wide + slots] = picked[
                local * slots : (local + 1) * slots
            ]
    if ahead:
        notes = [ref[bins : bins + NOTES, :bins] for ref in ahead_refs]
        pick_slots(notes, base, top, experts, ahead_picks[0])
        tokens = jnp.concatenate([ref[:bins] for ref in ahead_refs], axis=0)
        picked = dot_nn(ahead_picks[0][...], tokens).astype(jnp.bfloat16)
        more = ahead * CAP
        for local in range(experts):
            token_rows[local * wide + slots : (local + 1) * wide] = picked[
                local * more : (local + 1) * more
            ]

    @pl.loop(0, experts)
    def _(expert):
        if loads:
            for copy in copies(expert):
                copy.wait()
        rows = pl.ds(pl.multiple_of(expert * slots, 16), slots)
        if later:
            slopes = slope_refs[0][rows, :]
        else:
            wide_rows = pl.ds(pl.multiple_of(expert * wide, 16), wide)
            slopes = silu_slope(dot_nn(token_rows[wide_rows, :], up_ref[expert]))
        if ahead:
            more = ahead * CAP
            ahead_slopes[0][pl.ds(pl.multiple_of(expert * more, 16), more), :] = slopes[slots:]
            slopes = slopes[:slots]
        back_grad = dot_nt(gated_rows[rows, :], down_ref[expert])
        hidden_grad = (back_grad * slopes).astype(jnp.bfloat16)
        back_rows[rows, :] = dot_nt(hidden_grad, up_ref[expert]).astype(jnp.bfloat16)

    sums = dot_tn(pick_ref[...], back_rows[...])
    keep_ref[...] = sums[:bins].astype(jnp.bfloat16)
    rows = bins // pieces
    for piece, give_ref in enumerate(give_refs):
        give_ref[...] = sums[bins + piece * rows : bins + (piece + 1) * rows].astype(jnp.bfloat16)


def expert_back(base, blocks, weights, loads, bins, top, units, pieces, ahead, slopes):
    layout = [len(block) for block in blocks]
    later = slopes is not None
    experts, width, hidden = weights[0].shape
    slots = len(blocks) * CAP
    wide = slots + len(ahead) * CAP
    operands = [piece for block in blocks for piece in block] + list(ahead)
    operands += [slopes] if later else []
    more = [jax.ShapeDtypeStruct((experts * len(ahead) * CAP, hidden), jnp.float32)]
    out_shape = (
        [jax.ShapeDtypeStruct((bins, width), jnp.bfloat16)]
        + [jax.ShapeDtypeStruct((bins // pieces, width), jnp.bfloat16)] * pieces
        + (more if ahead else [])
        + ([jax.ShapeDtypeStruct(weight.shape, weight.dtype) for weight in weights] if loads else [])
    )
    return pl.pallas_call(
        functools.partial(expert_kernel, layout, len(ahead), later, loads, pieces, top),
        out_shape=out_shape,
        in_specs=[pl.BlockSpec(memory_space=pltpu.SMEM)]
        + [pl.BlockSpec(memory_space=pltpu.VMEM)] * len(operands)
        + [pl.BlockSpec(memory_space=pltpu.HBM if loads else pltpu.VMEM)] * 2,
        out_specs=[pl.BlockSpec(memory_space=pltpu.VMEM)] * len(out_shape),
        scratch_shapes=[
            pltpu.VMEM((experts * slots, len(blocks) * bins), jnp.bfloat16),
            pltpu.VMEM((16 if later else experts * wide, width), jnp.bfloat16),
            pltpu.VMEM((experts * slots, width), jnp.bfloat16),
            pltpu.VMEM((experts * slots, width), jnp.bfloat16),
        ]
        + [pltpu.VMEM((experts * len(ahead) * CAP, len(ahead) * bins), jnp.bfloat16)]
        * (1 if ahead else 0)
        + [pltpu.SemaphoreType.DMA((experts, 2 * PARTS))] * (1 if loads else 0),
        compiler_params=pltpu.CompilerParams(vmem_limit_bytes=VMEM_EXPERTS),
        cost_estimate=cost(units),
        name="expert_back",
    )(base, *operands, *weights)


def per_device(
    queries, key_rows, value_rows, out_grad, moe_input, routes, route_gates, up_weight, down_weight
):
    members = lax.axis_size("exp")
    me = lax.axis_index("exp")
    groups = lax.axis_size("ctx")
    chips = members // 2
    half = chips // 2
    _, bins, top = routes.shape
    base = (me * up_weight.shape[0]).astype(jnp.int32).reshape(1)

    def swap(block):
        return lax.ppermute(block, "exp", [(i, i ^ 1) for i in range(members)])

    def hop(block, step):
        return lax.ppermute(
            block, "exp", [(i, (i + 2 * step) % members) for i in range(members)]
        )

    def pair(*pieces):
        return [list(pieces), [swap(piece) for piece in pieces]]

    def work(blocks, weights, units, pieces=1, ahead=(), slopes=None, loads=False):
        kept, *rest = expert_back(
            base, blocks, weights, loads, bins, top, units, pieces, ahead, slopes
        )
        return kept, rest[:pieces], rest[pieces:]

    def add_up(*members):
        return functools.reduce(jnp.add, [member.astype(jnp.float32) for member in members])

    def joined(pieces):
        return pieces[0] if len(pieces) == 1 else jnp.concatenate(pieces, axis=0)

    barrier = lax.optimization_barrier
    own = make_block(moe_input[0], out_grad[0], routes[0], route_gates[0])
    left, right_rows = hop(own, -1), hop(own[: bins + NOTES], 1)
    own_pair = pair(own)
    mine = lax.axis_index("ctx").astype(jnp.int32).reshape(1)
    rows = (queries[0], key_rows[0], value_rows[0], out_grad[0])
    packed = pack_groups(mine, rows, groups)
    own_pair, packed = barrier((own_pair, packed))
    heads = exchange(packed)
    kept, give, weights = work(own_pair, (up_weight, down_weight), OWN_COST, loads=True)
    heads, kept, give, left = barrier((heads, kept, give, left))
    total = add_up(kept, joined([swap(piece) for piece in give]))
    left_pair, right_grads = pair(left), out_grad[0]
    results = heads_back(heads)
    left_pair, results, right_rows = barrier((left_pair, results, right_rows))
    results = exchange(results)
    right_partner = swap(right_rows)
    left_sums, slopes = [], None
    for d in range(1, half):
        left = hop(left, -1)
        ahead = () if d > 1 else (right_rows, right_partner)
        kept, give, more = work(left_pair, weights, LEFT_COST, ahead=ahead)
        slopes = more[0] if d == 1 else slopes
        left, results, kept, give = barrier((left, results, kept, give))
        left_sums.append(add_up(kept, joined([swap(piece) for piece in give])))
        left_pair = pair(left)
    carried = left_sums[-1].astype(jnp.bfloat16)
    for sums in reversed(left_sums[:-1]):
        carried = add_up(sums, hop(carried, 1)).astype(jnp.bfloat16)
    left_halves = [hop(carried[: bins // 2], 1), hop(carried[bins // 2 :], 1)]
    rights = [(right_rows, hop(right_grads, 1))]
    for d in range(2, half):
        rights.append(tuple(hop(member, 1) for member in rights[-1]))
    kept, give, _ = work(left_pair, weights, FAR_COST)
    left_halves[0], rights, kept, give = barrier((left_halves[0], rights, kept, give))
    carried = add_up(kept, joined([swap(piece) for piece in give]))
    for d in range(half - 1, 0, -1):
        cut = bins - bins // 4
        carried = carried.astype(jnp.bfloat16)
        most, last = hop(carried[:cut], -1), hop(carried[cut:], -1)
        right_pair = pair(*rights[d - 1])
        if d == 1:
            right_pair[1][0] = right_partner
        kept, give, _ = work(
            right_pair, weights, RIGHT_COST, 4, slopes=slopes if d == 1 else None
        )
        kept, give, left_halves = barrier((kept, give, left_halves))
        given = [swap(piece) for piece in give]
        sums = [add_up(kept[:cut], joined(given[:3]), most), add_up(kept[cut:], given[3], last)]
        carried = jnp.concatenate(sums, axis=0)
    total = add_up(total, joined(left_halves))
    total, sums[1] = barrier((total, sums[1]))
    returned = [hop(part.astype(jnp.bfloat16), -1) for part in sums]
    outs = unpack_groups(mine, results)
    total = add_up(total, joined(returned)).astype(jnp.bfloat16)
    return tuple(out[None] for out in outs) + (total[None],)


def solution(mesh):
    rows = P("exp", "ctx", None)
    experts = P("exp", None, None)
    return jax.shard_map(
        per_device,
        mesh=mesh,
        in_specs=(rows,) * 7 + (experts,) * 2,
        out_specs=(rows,) * 4,
        check_vma=False,
    )
```
